32 devices in a mesh: seq: 4 (over y, x), head: 8 (over z, core).
Axes of the slice: x: 2, y: 2, z: 4, core: 2. Of those that a mesh axis runs over, the one named last changes fastest.
Arguments:
- x_heads: bfloat16 [2, 1024, 16384], P(None, 'seq', 'head'), may hold values from -6 to 6
- gate_z: bfloat16 [2, 1024, 16384], P(None, 'seq', 'head'), may hold values from -6 to 6
- b_proj: bfloat16 [2, 1024, 128], P(None, 'seq'), may hold values from -0.59765625 to 0.59765625
- c_proj: bfloat16 [2, 1024, 128], P(None, 'seq'), may hold values from -6 to 6
- dt_raw: float32 [2, 1024, 256], P(None, 'seq', 'head'), may hold values from -3 to 3
- dt_bias: float32 [2, 256], P(None, 'head'), may hold values from -1 to 0.5
- decay_rate: float32 [2, 256], P(None, 'head'), may hold values from 0 to 1, as said below
- skip_d: float32 [2, 256], P(None, 'head'), may hold values from 0.5 to 1.5
- norm_gain: float32 [2, 16384], P(None, 'head'), may hold values from 0.5 to 1.5
- w_out: bfloat16 [2, 16384, 8192], P(None, 'head', 'seq'), may hold values from -0.046875 to 0.046875
- seg_ids: int32 [1024], P('seq'), may hold values from 0 to 2, never falling along the last dimension, each value on 1 to 512 neighbouring positions
Outputs:
- mixed: bfloat16 [2, 1024, 8192], P(None, 'head', 'seq')
The draws below stay inside these ranges and needn't reach their ends.
Inputs may be any that keep to these rules, and one draw needn't show every extreme that they name: `decay_rate`: Positive. `seg_ids`: document numbers start at 0, never fall along the sequence and take every value; one document has exactly 512 tokens.
All inputs are finite; a program needn't handle non-finite values.
Results may differ from the reference program's by a relative error of at most 0.019.
Values may be sent and summed in bfloat16 or wider, within the bound.
No kernel may reach another device: no remote copies, remote signals or barrier semaphores. Data moves between devices by JAX's collectives and lax.ppermute only.
A program may use at most 128 MiB of HBM per device.

```python
import math
import jax
import jax.numpy as jnp
import numpy as np
from jax import lax

D = 8192
HEADS = 256
HEADDIM = 64
STATE = 128
SPAN = 256
TOKENS = 1024
SEGS = 3
MOST = 512
N_HEAD = 8


def draw_decay_rate(key, part):
    key_pick, key_slow, key_fast = jax.random.split(key, 3)
    portion = 0.5
    chosen = jax.random.uniform(key_pick, (2, HEADS)) < portion
    slow_log = jax.random.uniform(key_slow, (2, HEADS), minval=jnp.log(0.1 / TOKENS), maxval=jnp.log(1.0 / TOKENS))
    fast_log = jax.random.uniform(key_fast, (2, HEADS), minval=jnp.log(1.0 / 50.0), maxval=jnp.log(1.0 / 30.0))
    return jnp.exp(jnp.where(chosen, slow_log, fast_log)).astype(jnp.float32)


def levels(own_key, shape, cuts, least, largest):
    def one(dim, parts):
        heights = jax.random.uniform(jax.random.fold_in(jax.random.fold_in(own_key, 6), dim), (parts,), jnp.float32, least / len(cuts), largest / len(cuts))
        return jnp.repeat(jnp.exp(heights), shape[dim] // parts).reshape((-1,) + (1,) * (len(shape) - dim - 1))

    factor_of = one(*cuts[0])
    for cut in cuts[1:]:
        factor_of = factor_of * one(*cut)
    return factor_of


def length_profile(amount, total, reach, lean):
    loads = [(1 << 20) // math.isqrt(standing ** lean) + 1 for standing in range(2, amount + 1)]
    spare, counts = total - reach - (amount - 1), [1] * (amount - 1)
    while spare > 0:
        candidates = [i for i in range(amount - 1) if counts[i] < reach]
        whole, remaining = sum([loads[i] for i in candidates]), spare
        for i in candidates:
            more = min(reach - counts[i], max(1, remaining * loads[i] // whole), spare)
            counts[i] = counts[i] + more
            spare = spare - more
    return np.array([reach] + counts)


def ragged_sizes(stream_key, number_of, total, bound, slope):
    if number_of == 2:
        one = jax.random.randint(stream_key, (), max(1, total - bound), min(bound, total - 1) + 1)
        return jnp.stack([one, total - one])
    sizes = jnp.asarray(length_profile(number_of, total, bound, slope), jnp.int32)
    pairs = (number_of - 1) // 2
    donor, receiver = sizes[1:1 + 2 * pairs:2], sizes[2:2 + 2 * pairs:2]
    slack = jnp.minimum(donor - 1, bound - receiver)
    passed = jax.random.randint(jax.random.fold_in(stream_key, 1), (pairs,), 0, 1 << 20) % (slack + 1)
    sizes = sizes.at[1:1 + 2 * pairs:2].set(donor - passed).at[2:2 + 2 * pairs:2].set(receiver + passed)
    return sizes[jax.random.permutation(jax.random.fold_in(stream_key, 2), number_of)]


def noise(rng, extent, scale, limit, cuts=(), held_as=jnp.bfloat16):
    array = jax.random.normal(rng, extent, jnp.float32) * scale
    if len(cuts) > 0:
        array = levels(rng, extent, cuts, -0.22, 0.18) * array
    return jnp.clip(array, min=-limit, max=limit).astype(held_as)


def setup_inputs(seed: int = 0) -> dict:
    seeds = jax.random.split(jax.random.key(seed), 12)
    return {
        "x_heads": noise(seeds[0], (2, TOKENS, HEADS * HEADDIM), 1.0, 6.0, ((1, 4), (2, 8))),
        "gate_z": noise(seeds[1], (2, TOKENS, HEADS * HEADDIM), 1.0, 6.0, ((1, 4), (2, 8))),
        "b_proj": noise(seeds[2], (2, TOKENS, STATE), 0.1, 0.59765625, ((1, 4),)),
        "c_proj": noise(seeds[3], (2, TOKENS, STATE), 1.0, 6.0, ((1, 4),)),
        "dt_raw": noise(seeds[4], (2, TOKENS, HEADS), 0.5, 3.0, ((1, 4), (2, 8)), jnp.float32),
        "dt_bias": jnp.clip(-1.0 + 1.5 * jax.random.uniform(seeds[5], (2, HEADS), jnp.float32) ** levels(seeds[5], (2, HEADS), ((1, 8),), -0.2, 0.2), -1.0, 0.5),
        "decay_rate": draw_decay_rate(jax.random.fold_in(seeds[11], 71), 0),
        "skip_d": jnp.clip(0.5 + 1.0 * jax.random.uniform(seeds[7], (2, HEADS), jnp.float32) ** levels(seeds[7], (2, HEADS), ((1, 8),), -0.2, 0.2), 0.5, 1.5),
        "norm_gain": jnp.clip(0.5 + 1.0 * jax.random.uniform(seeds[8], (2, HEADS * HEADDIM), jnp.float32) ** levels(seeds[8], (2, HEADS * HEADDIM), ((1, 8),), -0.2, 0.2), 0.5, 1.5),
        "w_out": noise(seeds[9], (2, HEADS * HEADDIM, D), (HEADS * HEADDIM) ** -0.5, 0.046875, ((1, 8), (2, 4))),
        "seg_ids": jnp.searchsorted(jnp.cumsum(ragged_sizes(seeds[10], SEGS, TOKENS, MOST, 0)), jnp.arange(TOKENS), side="right").astype(jnp.int32),
    }


highest = lax.Precision.HIGHEST

def to_blocks(tensor, nblocks):
    shaped = tensor.reshape((tensor.shape[0], nblocks, tensor.shape[1] // nblocks) + tensor.shape[2:])
    return jnp.moveaxis(shaped, 1, 0)

def from_blocks(tensor):
    moved = jnp.moveaxis(tensor, 0, 1)
    return moved.reshape((moved.shape[0], moved.shape[1] * moved.shape[2]) + moved.shape[3:])

def span_state(carried, before, offset, anchor, pieces):
    x_block, b_block, c_block, step_block, decay_block, seg_block = pieces
    running = jnp.cumsum(decay_block, axis=1)
    total = running[:, -1, :]
    kept = (seg_block == before).astype(jnp.float32)
    same_last = (seg_block == seg_block[-1]).astype(jnp.float32)
    tail_w = jnp.exp(total[:, None, :] - running) * same_last[None, :, None] * step_block
    fresh = jnp.einsum('mjh,mjhp,mjn->mhpn', tail_w, x_block, b_block, precision=highest)
    new_state = (jnp.exp(total) * kept[-1])[:, :, None, None] * carried + fresh
    factor = jnp.exp(offset[:, None, :] + running) * (seg_block == anchor).astype(jnp.float32)[None, :, None]
    return (new_state, factor, total)

def span_output(carried, before, pieces):
    x_block, b_block, c_block, step_block, decay_block, seg_block = pieces
    running = jnp.cumsum(decay_block, axis=1)
    kept = (seg_block == before).astype(jnp.float32)
    entry_w = jnp.exp(running) * kept[None, :, None]
    places = jnp.arange(seg_block.shape[0], dtype=jnp.int32)
    lower_mask = (places[:, None] >= places[None, :]) & (seg_block[:, None] == seg_block[None, :])
    run_t = jnp.transpose(running, (0, 2, 1))
    spread = run_t[:, :, :, None] - run_t[:, :, None, :]
    mixing = jnp.exp(jnp.minimum(spread, 0.0)) * lower_mask.astype(jnp.float32)
    products = jnp.einsum('min,mjn->mij', c_block, b_block, precision=highest)
    weights = mixing * products[:, None] * jnp.transpose(step_block, (0, 2, 1))[:, :, None, :]
    inside = jnp.einsum('mhij,mjhp->mihp', weights, x_block, precision=highest)
    entering = jnp.einsum('min,mhpn->mihp', c_block, carried, precision=highest)
    return inside + entry_w[..., None] * entering

def scan_turn(carry, pieces):
    carried, before = carry
    output = span_output(carried, before, pieces)
    new_state, factor_unused, total_unused = span_state(carried, before, jnp.zeros(carried.shape[:2], jnp.float32), before, pieces)
    return ((new_state, pieces[5][-1]), output)

def reference(x_heads, gate_z, b_proj, c_proj, dt_raw, dt_bias, decay_rate, skip_d, norm_gain, w_out, seg_ids):
    length = TOKENS
    block = min(SPAN, length)
    nblocks = length // block
    step_size = jax.nn.softplus(dt_raw + dt_bias[:, None, :])
    log_decay = -decay_rate[:, None, :] * step_size
    x_float = x_heads.astype(jnp.float32).reshape(2, length, HEADS, HEADDIM)
    b_float = b_proj.astype(jnp.float32)
    c_float = c_proj.astype(jnp.float32)
    pieces = (to_blocks(x_float, nblocks), to_blocks(b_float, nblocks), to_blocks(c_float, nblocks), to_blocks(step_size, nblocks), to_blocks(log_decay, nblocks), seg_ids.reshape(nblocks, block))
    start = (jnp.zeros((2, HEADS, HEADDIM, STATE), jnp.float32), seg_ids[0])
    end_unused, outputs = lax.scan(scan_turn, start, pieces)
    ssd_out = from_blocks(outputs) + skip_d[:, None, :, None] * x_float
    gated = ssd_out.reshape(2, length, HEADS * HEADDIM) * jax.nn.silu(gate_z.astype(jnp.float32))
    mean_square = lax.optimization_barrier(jnp.mean(gated * gated, axis=2))
    normed = (gated * lax.rsqrt(mean_square + 1e-05)[:, :, None] * norm_gain[:, None, :]).astype(jnp.bfloat16)
    width = HEADS * HEADDIM // N_HEAD
    grouped = normed.reshape(2, length, N_HEAD, width)
    weights = w_out.reshape(2, N_HEAD, width, D)

    def add_group(summed, index):
        part_in = lax.dynamic_index_in_dim(grouped, index, 2, keepdims=False)
        weight_in = lax.dynamic_index_in_dim(weights, index, 1, keepdims=False)
        term = jnp.einsum('mtk,mkd->mtd', part_in.astype(jnp.float32), weight_in.astype(jnp.float32))
        rounded = lax.optimization_barrier(term.astype(jnp.bfloat16))
        return (summed + rounded.astype(jnp.float32), None)
    summed, unused = lax.scan(add_group, jnp.zeros((2, length, D), jnp.float32), jnp.arange(N_HEAD, dtype=jnp.int32))
    return summed.astype(jnp.bfloat16)
```

```python
import functools
import jax
import jax.numpy as jnp
from jax import lax
from jax.experimental import pallas as pl
from jax.experimental.pallas import tpu as pltpu
from jax.sharding import PartitionSpec as P

F32, BF16 = jnp.float32, jnp.bfloat16
LANES = 128
EXTRA = 16
NEG = -1e30
EPS = 1e-05
PARAMS = pltpu.CompilerParams(vmem_limit_bytes=32 * 1024 * 1024)


def cost(flops, moved, trans=0):
    return pl.CostEstimate(flops=int(flops), bytes_accessed=int(moved), transcendentals=int(trans))


def dot(a, b):
    return jnp.dot(a, b, preferred_element_type=F32)


def lane_split(head_size, shape):
    return lax.broadcasted_iota(jnp.int32, shape, 1) // head_size


def spread(values, lane_head, first):
    shape = (values.shape[0], LANES)
    out = jnp.broadcast_to(values[:, first : first + 1], shape)
    for k in range(1, lane_head[1]):
        out = jnp.where(lane_head[0] == k, values[:, first + k : first + k + 1], out)
    return out


def lane_heads(head_size):
    return (lane_split(head_size, (1, LANES)), LANES // head_size)


def column(row):
    return jnp.broadcast_to(row, (LANES, row.shape[1])).T[:, :1]


def prep_kernel(model, head_size, x_ref, b_ref, raw_ref, bias_ref, rate_ref, seg_ref, msg_ref, run_ref, q_ref, step_ref):
    rows, channels = x_ref.shape[1:]
    heads = raw_ref.shape[2]
    state = b_ref.shape[2]
    step = jax.nn.softplus(raw_ref[0] + bias_ref[model : model + 1, :])
    log_decay = -rate_ref[model : model + 1, :] * step
    places = lax.broadcasted_iota(jnp.int32, (rows, rows), 0)
    others = lax.broadcasted_iota(jnp.int32, (rows, rows), 1)
    tri = (places >= others).astype(F32)
    run = jnp.dot(tri, log_decay, precision=lax.Precision.HIGHEST, preferred_element_type=F32)
    run_ref[...] = run
    step_ref[...] = step
    q = jnp.concatenate([run - jnp.log(step), jnp.zeros((rows, LANES - heads), F32)], axis=1)
    q_ref[...] = q.T[:heads]
    seg_row = seg_ref[...].astype(F32)
    seg_col = column(seg_row)
    last = seg_row[:, rows - 1 :]
    total = run[rows - 1 :, :]
    tail = jnp.exp(total - run) * step * (seg_col == last).astype(F32)
    etot = jnp.exp(total)
    b_t = b_ref[0].astype(F32).T.astype(BF16)
    lane_head = lane_heads(head_size)
    row_id = lax.broadcasted_iota(jnp.int32, (EXTRA, LANES), 0)
    for p in range(channels // LANES):
        cols = slice(p * LANES, (p + 1) * LANES)
        first = p * lane_head[1]
        xw = (x_ref[0, :, cols].astype(F32) * spread(tail, lane_head, first)).astype(BF16)
        msg_ref[:state, cols] = dot(b_t, xw).astype(BF16)
        decay = spread(etot, lane_head, first)
        high = decay.astype(BF16).astype(F32)
        extra = jnp.where(row_id == 0, high, jnp.where(row_id == 1, decay - high, jnp.where(row_id == 2, last, 0.0)))
        msg_ref[state:, cols] = extra.astype(BF16)


def prep(model, head_size, x, b, raw, bias, rate, seg_row):
    _, rows, channels = x.shape
    heads, state = raw.shape[2], b.shape[2]
    at = lambda i: (model, 0, 0)
    whole = lambda i: (0, 0)
    return pl.pallas_call(
        functools.partial(prep_kernel, model, head_size),
        name=f"prep_{model}",
        grid=(1,),
        in_specs=[
            pl.BlockSpec((1, rows, channels), at),
            pl.BlockSpec((1, rows, state), at),
            pl.BlockSpec((1, rows, heads), at),
            pl.BlockSpec(bias.shape, whole),
            pl.BlockSpec(rate.shape, whole),
            pl.BlockSpec(seg_row.shape, whole),
        ],
        out_specs=[
            pl.BlockSpec((state + EXTRA, channels), whole),
            pl.BlockSpec((rows, heads), whole),
            pl.BlockSpec((heads, rows), whole),
            pl.BlockSpec((rows, heads), whole),
        ],
        out_shape=[
            jax.ShapeDtypeStruct((state + EXTRA, channels), BF16),
            jax.ShapeDtypeStruct((rows, heads), F32),
            jax.ShapeDtypeStruct((heads, rows), F32),
            jax.ShapeDtypeStruct((rows, heads), F32),
        ],
        compiler_params=PARAMS,
        cost_estimate=cost(2 * rows * state * channels, 2 * rows * channels + 2 * state * channels),
    )(x, b, raw, bias, rate, seg_row)


def inside_kernel(model, head_size, x_ref, gate_ref, b_ref, c_ref, run_ref, q_ref, step_ref, skip_ref, seg_ref, yg_ref, fg_ref):
    rows, channels = x_ref.shape[1:]
    half = rows // 2
    lane_head = lane_heads(head_size)
    run, q = run_ref[...], q_ref[...]
    seg_row = seg_ref[...].astype(F32)
    seg_col = column(seg_row)
    products = lax.dot_general(c_ref[0], b_ref[0], (((1,), (1,)), ((), ())), preferred_element_type=F32)
    tri = lax.broadcasted_iota(jnp.int32, (half, half), 0) >= lax.broadcasted_iota(jnp.int32, (half, half), 1)
    parts = [slice(0, half), slice(half, rows)]
    masks = [tri & (seg_col[part] == seg_row[:, part]) for part in parts]
    diagonal = [products[part, part] for part in parts]
    below = jnp.where(seg_col[parts[1]] == seg_row[:, parts[0]], products[parts[1], parts[0]], 0.0).astype(BF16)
    middle = run[half - 1 : half, :]
    entry = jnp.exp(run[parts[1]] - middle)
    leave = jnp.exp(middle - run[parts[0]]) * step_ref[parts[0], :]
    factor = jnp.exp(run)
    skip = skip_ref[model : model + 1, :]
    for p in range(channels // LANES):
        cols = slice(p * LANES, (p + 1) * LANES)
        first = p * lane_head[1]
        x = x_ref[0, :, cols]
        xf = x.astype(F32)
        ys = []
        for part, mask, prod in zip(parts, masks, diagonal):
            y = None
            for k in range(lane_head[1]):
                h = first + k
                mixing = jnp.exp(jnp.where(mask, run[part, h : h + 1] - q[h : h + 1, part], NEG))
                term = dot((mixing * prod).astype(BF16), x[part])
                y = term if y is None else jnp.where(lane_head[0] == k, term, y)
            ys.append(y)
        sent = (xf[parts[0]] * spread(leave, lane_head, first)).astype(BF16)
        ys[1] = ys[1] + dot(below, sent) * spread(entry, lane_head, first)
        y = jnp.concatenate(ys, axis=0) + spread(skip, lane_head, first) * xf
        v = gate_ref[0, :, cols].astype(F32)
        silu = v / (1.0 + jnp.exp(-v))
        yg_ref[:, cols] = y * silu
        fg_ref[:, cols] = (spread(factor, lane_head, first) * silu).astype(BF16)


def inside(model, head_size, x, gate, b, c, run, q, step, skip, seg_row):
    _, rows, channels = x.shape
    heads, state = run.shape[1], b.shape[2]
    at = lambda i: (model, 0, 0)
    whole = lambda i: (0, 0)
    return pl.pallas_call(
        functools.partial(inside_kernel, model, head_size),
        name=f"inside_{model}",
        grid=(1,),
        in_specs=[
            pl.BlockSpec((1, rows, channels), at),
            pl.BlockSpec((1, rows, channels), at),
            pl.BlockSpec((1, rows, state), at),
            pl.BlockSpec((1, rows, state), at),
            pl.BlockSpec((rows, heads), whole),
            pl.BlockSpec((heads, rows), whole),
            pl.BlockSpec((rows, heads), whole),
            pl.BlockSpec(skip.shape, whole),
            pl.BlockSpec(seg_row.shape, whole),
        ],
        out_specs=[pl.BlockSpec((rows, channels), whole), pl.BlockSpec((rows, channels), whole)],
        out_shape=[jax.ShapeDtypeStruct((rows, channels), F32), jax.ShapeDtypeStruct((rows, channels), BF16)],
        compiler_params=PARAMS,
        cost_estimate=cost(2 * rows * rows * LANES * heads, 12 * rows * channels, rows * rows * heads // 2),
    )(x, gate, b, c, run, q, step, skip, seg_row)


def join_kernel(state, own_ref, got_ref, out_ref):
    own, got = own_ref[...].astype(F32), got_ref[...].astype(F32)
    same = (own[state + 2 : state + 3] == got[state + 2 : state + 3]).astype(F32)
    decay = (own[state : state + 1] + own[state + 1 : state + 2]) * same
    out_ref[:state, :] = (own[:state] + decay * got[:state]).astype(BF16)
    out_ref[state:, :] = own_ref[state:, :]


def join(model, state, own, got):
    return pl.pallas_call(
        functools.partial(join_kernel, state),
        name=f"join_{model}",
        out_shape=jax.ShapeDtypeStruct(own.shape, BF16),
        compiler_params=PARAMS,
        cost_estimate=cost(4 * own.size, 6 * own.size),
    )(own, got)


def gate_kernel(model, state, pair_ref, near_ref, *refs):
    far_refs = refs[:-8]
    c_ref, seg_ref, yg_ref, fg_ref, gain_ref, before_ref, g_ref, ss_ref = refs[-8:]
    rows, channels = yg_ref.shape
    paired = pair_ref[0] == 1
    near = near_ref[...].astype(F32)
    far = far_refs[0][...].astype(F32)
    for ref in far_refs[1:]:
        far = far + ref[...].astype(F32)
    last_near, last_far = near[state + 2 : state + 3], far[state + 2 : state + 3]
    decay = (near[state : state + 1] + near[state + 1 : state + 2]) * (last_near == last_far).astype(F32)
    entering = (near[:state] + jnp.where(paired, decay, 1.0) * far[:state]).astype(BF16)
    anchor = jnp.where(paired, last_near, last_far)[:, :1]
    reached = (column(seg_ref[...].astype(F32)) == anchor).astype(F32)
    squares = jnp.zeros((8, rows), F32)
    ones = jnp.ones((8, 512), BF16)
    for p in range(channels // 512):
        cols = slice(p * 512, (p + 1) * 512)
        gated = yg_ref[:, cols] + reached * fg_ref[:, cols].astype(F32) * dot(c_ref[0], entering[:, cols])
        g_ref[:, cols] = (gated * gain_ref[model : model + 1, cols]).astype(BF16)
        squares += lax.dot_general(ones, (gated * gated).astype(BF16), (((1,), (1,)), ((), ())), preferred_element_type=F32)
    ss_ref[...] = jnp.where(lax.broadcasted_iota(jnp.int32, (8, rows), 0) // 4 == model, squares, before_ref[...])


def gate_all(model, pair, near, far, c, seg_row, yg, fg, gain, before):
    rows, channels = yg.shape
    state = c.shape[2]
    whole = lambda i, *_: (0, 0)
    full = lambda a: pl.BlockSpec(a.shape, whole)
    return pl.pallas_call(
        functools.partial(gate_kernel, model, state),
        name=f"gated_{model}",
        grid_spec=pltpu.PrefetchScalarGridSpec(
            num_scalar_prefetch=1,
            grid=(1,),
            in_specs=[full(near)]
            + [full(a) for a in far]
            + [pl.BlockSpec((1, rows, state), lambda i, *_: (model, 0, 0))]
            + [full(a) for a in (seg_row, yg, fg, gain, before)],
            out_specs=[full(yg), pl.BlockSpec((8, rows), whole)],
        ),
        out_shape=[jax.ShapeDtypeStruct((rows, channels), BF16), jax.ShapeDtypeStruct((8, rows), F32)],
        compiler_params=PARAMS,
        cost_estimate=cost(2 * rows * channels * state, 10 * rows * channels),
    )(pair, near, *far, c, seg_row, yg, fg, gain, before)


def project_kernel(kinds, core_ref, *refs):
    count = sum(kinds)
    lhs_refs, (w_ref, keep_ref, send_ref, lhs) = refs[:count], refs[count:]
    half = keep_ref.shape[1]
    chunks = len(kinds)

    @pl.when(pl.program_id(0) == 0)
    def _():
        at = 0
        for i, kind in enumerate(kinds):
            for place, own in ((i, 0), (chunks + i, 1)):
                which = core_ref[0] if own == 0 else 1 - core_ref[0]
                if kind == 1:
                    value = lhs_refs[at][pl.ds(pl.multiple_of(which * half, half), half), :]
                else:
                    value = jnp.where(which == 0, lhs_refs[at][...], lhs_refs[at + 1][...])
                lhs[place * half : (place + 1) * half, :] = value
            at += kind

    result = dot(lhs[...], w_ref[0])
    for i in range(chunks):
        keep_ref[i] = result[i * half : (i + 1) * half]
        send_ref[i] = result[(chunks + i) * half : (chunks + i + 1) * half].astype(BF16)


def project(name, core, model, chunks, w):
    kinds = [len(c) for c in chunks]
    flat = [a for c in chunks for a in c]
    depth, width = w.shape[1:]
    rows = sum(a.shape[0] for a in flat)
    half = rows // len(chunks) // 2
    tile = min(512, width)
    n = len(chunks)
    return pl.pallas_call(
        functools.partial(project_kernel, kinds),
        name=f"{name}_{model}",
        grid_spec=pltpu.PrefetchScalarGridSpec(
            num_scalar_prefetch=1,
            grid=(width // tile,),
            in_specs=[pl.BlockSpec(a.shape, lambda j, *_: (0, 0)) for a in flat]
            + [pl.BlockSpec((1, depth, tile), lambda j, *_: (model, 0, j))],
            out_specs=[pl.BlockSpec((n, half, tile), lambda j, *_: (0, 0, j))] * 2,
            scratch_shapes=[pltpu.VMEM((rows, depth), BF16)],
        ),
        out_shape=[jax.ShapeDtypeStruct((n, half, width), F32), jax.ShapeDtypeStruct((n, half, width), BF16)],
        compiler_params=PARAMS,
        cost_estimate=cost(2 * rows * depth * width, 2 * depth * width + 2 * rows * depth + 6 * n * half * width),
    )(core, *flat, w)


def pair_kernel(order_ref, keep0, got0, keep1, got1, first_ref, second_ref):
    a = keep0[0] + got0[0].astype(F32)
    b = keep1[0] + got1[0].astype(F32)
    turned = order_ref[0] == 1
    first_ref[...] = jnp.where(turned, b, a).astype(BF16)
    second_ref[...] = jnp.where(turned, a, b).astype(BF16)


def pair_sums(name, order, keeps, gots):
    def views(arrays):
        if len(arrays) == 1:
            return [(arrays[0], 0), (arrays[0], 1)]
        return [(arrays[0], 0), (arrays[1], 0)]
    (k0, k1), (g0, g1) = views(keeps), views(gots)
    operands = [k0, g0, k1, g1]
    half, width = keeps[0].shape[1:]
    tile = min(1024, width)
    return pl.pallas_call(
        pair_kernel,
        name=name,
        grid_spec=pltpu.PrefetchScalarGridSpec(
            num_scalar_prefetch=1,
            grid=(width // tile,),
            in_specs=[pl.BlockSpec((1, half, tile), lambda j, *_, i=i: (i, 0, j)) for _, i in operands],
            out_specs=[pl.BlockSpec((half, tile), lambda j, *_: (0, j))] * 2,
        ),
        out_shape=[jax.ShapeDtypeStruct((half, width), BF16)] * 2,
        compiler_params=PARAMS,
        cost_estimate=cost(2 * half * width, 16 * half * width),
    )(order, *[a for a, _ in operands])


def last_kernel(total, model, where_ref, ss_ref, *refs):
    out_ref = refs[-1]
    pieces = refs[-9:-1] if len(refs) >= 9 else refs[:-1]
    half = out_ref.shape[1]
    rows = ss_ref.shape[1]
    core = where_ref[1]
    row = ss_ref[4 * model : 4 * model + 1, :]
    row = jnp.where(core == 0, row[:, :half], row[:, half:])
    scale = column(lax.rsqrt(row / total + EPS))
    own = jnp.where(where_ref[0] == 1, pieces[6][...], pieces[7][...]).astype(F32)
    value = own
    for ref in pieces[:6]:
        value = value + ref[...].astype(F32)
    out_ref[0] = (value * scale).astype(BF16)


def last(model, total, where, ss, pieces, before):
    half, width = pieces[0].shape
    tile = min(1024, width)
    specs = [pl.BlockSpec(ss.shape, lambda j, *_: (0, 0))]
    operands = [ss]
    aliases = {}
    if before is not None:
        specs.append(pl.BlockSpec(memory_space=pl.ANY))
        operands.append(before)
        aliases = {2: 0}
    specs += [pl.BlockSpec((half, tile), lambda j, *_: (0, j))] * len(pieces)
    return pl.pallas_call(
        functools.partial(last_kernel, total, model),
        name=f"last_{model}",
        grid_spec=pltpu.PrefetchScalarGridSpec(
            num_scalar_prefetch=1,
            grid=(width // tile,),
            in_specs=specs,
            out_specs=pl.BlockSpec((1, half, tile), lambda j, *_: (model, 0, j)),
        ),
        out_shape=jax.ShapeDtypeStruct((2, half, width), BF16),
        input_output_aliases=aliases,
        compiler_params=PARAMS,
        cost_estimate=cost(10 * half * width, 18 * half * width),
    )(where, *operands, *pieces)


def xor_pairs(n, k):
    return [(i, i ^ k) for i in range(n)]


def fast(x, gate, b, c, raw, bias, rate, skip, gain, w, seg):
    head_size = x.shape[2] // raw.shape[2]
    state = b.shape[2]
    n_seq, n_head = lax.axis_size("seq"), lax.axis_size("head")
    total = x.shape[2] * n_head
    seg_row = seg.reshape(1, -1)
    s, h = lax.axis_index("seq"), lax.axis_index("head")
    z, core = h // 2, h % 2
    away = jnp.bitwise_xor(s, z)
    one = lambda v: jnp.reshape(v.astype(jnp.int32), (1,))
    core_arr, pair_arr = one(core), one(s % 2)
    order_xy, order_od = one(away % 2), one(1 - away % 2)
    is_od = ((away == 0) | (away == 3)).astype(jnp.int32)
    where = jnp.stack([is_od, core]).astype(jnp.int32)

    def flat(si, zi, ci):
        return si * n_head + zi * 2 + ci

    def sends(kinds, j):
        return [
            (flat(si, si ^ k ^ j, ci), flat(si, si ^ k, ci))
            for si in range(n_seq) for k in kinds for ci in range(2)
        ]

    preps = [prep(m, head_size, x, b, raw, bias, rate, seg_row) for m in range(2)]
    near = [lax.ppermute(preps[m][0], "seq", [(0, 1), (2, 3)]) for m in range(2)]
    insides = [
        inside(m, head_size, x, gate, b, c, preps[m][1], preps[m][2], preps[m][3], skip, seg_row) for m in range(2)
    ]
    joined = [join(m, state, preps[m][0], near[m]) for m in range(2)]
    far = [[lax.ppermute(joined[m], "seq", [(1, t)]) for t in (2, 3)] for m in range(2)]
    ss = jnp.zeros((8, x.shape[1]), F32)
    gs = []
    for m in range(2):
        g, ss = gate_all(m, pair_arr, near[m], far[m], c, seg_row, *insides[m], gain, ss)
        gs.append(g)
    for k in (1, 2, 4):
        ss = ss + lax.ppermute(ss, "head", xor_pairs(n_head, k))
    ss = lax.ppermute(
        ss, ("seq", "head"),
        [(flat(zi, si, ci), flat(si, zi, ci)) for si in range(n_seq) for zi in range(n_seq) for ci in range(2)],
    )
    half = x.shape[1] // 2
    out = None
    for m in range(2):
        g = gs[m]
        px = lax.ppermute(g, "seq", xor_pairs(n_seq, 1))
        py = lax.ppermute(g, "seq", xor_pairs(n_seq, 2))
        d0 = lax.ppermute(px[:half], "seq", xor_pairs(n_seq, 2))
        d1 = lax.ppermute(py[half:], "seq", xor_pairs(n_seq, 1))
        across = lambda a: lax.ppermute(a, "head", xor_pairs(n_head, 1))
        keep_o, send_o = project("own", core_arr, m, [(g,)], w)
        got_o = across(send_o)
        keep_n, send_n = project("next", core_arr, m, [(px,), (py,)], w)
        got_n = across(send_n)
        keep_d, send_d = project("opposite", core_arr, m, [(d0, d1)], w)
        got_d = across(send_d)
        first_n, second_n = pair_sums(f"sum_next_{m}", order_xy, [keep_n], [got_n])
        rest = [
            lax.ppermute(a, ("seq", "head"), sends((1, 2), j)) for a, j in ((first_n, 1), (second_n, 2), (first_n, 3))
        ]
        first_d, second_d = pair_sums(f"sum_opposite_{m}", order_od, [keep_o, keep_d], [got_o, got_d])
        rest += [
            lax.ppermute(a, ("seq", "head"), sends((0, 3), j)) for a, j in ((first_d, 1), (second_d, 2), (first_d, 3))
        ]
        out = last(m, total, where, ss, rest + [second_d, second_n], out)
    return out


def plain(x, gate, b, c, raw, bias, rate, skip, gain, w, seg):
    head_size = x.shape[2] // raw.shape[2]
    state = b.shape[2]
    n_seq, n_head = lax.axis_size("seq"), lax.axis_size("head")
    total = x.shape[2] * n_head
    seg_row = seg.reshape(1, -1)
    s, h = lax.axis_index("seq"), lax.axis_index("head")
    ss = jnp.zeros((8, x.shape[1]), F32)
    gs = []
    for m in range(2):
        msg, run, q, step = prep(m, head_size, x, b, raw, bias, rate, seg_row)
        every = lax.all_gather(msg, "seq").astype(F32)
        entering, before = jnp.zeros_like(every[0]), every[0]
        for k in range(n_seq - 1):
            now = every[k]
            same = (now[state + 2] == before[state + 2]).astype(F32)
            decay = (now[state] + now[state + 1]) * same
            new = jnp.concatenate([now[:state] + decay * entering[:state], now[state:]])
            entering = jnp.where(k < s, new, entering)
            before = now
        yg, fg = inside(m, head_size, x, gate, b, c, run, q, step, skip, seg_row)
        near = entering.astype(BF16)
        g, ss = gate_all(m, jnp.ones((1,), jnp.int32), near, [jnp.zeros_like(near)], c, seg_row, yg, fg, gain, ss)
        gs.append(g)
    g = lax.all_gather(jnp.stack(gs), "seq", axis=1, tiled=True)
    terms = jnp.einsum("mtk,mkd->mtd", g, w, preferred_element_type=F32)
    summed = lax.psum_scatter(terms.astype(BF16), "head", scatter_dimension=1, tiled=True)
    squares = lax.all_gather(lax.psum(ss[::4], "head"), "seq", axis=1, tiled=True)
    mine = lax.dynamic_slice_in_dim(squares, h * summed.shape[1], summed.shape[1], axis=1)
    return (summed.astype(F32) * lax.rsqrt(mine / total + EPS)[:, :, None]).astype(BF16)


def solution(mesh):
    placed = (
        P(None, "seq", "head"),
        P(None, "seq", "head"),
        P(None, "seq", None),
        P(None, "seq", None),
        P(None, "seq", "head"),
        P(None, "head"),
        P(None, "head"),
        P(None, "head"),
        P(None, "head"),
        P(None, "head", "seq"),
        P("seq"),
    )
    local = fast if mesh.shape["seq"] == 4 and mesh.shape["head"] == 8 else plain
    return jax.shard_map(
        local, mesh=mesh, in_specs=placed, out_specs=P(None, "head", "seq"), check_vma=False
    )
```

```python
import functools
import jax
import jax.numpy as jnp
from jax import lax
from jax.experimental import pallas as pl
from jax.experimental.pallas import tpu as pltpu
from jax.sharding import PartitionSpec as P

F32, BF16 = jnp.float32, jnp.bfloat16
LANES = 128
EXTRA = 16
NEG = -1e30
EPS = 1e-05
IN_VMEM = pl.BlockSpec(memory_space=pltpu.VMEM)
ANYWHERE = pl.BlockSpec(memory_space=pl.ANY)
SCOPE = 14 * 1024 * 1024


def dot(a, b):
    return jnp.dot(a, b, preferred_element_type=F32)


def call(kernel, name, operands, outs, far=(), after=(), carry=(), scratch=(), **kw):
    given, idle = len(operands) + len(far), len(after) + len(carry)

    def body(*refs):
        rest = refs[given + idle :]
        return kernel(*refs[:given], *rest[: len(outs)], *rest[len(outs) + len(carry) :])

    return pl.pallas_call(
        body,
        name=name,
        in_specs=[IN_VMEM] * len(operands)
        + [ANYWHERE] * len(far)
        + [IN_VMEM] * len(after)
        + [ANYWHERE] * len(carry),
        out_specs=[IN_VMEM] * len(outs) + [ANYWHERE] * len(carry),
        out_shape=[pltpu.VMEM(shape, dtype) for shape, dtype in outs]
        + [jax.ShapeDtypeStruct(a.shape, a.dtype) for a in carry],
        scratch_shapes=list(scratch),
        input_output_aliases={given + len(after) + i: len(outs) + i for i in range(len(carry))},
        compiler_params=pltpu.CompilerParams(vmem_limit_bytes=SCOPE),
        cost_estimate=pl.CostEstimate(flops=1, bytes_accessed=1, transcendentals=0),
        **kw,
    )(*operands, *far, *after, *carry)


def start_all(sems, pairs):
    fetches = [pltpu.make_async_copy(source, target, sems.at[i]) for i, (source, target) in enumerate(pairs)]
    for fetch in fetches:
        fetch.start()
    return fetches


def tiles(width):
    tile = min(512, width)
    return [slice(i, i + tile) for i in range(0, width, tile)]


def lane_split(head_size, shape):
    return lax.broadcasted_iota(jnp.int32, shape, 1) // head_size


def spread(values, lane_head, first):
    shape = (values.shape[0], LANES)
    out = jnp.broadcast_to(values[:, first : first + 1], shape)
    for k in range(1, lane_head[1]):
        out = jnp.where(lane_head[0] == k, values[:, first + k : first + k + 1], out)
    return out


def lane_heads(head_size):
    return (lane_split(head_size, (1, LANES)), LANES // head_size)


def column(row):
    return jnp.broadcast_to(row, (LANES, row.shape[1])).T[:, :1]


def head_column(row):
    heads = row.shape[1]
    padded = jnp.concatenate([row, jnp.zeros((1, LANES - heads), F32)], axis=1)
    return jnp.broadcast_to(padded, (LANES, LANES)).T[:heads, :1]


def turned(values):
    heads, rows = values.shape
    return jnp.concatenate([values, jnp.zeros((LANES - heads, rows), F32)], axis=0).T[:, :heads]


def prep_kernel(model, head_size, x_all, b_all, raw_all, bias_all, rate_all, skip_all, seg_all, msg_ref, run_ref, q_ref, step_ref, row_ref, *scratch):
    x_ref, b_ref, raw_ref, bias_ref, rate_ref, skip_ref, seg_ref, sems = scratch
    rows, channels = x_ref.shape[1:]
    mine = pl.ds(model, 1)
    cuts = tiles(channels)
    fetches = start_all(
        sems,
        [(raw_all.at[mine], raw_ref), (bias_all, bias_ref), (rate_all, rate_ref), (skip_all, skip_ref)]
        + [(seg_all, seg_ref), (b_all.at[mine], b_ref)]
        + [(x_all.at[mine, :, cut], x_ref.at[:, :, cut]) for cut in cuts],
    )
    for fetch in fetches[:6]:
        fetch.wait()
    heads = raw_ref.shape[1]
    state = b_ref.shape[2]
    step_t = jax.nn.softplus(raw_ref[0] + head_column(bias_ref[model : model + 1, :]))
    log_decay = -head_column(rate_ref[model : model + 1, :]) * step_t
    earlier = lax.broadcasted_iota(jnp.int32, (rows, rows), 0)
    later = lax.broadcasted_iota(jnp.int32, (rows, rows), 1)
    tri = (later >= earlier).astype(F32)
    run_t = jnp.dot(log_decay, tri, precision=lax.Precision.HIGHEST, preferred_element_type=F32)
    run, step = turned(run_t), turned(step_t)
    run_ref[:, :rows] = run_t
    run_ref[:, rows:] = jnp.broadcast_to(head_column(skip_ref[model : model + 1, :]), (heads, LANES))
    step_ref[...] = step_t
    q_ref[...] = run_t - jnp.log(step_t)
    seg_row = seg_ref[...].astype(F32)
    row_ref[...] = seg_row
    seg_col = column(seg_row)
    last = seg_row[:, rows - 1 :]
    total = run[rows - 1 :, :]
    tail = jnp.exp(total - run) * step * (seg_col == last).astype(F32)
    etot = jnp.exp(total)
    b_t = b_ref[0].astype(F32).T.astype(BF16)
    lane_head = lane_heads(head_size)
    row_id = lax.broadcasted_iota(jnp.int32, (EXTRA, LANES), 0)
    for p in range(channels // LANES):
        cols = slice(p * LANES, (p + 1) * LANES)
        first = p * lane_head[1]
        for cut, fetch in zip(cuts, fetches[6:]):
            if cut.start == cols.start:
                fetch.wait()
        xw = (x_ref[0, :, cols].astype(F32) * spread(tail, lane_head, first)).astype(BF16)
        msg_ref[:state, cols] = dot(b_t, xw).astype(BF16)
        decay = spread(etot, lane_head, first)
        high = decay.astype(BF16).astype(F32)
        extra = jnp.where(row_id == 0, high, jnp.where(row_id == 1, decay - high, jnp.where(row_id == 2, last, 0.0)))
        msg_ref[state:, cols] = extra.astype(BF16)


def prep(model, head_size, x, b, raw, bias, rate, skip, seg_row, after=()):
    _, rows, channels = x.shape
    heads, state = raw.shape[1], b.shape[2]
    far = (x, b, raw, bias, rate, skip, seg_row)
    return call(
        functools.partial(prep_kernel, model, head_size),
        f"prep_{model}",
        (),
        [((state + EXTRA, channels), BF16), ((heads, rows + LANES), F32), ((heads, rows), F32), ((heads, rows), F32), ((1, rows), F32)],
        far,
        after,
        scratch=[pltpu.VMEM((1,) + a.shape[1:] if a.ndim == 3 else a.shape, a.dtype) for a in far]
        + [pltpu.SemaphoreType.DMA((6 + len(tiles(channels)),))],
    )


def inside_kernel(model, head_size, run_ref, q_ref, step_ref, seg_ref, x_all, gate_all_, b_all, c_all, yg_ref, fg_ref, *scratch):
    x_ref, gate_ref, b_ref, c_ref, sems = scratch
    rows, channels = x_ref.shape[1:]
    mine = pl.ds(model, 1)
    cuts = tiles(channels)
    fetches = start_all(
        sems,
        [(b_all.at[mine], b_ref), (c_all.at[mine], c_ref)]
        + [pair for cut in cuts for pair in ((x_all.at[mine, :, cut], x_ref.at[:, :, cut]), (gate_all_.at[mine, :, cut], gate_ref.at[:, :, cut]))],
    )
    for fetch in fetches[:2]:
        fetch.wait()
    half = rows // 2
    lane_head = lane_heads(head_size)
    run, step, q = turned(run_ref[:, :rows]), turned(step_ref[...]), q_ref[...]
    skip = turned(run_ref[:, rows:])[:1]
    seg_row = seg_ref[...].astype(F32)
    seg_col = column(seg_row)

    products = lax.dot_general(c_ref[0], b_ref[0], (((1,), (1,)), ((), ())), preferred_element_type=F32)
    tri = lax.broadcasted_iota(jnp.int32, (half, half), 0) >= lax.broadcasted_iota(jnp.int32, (half, half), 1)
    parts = [slice(0, half), slice(half, rows)]
    masks = [tri & (seg_col[part] == seg_row[:, part]) for part in parts]
    diagonal = [products[part, part] for part in parts]
    below = jnp.where(seg_col[parts[1]] == seg_row[:, parts[0]], products[parts[1], parts[0]], 0.0).astype(BF16)
    middle = run[half - 1 : half, :]
    entry = jnp.exp(run[parts[1]] - middle)
    leave = jnp.exp(middle - run[parts[0]]) * step[parts[0]]
    factor = jnp.exp(run)
    for p in range(channels // LANES):
        cols = slice(p * LANES, (p + 1) * LANES)
        first = p * lane_head[1]
        for i, cut in enumerate(cuts):
            if cut.start == cols.start:
                fetches[2 + 2 * i].wait()
                fetches[3 + 2 * i].wait()
        x = x_ref[0, :, cols]
        xf = x.astype(F32)
        ys = []
        for part, mask, prod in zip(parts, masks, diagonal):
            y = None
            for k in range(lane_head[1]):
                h = first + k
                mixing = jnp.exp(jnp.where(mask, run[part, h : h + 1] - q[h : h + 1, part], NEG))
                term = dot((mixing * prod).astype(BF16), x[part])
                y = term if y is None else jnp.where(lane_head[0] == k, term, y)
            ys.append(y)
        sent = (xf[parts[0]] * spread(leave, lane_head, first)).astype(BF16)
        ys[1] = ys[1] + dot(below, sent) * spread(entry, lane_head, first)
        y = jnp.concatenate(ys, axis=0) + spread(skip, lane_head, first) * xf
        v = gate_ref[0, :, cols].astype(F32)
        silu = v / (1.0 + jnp.exp(-v))
        yg_ref[:, cols] = (y * silu).astype(BF16)
        fg_ref[:, cols] = (spread(factor, lane_head, first) * silu).astype(BF16)


def inside(model, head_size, x, gate, b, c, run, q, step, seg_row, after=()):
    _, rows, channels = x.shape
    far = (x, gate, b, c)
    return call(
        functools.partial(inside_kernel, model, head_size),
        f"inside_{model}",
        (run, q, step, seg_row),
        [((rows, channels), BF16)] * 2,
        far,
        after,
        scratch=[pltpu.VMEM((1,) + a.shape[1:], a.dtype) for a in far]
        + [pltpu.SemaphoreType.DMA((2 + 2 * len(tiles(channels)),))],
    )


def load_kernel(w_all, w_ref, sems):
    for fetch in start_all(sems, [(w_all.at[i], w_ref.at[i]) for i in range(w_all.shape[0])]):
        fetch.wait()


def load(w, after):
    return call(load_kernel, "load", (), [(w.shape, BF16)], (w,), after, scratch=[pltpu.SemaphoreType.DMA((w.shape[0],))])[0]


def join_kernel(state, own_ref, got_ref, out_ref):
    own, got = own_ref[...].astype(F32), got_ref[...].astype(F32)
    same = (own[state + 2 : state + 3] == got[state + 2 : state + 3]).astype(F32)
    decay = (own[state : state + 1] + own[state + 1 : state + 2]) * same
    out_ref[:state, :] = (own[:state] + decay * got[:state]).astype(BF16)
    out_ref[state:, :] = own_ref[state:, :]


def join(model, state, own, got, after=()):
    return call(functools.partial(join_kernel, state), f"join_{model}", (own, got), [(own.shape, BF16)], (), after)[0]


def gate_kernel(model, state, alone, near_ref, *refs):
    far_refs, refs = refs[:-7], refs[-7:]
    c_ref, seg_ref, yg_ref, fg_ref, gain_ref, g_ref, ss_ref = refs
    rows, channels = yg_ref.shape
    paired = True if alone else lax.axis_index("seq") % 2 == 1
    seg_col = column(seg_ref[...])
    squares = jnp.zeros((8, rows), F32)
    for cols in tiles(channels):
        near = near_ref[:, cols].astype(F32)
        far = far_refs[0][:, cols].astype(F32)
        for ref in far_refs[1:]:
            far = far + ref[:, cols].astype(F32)
        last_near, last_far = near[state + 2 : state + 3], far[state + 2 : state + 3]
        decay = (near[state : state + 1] + near[state + 1 : state + 2]) * (last_near == last_far).astype(F32)
        entering = (near[:state] + jnp.where(paired, decay, 1.0) * far[:state]).astype(BF16)
        anchor = jnp.where(paired, last_near, last_far)[:, :1]
        reached = (seg_col == anchor).astype(F32)
        gated = yg_ref[:, cols].astype(F32) + reached * fg_ref[:, cols].astype(F32) * dot(c_ref[model], entering)
        g_ref[:, cols] = (gated * gain_ref[model : model + 1, cols]).astype(BF16)
        ones = jnp.ones((8, cols.stop - cols.start), BF16)
        squares += lax.dot_general(
            ones, (gated * gated).astype(BF16), (((1,), (1,)), ((), ())), preferred_element_type=F32
        )
    ss_ref[...] = squares


def gate_all(model, alone, near, far, c, seg_row, yg, fg, gain, after=()):
    return call(
        functools.partial(gate_kernel, model, c.shape[2], alone),
        f"gated_{model}",
        (near, *far, c, seg_row, yg, fg, gain),
        [(yg.shape, BF16), ((8, yg.shape[0]), F32)],
        (),
        after,
    )


def project_kernel(groups, forward, *refs):
    shapes = [(model, [len(block) for block in blocks]) for model, blocks in groups]
    number = sum(sum(shape) for _, shape in shapes)
    given, (w_ref, keep_ref, *refs) = refs[:number], refs[number:]
    count = len(shapes[0][1])
    half, width = keep_ref.shape[1:]
    send_refs, refs = refs[:count], refs[count:]
    first = lax.axis_index("head") % 2 == 0
    if forward:
        refs[0][...] = given[0][:half, :]
        refs[1][...] = given[1][half:, :]
    at = 0
    for i, (model, shape) in enumerate(shapes):
        for k, pieces in enumerate(shape):
            if pieces == 1:
                lhs = given[at]
            else:
                lhs = refs[-1]
                lhs[:half, :] = given[at][...]
                lhs[half:, :] = given[at + 1][...]
            at += pieces
            for cols in tiles(width):
                result = dot(lhs[...], w_ref[model, :, cols]).astype(BF16)
                keep_ref[i * count + k, :, cols] = jnp.where(first, result[:half], result[half:])
                send_refs[k][i, :, cols] = jnp.where(first, result[half:], result[:half])


def project(name, groups, w, after=(), forward=False):
    flat = [a for _, blocks in groups for block in blocks for a in block]
    depth, width = w.shape[1:]
    n = len(groups[0][1])
    half = sum(a.shape[0] for a in flat) // (2 * n * len(groups))
    return call(
        functools.partial(project_kernel, groups, forward),
        name,
        (*flat, w),
        [((len(groups) * n, half, width), BF16)]
        + [((len(groups), half, width), BF16)] * n
        + [((half, depth), BF16)] * (2 * forward),
        (),
        after,
        scratch=[pltpu.VMEM((2 * half, depth), BF16)],
    )


def release(name, arrays, after):
    return call(lambda *refs: None, name, (), [], (), after, carry=arrays)


def pair_kernel(places, turn_at, keep0, got0, keep1, got1, first_ref, second_ref):
    a = keep0[places[0]].astype(F32) + got0[places[1]].astype(F32)
    b = keep1[places[2]].astype(F32) + got1[places[3]].astype(F32)
    away = lax.axis_index("seq") + lax.axis_index("head") // 2
    turned_round = away % 2 == turn_at
    first_ref[...] = jnp.where(turned_round, b, a).astype(BF16)
    second_ref[...] = jnp.where(turned_round, a, b).astype(BF16)


def pair_sums(name, turn_at, one, other, after=()):
    return call(
        functools.partial(pair_kernel, (one[1], one[3], other[1], other[3]), turn_at),
        name,
        (one[0], one[2], other[0], other[2]),
        [(one[0].shape[1:], BF16)] * 2,
        (),
        after,
    )


def add_kernel(own_ref, got_ref, out_ref):
    out_ref[...] = (own_ref[...].astype(F32) + got_ref[...].astype(F32)).astype(BF16)


def add(name, own, got, after=()):
    return call(add_kernel, name, (own, got), [(own.shape, BF16)], (), after)[0]


def first_sums_kernel(one_ref, other_ref, out_ref):
    rows = lax.broadcasted_iota(jnp.int32, out_ref.shape, 0)
    out_ref[...] = jnp.where(rows < 4, one_ref[...], other_ref[...])


def sums_kernel(one_ref, other_ref, out_ref):
    out_ref[...] = one_ref[...] + other_ref[...]


def last_kernel(total, model, ss_ref, *refs):
    beside, opposite, out_ref = refs[:3], refs[3:6], refs[6]
    s, h = lax.axis_index("seq"), lax.axis_index("head")
    straight = (s == h // 2) | (s + h // 2 == 3)
    half = out_ref.shape[1]
    row = ss_ref[4 * model : 4 * model + 1, :]
    row = jnp.where(h % 2 == 0, row[:, :half], row[:, half:])
    scale = column(lax.rsqrt(row / total + EPS))

    def write(refs):
        value = refs[0][...].astype(F32)
        for ref in refs[1:]:
            value = value + ref[...].astype(F32)
        out_ref[0] = (value * scale).astype(BF16)

    pl.when(straight)(lambda: write(opposite))
    pl.when(~straight)(lambda: write(beside))


def last(model, total, ss, beside, opposite, before, after=()):
    half, width = beside[0].shape
    operands = (ss, *beside, *opposite)
    earlier = () if before is None else (before,)
    kernel = functools.partial(last_kernel, total, model)
    return pl.pallas_call(
        lambda *refs: kernel(*refs[: len(operands)], refs[-1]),
        name=f"last_{model}",
        grid=(1,),
        in_specs=[IN_VMEM] * (len(operands) + len(after))
        + [ANYWHERE] * len(earlier),
        out_specs=pl.BlockSpec((1, half, width), lambda i: (model, 0, 0)),
        out_shape=jax.ShapeDtypeStruct((2, half, width), BF16),
        input_output_aliases={len(operands) + len(after): 0} if earlier else {},
        compiler_params=pltpu.CompilerParams(vmem_limit_bytes=SCOPE),
        cost_estimate=pl.CostEstimate(flops=1, bytes_accessed=1, transcendentals=0),
    )(*operands, *after, *earlier)


def xor_pairs(n, k):
    return [(i, i ^ k) for i in range(n)]


def fast(x, gate, b, c, raw, bias, rate, skip, gain, w, seg):
    raw = jnp.swapaxes(raw, 1, 2)
    head_size = x.shape[2] // raw.shape[1]
    state = b.shape[2]
    n_seq, n_head = lax.axis_size("seq"), lax.axis_size("head")
    total = x.shape[2] * n_head
    seg_row = seg.reshape(1, -1)
    def flat(si, zi, ci):
        return si * n_head + zi * 2 + ci

    def sends(kinds, turn):
        pairs = []
        for si in range(n_seq):
            owners = [si ^ k for k in kinds]
            if 0 in owners:
                steps = ([(1, 0), (3, 2), (2, 3), (0, 1)], [], [(2, 0), (1, 3)])[turn]
            else:
                steps = [(o ^ (1, 3, 2)[turn], o) for o in owners]
            pairs += [(flat(si, a, ci), flat(si, o, ci)) for a, o in steps for ci in range(2)]
        return pairs

    ring = [(0, 1), (2, 3)]
    across = lambda a: lax.ppermute(a, "head", xor_pairs(n_head, 1))
    beside = lambda a, k: lax.ppermute(a, "seq", xor_pairs(n_seq, k))
    ss = jnp.zeros((8, x.shape[1]), F32)

    x, gate, raw, bias, rate, skip, w = (
        pltpu.with_memory_space_constraint(a, pltpu.HBM) for a in (x, gate, raw, bias, rate, skip, w)
    )
    b_far, c_far, seg_far = (pltpu.with_memory_space_constraint(a, pltpu.HBM) for a in (b, c, seg_row))
    msg0, *scan0 = prep(0, head_size, x, b_far, raw, bias, rate, skip, seg_far)
    near0 = lax.ppermute(msg0, "seq", ring)
    msg1, *scan1 = prep(1, head_size, x, b_far, raw, bias, rate, skip, seg_far, (msg0, *scan0))
    near1 = lax.ppermute(msg1, "seq", ring)
    yg0, fg0 = inside(0, head_size, x, gate, b_far, c_far, *scan0, (msg0, msg1, *scan1))
    end0 = join(0, state, msg0, near0, (yg0, fg0, msg1, scan0[-1], *scan1))
    far0 = [lax.ppermute(end0, "seq", [(1, t)]) for t in (2, 3)]
    yg1, fg1 = inside(1, head_size, x, gate, b_far, c_far, *scan1, (end0, yg0, fg0, near0, msg1, scan0[-1]))
    end1 = join(1, state, msg1, near1, (yg0, fg0, near0, yg1, fg1, scan0[-1], scan1[-1], *far0))
    far1 = [lax.ppermute(end1, "seq", [(1, t)]) for t in (2, 3)]
    g0, ss0 = gate_all(0, False, near0, far0, c, scan0[-1], yg0, fg0, gain, (end1, near1, yg1, fg1, scan1[-1]))
    x0, y0 = beside(g0, 1), beside(g0, 2)
    w = load(w, (g0, ss0, near1, yg1, fg1, scan1[-1]))
    g1, ss1 = gate_all(1, False, near1, far1, c, scan1[-1], yg1, fg1, gain, (w, g0, ss0))
    x1, y1 = beside(g1, 1), beside(g1, 2)
    ss = call(first_sums_kernel, "sums_0", (ss0, ss1), [(ss0.shape, F32)], (), (w, g0, g1))[0]
    for k in (1, 2, 4):
        other = lax.ppermute(ss, "head", xor_pairs(n_head, k))
        ss = call(sums_kernel, f"sums_{k}", (ss, other), [(ss.shape, F32)], (), (w, g0, g1))[0]

    def both(forwarded):
        return beside(forwarded[0], 2), beside(forwarded[1], 1)

    def turn(value, kinds, i):
        return lax.ppermute(value, ("seq", "head"), sends(kinds, i))

    xy, od = (1, 2), (0, 3)
    keep_o, send_o = project("own", [(0, [(g0,)]), (1, [(g1,)])], w)
    keep_n0, *send_n0, f0, l0 = project(
        "next_0", [(0, [(x0,), (y0,)])], w, (keep_o, send_o, ss), True
    )
    got_n0 = [across(a) for a in send_n0]
    first_n0, second_n0 = pair_sums(
        "sum_next_0", 1, (keep_n0, 0, got_n0[0], 0), (keep_n0, 1, got_n0[1], 0), (w, keep_o, send_o, f0, l0)
    )
    one_n0, two_n0 = turn(first_n0, xy, 0), turn(first_n0, xy, 1)
    f0, l0, send_o = release("release_0", (f0, l0, send_o), (x1, y1, first_n0, second_n0, w, keep_o))
    d0, got_o = both((f0, l0)), across(send_o)
    join_n0 = add("add_next_0", second_n0, one_n0, (f0, two_n0, got_o, w, keep_o, x1, y1))
    three_n0 = turn(join_n0, xy, 2)
    own = (keep_o, got_o)
    keep_n1, *send_n1, f1, l1 = project(
        "next_1", [(1, [(x1,), (y1,)])], w, (join_n0, two_n0, *own), True
    )
    got_n1 = [across(a) for a in send_n1]
    held = (w, *own, join_n0, two_n0)
    f1, l1 = release("release_1", (f1, l1), (*d0, keep_n1, *held))
    d1 = both((f1, l1))
    first_n1, second_n1 = pair_sums(
        "sum_next_1", 1, (keep_n1, 0, got_n1[0], 0), (keep_n1, 1, got_n1[1], 0), (f1, three_n0, *d0, *held)
    )
    one_n1, two_n1 = turn(first_n1, xy, 0), turn(first_n1, xy, 1)
    held = (*own, join_n0, two_n0, three_n0)
    keep_d0, send_d0 = project("opposite_0", [(0, [d0])], w, (first_n1, second_n1, *held))
    got_d0 = across(send_d0)
    keep_d1, send_d1 = project("opposite_1", [(1, [d1])], w, (keep_d0, second_n1, *held))
    got_d1 = across(send_d1)
    join_n1 = add("add_next_1", second_n1, one_n1, (keep_d1, two_n1, keep_d0, *held))
    three_n1 = turn(join_n1, xy, 2)
    held = (*held, join_n1, two_n1)
    first_d0, second_d0 = pair_sums(
        "sum_opposite_0", 0, (keep_o, 0, got_o, 0), (keep_d0, 0, got_d0, 0), (keep_d1, *held)
    )
    one_d0, two_d0 = turn(first_d0, od, 0), turn(first_d0, od, 1)
    held = (join_n0, two_n0, three_n0, join_n1, two_n1)
    first_d1, second_d1 = pair_sums(
        "sum_opposite_1", 0, (keep_o, 1, got_o, 1), (keep_d1, 0, got_d1, 0), (first_d0, second_d0, *held)
    )
    one_d1, two_d1 = turn(first_d1, od, 0), turn(first_d1, od, 1)
    join_d0 = add("add_opposite_0", second_d0, one_d0, (two_d0, first_d1, second_d1, three_n1, *held))
    three_d0 = turn(join_d0, od, 2)
    held = (*held, three_n1, two_d0, join_d0)
    join_d1 = add("add_opposite_1", second_d1, one_d1, (two_d1, *held))
    three_d1 = turn(join_d1, od, 2)
    ss, = release("release_sums", (ss,), (join_n1,))
    ss = lax.ppermute(
        ss, ("seq", "head"),
        [(flat(zi, si, ci), flat(si, zi, ci)) for si in range(n_seq) for zi in range(n_seq) for ci in range(2)],
    )
    held = (join_n1, two_n1, three_n1, join_d1, two_d1)
    out = last(0, total, ss, (join_n0, two_n0, three_n0), (join_d0, two_d0, three_d0), None, held)
    return last(1, total, ss, (join_n1, two_n1, three_n1), (join_d1, two_d1, three_d1), out)


def plain(x, gate, b, c, raw, bias, rate, skip, gain, w, seg):
    raw = jnp.swapaxes(raw, 1, 2)
    head_size = x.shape[2] // raw.shape[1]
    state = b.shape[2]
    n_seq, n_head = lax.axis_size("seq"), lax.axis_size("head")
    total = x.shape[2] * n_head
    seg_row = seg.reshape(1, -1)
    s, h = lax.axis_index("seq"), lax.axis_index("head")
    gs, sums = [], []
    for m in range(2):
        msg, *scan = prep(m, head_size, x, b, raw, bias, rate, skip, seg_row)
        every = lax.all_gather(msg, "seq").astype(F32)
        entering, before = jnp.zeros_like(every[0]), every[0]
        for k in range(n_seq - 1):
            now = every[k]
            same = (now[state + 2] == before[state + 2]).astype(F32)
            decay = (now[state] + now[state + 1]) * same
            new = jnp.concatenate([now[:state] + decay * entering[:state], now[state:]])
            entering = jnp.where(k < s, new, entering)
            before = now
        yg, fg = inside(m, head_size, x, gate, b, c, *scan)
        near = entering.astype(BF16)
        g, ss = gate_all(m, True, near, [jnp.zeros_like(near)], c, scan[-1], yg, fg, gain)
        gs.append(g)
        sums.append(ss[0])
    g = lax.all_gather(jnp.stack(gs), "seq", axis=1, tiled=True)
    terms = jnp.einsum("mtk,mkd->mtd", g, w, preferred_element_type=F32)
    summed = lax.psum_scatter(terms.astype(BF16), "head", scatter_dimension=1, tiled=True)
    squares = lax.all_gather(lax.psum(jnp.stack(sums), "head"), "seq", axis=1, tiled=True)
    mine = lax.dynamic_slice_in_dim(squares, h * summed.shape[1], summed.shape[1], axis=1)
    return (summed.astype(F32) * lax.rsqrt(mine / total + EPS)[:, :, None]).astype(BF16)


def solution(mesh):
    placed = (
        P(None, "seq", "head"),
        P(None, "seq", "head"),
        P(None, "seq", None),
        P(None, "seq", None),
        P(None, "seq", "head"),
        P(None, "head"),
        P(None, "head"),
        P(None, "head"),
        P(None, "head"),
        P(None, "head", "seq"),
        P("seq"),
    )
    local = fast if mesh.shape["seq"] == 4 and mesh.shape["head"] == 8 else plain
    return jax.shard_map(
        local, mesh=mesh, in_specs=placed, out_specs=P(None, "head", "seq"), check_vma=False
    )
```

```python
import functools
import jax
import jax.numpy as jnp
from jax import lax
from jax.experimental import pallas as pl
from jax.experimental.pallas import tpu as pltpu
from jax.sharding import PartitionSpec as P

F32, BF16 = jnp.float32, jnp.bfloat16
LANES = 128
EXTRA = 16
NEG = -1e30
EPS = 1e-05
IN_VMEM = pl.BlockSpec(memory_space=pltpu.VMEM)
ANYWHERE = pl.BlockSpec(memory_space=pl.ANY)
SCOPE = 16 * 1024 * 1024
HEAVY = 10**11


def dot(a, b):
    return jnp.dot(a, b, preferred_element_type=F32)


def call(kernel, name, operands, outs, far=(), after=(), carry=(), scratch=(), weight=1, **kw):
    given, idle = len(operands) + len(far), len(after) + len(carry)

    def body(*refs):
        rest = refs[given + idle :]
        return kernel(*refs[:given], *rest[: len(outs)], *rest[len(outs) + len(carry) :])

    return pl.pallas_call(
        body,
        name=name,
        in_specs=[IN_VMEM] * len(operands)
        + [ANYWHERE] * len(far)
        + [IN_VMEM] * len(after)
        + [ANYWHERE] * len(carry),
        out_specs=[IN_VMEM] * len(outs) + [ANYWHERE] * len(carry),
        out_shape=[pltpu.VMEM(shape, dtype) for shape, dtype in outs]
        + [jax.ShapeDtypeStruct(a.shape, a.dtype) for a in carry],
        scratch_shapes=list(scratch),
        input_output_aliases={given + len(after) + i: len(outs) + i for i in range(len(carry))},
        compiler_params=pltpu.CompilerParams(vmem_limit_bytes=SCOPE),
        cost_estimate=pl.CostEstimate(flops=weight, bytes_accessed=1, transcendentals=0),
        **kw,
    )(*operands, *far, *after, *carry)


def start_all(sems, pairs):
    fetches = [pltpu.make_async_copy(source, target, sems.at[i]) for i, (source, target) in enumerate(pairs)]
    for fetch in fetches:
        fetch.start()
    return fetches


def tiles(width):
    tile = min(512, width)
    return [slice(i, i + tile) for i in range(0, width, tile)]


def lane_split(head_size, shape):
    return lax.broadcasted_iota(jnp.int32, shape, 1) // head_size


def spread(values, lane_head, first):
    shape = (values.shape[0], LANES)
    out = jnp.broadcast_to(values[:, first : first + 1], shape)
    for k in range(1, lane_head[1]):
        out = jnp.where(lane_head[0] == k, values[:, first + k : first + k + 1], out)
    return out


def lane_heads(head_size):
    return (lane_split(head_size, (1, LANES)), LANES // head_size)


def column(row):
    return jnp.broadcast_to(row, (LANES, row.shape[1])).T[:, :1]


def head_column(row):
    heads = row.shape[1]
    padded = jnp.concatenate([row, jnp.zeros((1, LANES - heads), F32)], axis=1)
    return jnp.broadcast_to(padded, (LANES, LANES)).T[:heads, :1]


def turned(values):
    heads, rows = values.shape
    return jnp.concatenate([values, jnp.zeros((LANES - heads, rows), F32)], axis=0).T[:, :heads]


def prep_kernel(model, head_size, x_all, b_all, raw_all, bias_all, rate_all, skip_all, seg_all, msg_ref, run_ref, q_ref, step_ref, row_ref, *scratch):
    x_ref, b_ref, raw_ref, bias_ref, rate_ref, skip_ref, seg_ref, sems = scratch
    rows, channels = x_ref.shape[1:]
    mine = pl.ds(model, 1)
    cuts = tiles(channels)
    fetches = start_all(
        sems,
        [(raw_all.at[mine], raw_ref), (bias_all, bias_ref), (rate_all, rate_ref), (skip_all, skip_ref)]
        + [(seg_all, seg_ref), (b_all.at[mine], b_ref)]
        + [(x_all.at[mine, :, cut], x_ref.at[:, :, cut]) for cut in cuts],
    )
    for fetch in fetches[:6]:
        fetch.wait()
    heads = raw_ref.shape[1]
    state = b_ref.shape[2]
    step_t = jax.nn.softplus(raw_ref[0] + head_column(bias_ref[model : model + 1, :]))
    log_decay = -head_column(rate_ref[model : model + 1, :]) * step_t
    earlier = lax.broadcasted_iota(jnp.int32, (rows, rows), 0)
    later = lax.broadcasted_iota(jnp.int32, (rows, rows), 1)
    tri = (later >= earlier).astype(F32)
    run_t = jnp.dot(log_decay, tri, precision=lax.Precision.HIGHEST, preferred_element_type=F32)
    run, step = turned(run_t), turned(step_t)
    run_ref[:, :rows] = run_t
    run_ref[:, rows:] = jnp.broadcast_to(head_column(skip_ref[model : model + 1, :]), (heads, LANES))
    step_ref[...] = step_t
    q_ref[...] = run_t - jnp.log(step_t)
    seg_row = seg_ref[...].astype(F32)
    row_ref[...] = seg_row
    seg_col = column(seg_row)
    last = seg_row[:, rows - 1 :]
    total = run[rows - 1 :, :]
    tail = jnp.exp(total - run) * step * (seg_col == last).astype(F32)
    etot = jnp.exp(total)
    b_t = b_ref[0].astype(F32).T.astype(BF16)
    lane_head = lane_heads(head_size)
    row_id = lax.broadcasted_iota(jnp.int32, (EXTRA, LANES), 0)
    for p in range(channels // LANES):
        cols = slice(p * LANES, (p + 1) * LANES)
        first = p * lane_head[1]
        for cut, fetch in zip(cuts, fetches[6:]):
            if cut.start == cols.start:
                fetch.wait()
        xw = (x_ref[0, :, cols].astype(F32) * spread(tail, lane_head, first)).astype(BF16)
        msg_ref[:state, cols] = dot(b_t, xw).astype(BF16)
        decay = spread(etot, lane_head, first)
        high = decay.astype(BF16).astype(F32)
        extra = jnp.where(row_id == 0, high, jnp.where(row_id == 1, decay - high, jnp.where(row_id == 2, last, 0.0)))
        msg_ref[state:, cols] = extra.astype(BF16)


def prep(model, head_size, x, b, raw, bias, rate, skip, seg_row, after=()):
    _, rows, channels = x.shape
    heads, state = raw.shape[1], b.shape[2]
    far = (x, b, raw, bias, rate, skip, seg_row)
    return call(
        functools.partial(prep_kernel, model, head_size),
        f"prep_{model}",
        (),
        [((state + EXTRA, channels), BF16), ((heads, rows + LANES), F32), ((heads, rows), F32), ((heads, rows), F32), ((1, rows), F32)],
        far,
        after,
        scratch=[pltpu.VMEM((1,) + a.shape[1:] if a.ndim == 3 else a.shape, a.dtype) for a in far]
        + [pltpu.SemaphoreType.DMA((6 + len(tiles(channels)),))],
    )


def inside_kernel(model, head_size, run_ref, q_ref, step_ref, seg_ref, x_all, gate_all_, b_all, c_all, yg_ref, fg_ref, *scratch):
    x_ref, gate_ref, b_ref, c_ref, sems = scratch
    rows, channels = x_ref.shape[1:]
    mine = pl.ds(model, 1)
    cuts = tiles(channels)
    fetches = start_all(
        sems,
        [(b_all.at[mine], b_ref), (c_all.at[mine], c_ref)]
        + [pair for cut in cuts for pair in ((x_all.at[mine, :, cut], x_ref.at[:, :, cut]), (gate_all_.at[mine, :, cut], gate_ref.at[:, :, cut]))],
    )
    for fetch in fetches[:2]:
        fetch.wait()
    half = rows // 2
    lane_head = lane_heads(head_size)
    run, step, q = turned(run_ref[:, :rows]), turned(step_ref[...]), q_ref[...]
    skip = turned(run_ref[:, rows:])[:1]
    seg_row = seg_ref[...].astype(F32)
    seg_col = column(seg_row)

    products = lax.dot_general(c_ref[0], b_ref[0], (((1,), (1,)), ((), ())), preferred_element_type=F32)
    tri = lax.broadcasted_iota(jnp.int32, (half, half), 0) >= lax.broadcasted_iota(jnp.int32, (half, half), 1)
    parts = [slice(0, half), slice(half, rows)]
    masks = [tri & (seg_col[part] == seg_row[:, part]) for part in parts]
    diagonal = [products[part, part] for part in parts]
    below = jnp.where(seg_col[parts[1]] == seg_row[:, parts[0]], products[parts[1], parts[0]], 0.0).astype(BF16)
    middle = run[half - 1 : half, :]
    entry = jnp.exp(run[parts[1]] - middle)
    leave = jnp.exp(middle - run[parts[0]]) * step[parts[0]]
    factor = jnp.exp(run)
    for p in range(channels // LANES):
        cols = slice(p * LANES, (p + 1) * LANES)
        first = p * lane_head[1]
        for i, cut in enumerate(cuts):
            if cut.start == cols.start:
                fetches[2 + 2 * i].wait()
                fetches[3 + 2 * i].wait()
        x = x_ref[0, :, cols]
        xf = x.astype(F32)
        ys = []
        for part, mask, prod in zip(parts, masks, diagonal):
            y = None
            for k in range(lane_head[1]):
                h = first + k
                mixing = jnp.exp(jnp.where(mask, run[part, h : h + 1] - q[h : h + 1, part], NEG))
                term = dot((mixing * prod).astype(BF16), x[part])
                y = term if y is None else jnp.where(lane_head[0] == k, term, y)
            ys.append(y)
        sent = (xf[parts[0]] * spread(leave, lane_head, first)).astype(BF16)
        ys[1] = ys[1] + dot(below, sent) * spread(entry, lane_head, first)
        y = jnp.concatenate(ys, axis=0) + spread(skip, lane_head, first) * xf
        v = gate_ref[0, :, cols].astype(F32)
        silu = v / (1.0 + jnp.exp(-v))
        yg_ref[:, cols] = (y * silu).astype(BF16)
        fg_ref[:, cols] = (spread(factor, lane_head, first) * silu).astype(BF16)


def inside(model, head_size, x, gate, b, c, run, q, step, seg_row, after=()):
    _, rows, channels = x.shape
    far = (x, gate, b, c)
    return call(
        functools.partial(inside_kernel, model, head_size),
        f"inside_{model}",
        (run, q, step, seg_row),
        [((rows, channels), BF16)] * 2,
        far,
        after,
        scratch=[pltpu.VMEM((1,) + a.shape[1:], a.dtype) for a in far]
        + [pltpu.SemaphoreType.DMA((2 + 2 * len(tiles(channels)),))],
    )


def load_kernel(w_all, gain_all, w_ref, inverse_ref, gain_ref, sems):
    fetches = start_all(sems, [(gain_all, gain_ref)] + [(w_all.at[i], w_ref.at[i]) for i in range(w_all.shape[0])])
    fetches[0].wait()
    inverse_ref[...] = 1.0 / gain_ref[...]
    for fetch in fetches[1:]:
        fetch.wait()


def load(w, gain, after):
    return call(
        load_kernel,
        "load",
        (),
        [(w.shape, BF16), (gain.shape, F32)],
        (w, gain),
        after,
        scratch=[pltpu.VMEM(gain.shape, F32), pltpu.SemaphoreType.DMA((1 + w.shape[0],))],
    )


def join_kernel(state, own_ref, got_ref, out_ref):
    own, got = own_ref[...].astype(F32), got_ref[...].astype(F32)
    same = (own[state + 2 : state + 3] == got[state + 2 : state + 3]).astype(F32)
    decay = (own[state : state + 1] + own[state + 1 : state + 2]) * same
    out_ref[:state, :] = (own[:state] + decay * got[:state]).astype(BF16)
    out_ref[state:, :] = own_ref[state:, :]


def join(model, state, own, got, after=()):
    return call(functools.partial(join_kernel, state), f"join_{model}", (own, got), [(own.shape, BF16)], (), after)[0]


def gate_kernel(model, state, alone, near_ref, *refs):
    further = 7 if alone else 6
    far_refs, refs = refs[:-further], refs[-further:]
    c_ref, seg_ref, yg_ref, fg_ref, gain_ref, g_ref, *ss_ref = refs
    rows, channels = yg_ref.shape
    paired = True if alone else lax.axis_index("seq") % 2 == 1
    seg_col = column(seg_ref[...])
    squares = jnp.zeros((8, rows), F32)
    for cols in tiles(channels):
        near = near_ref[:, cols].astype(F32)
        far = far_refs[0][:, cols].astype(F32)
        for ref in far_refs[1:]:
            far = far + ref[:, cols].astype(F32)
        last_near, last_far = near[state + 2 : state + 3], far[state + 2 : state + 3]
        decay = (near[state : state + 1] + near[state + 1 : state + 2]) * (last_near == last_far).astype(F32)
        entering = (near[:state] + jnp.where(paired, decay, 1.0) * far[:state]).astype(BF16)
        anchor = jnp.where(paired, last_near, last_far)[:, :1]
        reached = (seg_col == anchor).astype(F32)
        gated = yg_ref[:, cols].astype(F32) + reached * fg_ref[:, cols].astype(F32) * dot(c_ref[model], entering)
        g_ref[:, cols] = (gated * gain_ref[model : model + 1, cols]).astype(BF16)
        if alone:
            ones = jnp.ones((8, cols.stop - cols.start), BF16)
            squares += lax.dot_general(
                ones, (gated * gated).astype(BF16), (((1,), (1,)), ((), ())), preferred_element_type=F32
            )
    if alone:
        ss_ref[0][...] = squares


def gate_all(model, alone, near, far, c, seg_row, yg, fg, gain, after=()):
    return call(
        functools.partial(gate_kernel, model, c.shape[2], alone),
        f"gated_{model}",
        (near, *far, c, seg_row, yg, fg, gain),
        [(yg.shape, BF16)] + [((8, yg.shape[0]), F32)] * alone,
        (),
        after,
    )


def project_kernel(model, shapes, forward, sends, *refs):
    given, (w_ref, inverse_ref, keep_ref, *refs) = refs[: sum(shapes)], refs[sum(shapes) :]
    count = len(shapes)
    half, width = keep_ref.shape[1], w_ref.shape[2]
    send_refs, (*refs, lhs) = refs[: len(sends)], refs[len(sends) :]
    first = lax.axis_index("head") % 2 == 0
    if forward:
        refs[0][...] = given[0][:half, :]
        refs[1][...] = given[1][half:, :]
    row = 0
    for ref in given:
        lhs[row : row + ref.shape[0], :] = ref[...]
        row += ref.shape[0]
    squares = jnp.zeros((row, LANES), F32)
    for part in tiles(w_ref.shape[1]):
        gated = lhs[:, part].astype(F32) * inverse_ref[model : model + 1, part]
        squares += dot((gated * gated).astype(BF16), jnp.ones((part.stop - part.start, LANES), BF16))

    def put(result, ref, blocks, start, at, size):
        for k in range(count):
            early = result[2 * k * half : (2 * k + 1) * half].astype(BF16)
            late = result[(2 * k + 1) * half : (2 * k + 2) * half].astype(BF16)
            keep_ref[k, :, pl.ds(start + at, size)] = jnp.where(first, early, late)
            which, place = (ref, blocks.index(k)) if k in blocks else (None, 0)
            if which is None:
                which, place = [(r, part.index(k)) for r, (part, *_) in zip(send_refs, sends) if k in part][0]
            which[place, :, pl.ds(at, size)] = jnp.where(first, late, early)

    tile = min(512, width)
    done = set()
    for ref, (blocks, start, stop) in zip(send_refs, sends):
        if start in done:
            continue
        done.add(start)

        def step(j, _, ref=ref, blocks=blocks, start=start):
            at = pl.multiple_of(j * tile, tile)
            put(dot(lhs[...], w_ref[model, :, pl.ds(start + at, tile)]), ref, blocks, start, at, tile)
            return 0

        lax.fori_loop(0, (min(stop, width) - start) // tile, step, 0)
        if stop > width:
            put(squares, ref, blocks, start, width - start, LANES)


def project(name, model, blocks, weights, after=(), forward=False, split=None, weight=1):
    w, inverse = weights
    flat = [a for block in blocks for a in block]
    depth, width = w.shape[1:]
    n, full = len(blocks), width + LANES
    half = sum(a.shape[0] for a in flat) // (2 * n)
    if split == "blocks":
        sends = [([k], 0, full) for k in range(n)]
    elif split == "columns":
        sends = [(list(range(n)), 0, width // 2), (list(range(n)), width // 2, full)]
    else:
        sends = [(list(range(n)), 0, full)]
    return call(
        functools.partial(project_kernel, model, [len(block) for block in blocks], forward, sends),
        name,
        (*flat, w, inverse),
        [((n, half, full), BF16)]
        + [((len(part), half, stop - start), BF16) for part, start, stop in sends]
        + [((half, depth), BF16)] * (2 * forward),
        (),
        after,
        scratch=[pltpu.VMEM((2 * half * n, depth), BF16)],
        weight=weight,
    )


def release(name, arrays, after, weight=1):
    return call(lambda *refs: None, name, (), [], (), after, carry=arrays, weight=weight)


def pair_kernel(places, counts, *refs):
    keeps, gots = refs[:2], (refs[2 : 2 + counts[0]], refs[2 + counts[0] : 2 + sum(counts)])
    first_ref, second_ref = refs[-2:]
    turned_round = (lax.axis_index("seq") // 2 + lax.axis_index("head") // 2) % 2 == 0

    def ends(pieces):
        stops = [0]
        for ref in pieces:
            stops.append(stops[-1] + ref.shape[2])
        return stops

    bounds = sorted({*ends(gots[0]), *ends(gots[1])})
    for start, stop in zip(bounds, bounds[1:]):
        sums = []
        for keep, pieces, (at, got_at) in zip(keeps, gots, places):
            stops = ends(pieces)
            piece = max(i for i, lower in enumerate(stops) if lower <= start)
            got = pieces[piece][got_at, :, start - stops[piece] : stop - stops[piece]]
            sums.append(keep[at, :, start:stop].astype(F32) + got.astype(F32))
        first_ref[:, start:stop] = jnp.where(turned_round, sums[1], sums[0]).astype(BF16)
        second_ref[:, start:stop] = jnp.where(turned_round, sums[0], sums[1]).astype(BF16)


def pair_sums(name, one, other, after=()):
    return call(
        functools.partial(pair_kernel, ((one[1], one[3]), (other[1], other[3])), (len(one[2]), len(other[2]))),
        name,
        (one[0], other[0], *one[2], *other[2]),
        [(one[0].shape[1:], BF16)] * 2,
        (),
        after,
    )


def add_kernel(own_ref, got_ref, out_ref):
    out_ref[...] = (own_ref[...].astype(F32) + got_ref[...].astype(F32)).astype(BF16)


def add(name, own, got, after=()):
    return call(add_kernel, name, (own, got), [(own.shape, BF16)], (), after)


def last_kernel(total, model, *refs):
    beside, opposite, out_ref = refs[:4], refs[4:8], refs[8]
    width = out_ref.shape[2]
    s, z = lax.axis_index("seq"), lax.axis_index("head") // 2
    straight = (s == z) | (s + z == 3)
    inner = (z == 1) | (z == 2)

    def write(refs):
        value = jnp.where(inner, refs[0][...], refs[1][...]).astype(F32)
        for ref in refs[2:]:
            value = value + ref[...].astype(F32)
        scale = lax.rsqrt(value[:, width : width + 1] / total + EPS)
        out_ref[0] = (value[:, :width] * scale).astype(BF16)

    pl.when(straight)(lambda: write(opposite))
    pl.when(~straight)(lambda: write(beside))


def last(model, total, beside, opposite, before, after=()):
    half, width = beside[0].shape[0], beside[0].shape[1] - LANES
    operands = (*beside, *opposite)
    earlier = () if before is None else (before,)
    kernel = functools.partial(last_kernel, total, model)
    return pl.pallas_call(
        lambda *refs: kernel(*refs[: len(operands)], refs[-1]),
        name=f"last_{model}",
        grid=(1,),
        in_specs=[IN_VMEM] * (len(operands) + len(after))
        + [ANYWHERE] * len(earlier),
        out_specs=pl.BlockSpec((1, half, width), lambda i: (model, 0, 0)),
        out_shape=jax.ShapeDtypeStruct((2, half, width), BF16),
        input_output_aliases={len(operands) + len(after): 0} if earlier else {},
        compiler_params=pltpu.CompilerParams(vmem_limit_bytes=SCOPE),
        cost_estimate=pl.CostEstimate(flops=1 if earlier else HEAVY, bytes_accessed=1, transcendentals=0),
    )(*operands, *after, *earlier)


def xor_pairs(n, k):
    return [(i, i ^ k) for i in range(n)]


def fast(x, gate, b, c, raw, bias, rate, skip, gain, w, seg):
    raw = jnp.swapaxes(raw, 1, 2)
    head_size = x.shape[2] // raw.shape[1]
    state = b.shape[2]
    n_seq, n_head = lax.axis_size("seq"), lax.axis_size("head")
    total = x.shape[2] * n_head
    seg_row = seg.reshape(1, -1)
    def flat(si, zi, ci):
        return si * n_head + zi * 2 + ci

    def sends(kinds, turn):
        pairs = []
        for si in range(n_seq):
            if 0 in [si ^ k for k in kinds]:
                steps = ([(1, 0), (3, 2), (2, 3), (0, 1)], [], [(2, 0), (1, 3)])[turn]
            else:
                steps = ([(0, 1), (3, 2)], [(0, 1), (3, 2)], [(1, 2), (2, 1)])[turn]
            pairs += [(flat(si, a, ci), flat(si, o, ci)) for a, o in steps for ci in range(2)]
        return pairs

    ring = [(0, 1), (2, 3)]
    across = lambda a: lax.ppermute(a, "head", xor_pairs(n_head, 1))
    beside = lambda a, k: lax.ppermute(a, "seq", xor_pairs(n_seq, k))
    ss = jnp.zeros((8, x.shape[1]), F32)

    x, gate, raw, bias, rate, skip, w = (
        pltpu.with_memory_space_constraint(a, pltpu.HBM) for a in (x, gate, raw, bias, rate, skip, w)
    )
    b_far, c_far, seg_far, gain_far = (pltpu.with_memory_space_constraint(a, pltpu.HBM) for a in (b, c, seg_row, gain))
    msg0, *scan0 = prep(0, head_size, x, b_far, raw, bias, rate, skip, seg_far)
    near0 = lax.ppermute(msg0, "seq", ring)
    msg1, *scan1 = prep(1, head_size, x, b_far, raw, bias, rate, skip, seg_far, (msg0, *scan0))
    near1 = lax.ppermute(msg1, "seq", ring)
    yg0, fg0 = inside(0, head_size, x, gate, b_far, c_far, *scan0, (msg0, msg1, *scan1))
    end0 = join(0, state, msg0, near0, (yg0, fg0, msg1, scan0[-1], *scan1))
    far0 = [lax.ppermute(end0, "seq", [(1, t)]) for t in (2, 3)]
    yg1, fg1 = inside(1, head_size, x, gate, b_far, c_far, *scan1, (end0, yg0, fg0, near0, msg1, scan0[-1]))
    end1 = join(1, state, msg1, near1, (yg0, fg0, near0, yg1, fg1, scan0[-1], scan1[-1], *far0))
    far1 = [lax.ppermute(end1, "seq", [(1, t)]) for t in (2, 3)]
    held = (near1, yg1, fg1, scan1[-1])
    w = load(w, gain_far, (end1, near0, yg0, fg0, scan0[-1], *far0, *held))
    g0, = gate_all(0, False, near0, far0, c, scan0[-1], yg0, fg0, gain, (*w, *far1, *held))
    x0, y0 = beside(g0, 1), beside(g0, 2)
    g1, = gate_all(1, False, near1, far1, c, scan1[-1], yg1, fg1, gain, (*w, g0))
    x1, y1 = beside(g1, 1), beside(g1, 2)

    def both(forwarded):
        return beside(forwarded[0], 2), beside(forwarded[1], 1)

    def turn(value, kinds, i):
        return lax.ppermute(value, ("seq", "head"), sends(kinds, i))

    xy, od = (1, 2), (0, 3)
    keep_n0, *send_n0, f0, l0 = project("next_0", 0, [(x0,), (y0,), (g0,)], w, (g1,), True, "blocks")
    got_n0 = [across(a) for a in send_n0]
    keep_o1, send_o1 = project("own_1", 1, [(g1,)], w, (keep_n0, f0, l0))
    held = (*w, keep_n0, keep_o1)
    first_n0, second_n0 = pair_sums(
        "sum_next_0", (keep_n0, 0, got_n0[:1], 0), (keep_n0, 1, got_n0[1:2], 0), (f0, l0, got_n0[2], send_o1, *held)
    )
    one_n0, two_n0 = turn(first_n0, xy, 0), turn(second_n0, xy, 1)
    got_o1 = across(send_o1)
    own0, own1 = (keep_n0, 2, got_n0[2:], 0), (keep_o1, 0, (got_o1,), 0)
    held = (*held, first_n0, got_n0[2])
    f0, l0 = release("release_0", (f0, l0), (x1, y1, second_n0, *held), HEAVY)
    d0 = both((f0, l0))
    held = (*held, second_n0)
    keep_n1, send_n1, f1, l1 = project("next_1", 1, [(x1,), (y1,)], w, (f0, *held), True)
    got_n1 = across(send_n1)
    held = (*held[:-1], keep_n1, f1, l1)
    join_n0, = add("add_next_0", second_n0, one_n0, (got_o1, *held))
    three_n0 = turn(join_n0, xy, 2)
    held = (*held[:-3], got_o1, join_n0)
    f1, l1 = release("release_1", (f1, l1), (*d0, keep_n1, *held))
    d1 = both((f1, l1))
    keep_n1, = release("gate_1", (keep_n1,), (f1, two_n0, *d0, *held), HEAVY)
    held = (*held, two_n0)
    first_n1, second_n1 = pair_sums("sum_next_1", (keep_n1, 0, (got_n1,), 0), (keep_n1, 1, (got_n1,), 1), (three_n0, *d0, *held))
    one_n1 = turn(first_n1, xy, 0)
    held = (*held, three_n0, first_n1, second_n1)
    keep_d0, *send_d0 = project("opposite_0", 0, [d0], w, held, False, "columns")
    got_d0 = [across(a) for a in send_d0]
    first_d0, second_d0 = pair_sums("sum_opposite_0", own0, (keep_d0, 0, got_d0, 0), held)
    one_d0, two_d0 = turn(first_d0, od, 0), turn(second_d0, od, 1)
    held = (keep_o1, got_o1, first_n0, join_n0, two_n0, three_n0, first_n1, second_n1, first_d0, second_d0)
    keep_d1, *send_d1 = project("opposite_1", 1, [d1], w, held, False, "columns", HEAVY)
    got_d1 = [across(a) for a in send_d1]
    first_d1, second_d1 = pair_sums("sum_opposite_1", own1, (keep_d1, 0, got_d1, 0), held)
    one_d1, two_d1 = turn(first_d1, od, 0), turn(second_d1, od, 1)
    held = (*held[2:], first_d1, second_d1)
    join_n1, = add("add_next_1", second_n1, one_n1, held)
    three_n1 = turn(join_n1, xy, 2)
    held = (*held, join_n1)
    join_d0, = add("add_opposite_0", second_d0, one_d0, held)
    three_d0 = turn(join_d0, od, 2)
    held = (*held, join_d0)
    join_d1, = add("add_opposite_1", second_d1, one_d1, (three_n1, *held))
    three_d1 = turn(join_d1, od, 2)
    second_n1, = release("release_2", (second_n1,), (join_d1, three_n1, first_n1, join_n1, first_d1))
    two_n1 = turn(second_n1, xy, 1)
    held = (first_n1, join_n1, three_n1, first_d1, join_d1)
    out = last(0, total, (first_n0, join_n0, two_n0, three_n0), (first_d0, join_d0, two_d0, three_d0), None, held)
    return last(1, total, (first_n1, join_n1, two_n1, three_n1), (first_d1, join_d1, two_d1, three_d1), out)


def plain(x, gate, b, c, raw, bias, rate, skip, gain, w, seg):
    raw = jnp.swapaxes(raw, 1, 2)
    head_size = x.shape[2] // raw.shape[1]
    state = b.shape[2]
    n_seq, n_head = lax.axis_size("seq"), lax.axis_size("head")
    total = x.shape[2] * n_head
    seg_row = seg.reshape(1, -1)
    s, h = lax.axis_index("seq"), lax.axis_index("head")
    gs, sums = [], []
    for m in range(2):
        msg, *scan = prep(m, head_size, x, b, raw, bias, rate, skip, seg_row)
        every = lax.all_gather(msg, "seq").astype(F32)
        entering, before = jnp.zeros_like(every[0]), every[0]
        for k in range(n_seq - 1):
            now = every[k]
            same = (now[state + 2] == before[state + 2]).astype(F32)
            decay = (now[state] + now[state + 1]) * same
            new = jnp.concatenate([now[:state] + decay * entering[:state], now[state:]])
            entering = jnp.where(k < s, new, entering)
            before = now
        yg, fg = inside(m, head_size, x, gate, b, c, *scan)
        near = entering.astype(BF16)
        g, ss = gate_all(m, True, near, [jnp.zeros_like(near)], c, scan[-1], yg, fg, gain)
        gs.append(g)
        sums.append(ss[0])
    g = lax.all_gather(jnp.stack(gs), "seq", axis=1, tiled=True)
    terms = jnp.einsum("mtk,mkd->mtd", g, w, preferred_element_type=F32)
    summed = lax.psum_scatter(terms.astype(BF16), "head", scatter_dimension=1, tiled=True)
    squares = lax.all_gather(lax.psum(jnp.stack(sums), "head"), "seq", axis=1, tiled=True)
    mine = lax.dynamic_slice_in_dim(squares, h * summed.shape[1], summed.shape[1], axis=1)
    return (summed.astype(F32) * lax.rsqrt(mine / total + EPS)[:, :, None]).astype(BF16)


def solution(mesh):
    placed = (
        P(None, "seq", "head"),
        P(None, "seq", "head"),
        P(None, "seq", None),
        P(None, "seq", None),
        P(None, "seq", "head"),
        P(None, "head"),
        P(None, "head"),
        P(None, "head"),
        P(None, "head"),
        P(None, "head", "seq"),
        P("seq"),
    )
    local = fast if mesh.shape["seq"] == 4 and mesh.shape["head"] == 8 else plain
    return jax.shard_map(
        local, mesh=mesh, in_specs=placed, out_specs=P(None, "head", "seq"), check_vma=False
    )
```

```python
import functools
import jax
import jax.numpy as jnp
from jax import lax
from jax.experimental import pallas as pl
from jax.experimental.pallas import tpu as pltpu
from jax.sharding import PartitionSpec as P

F32, BF16 = jnp.float32, jnp.bfloat16
LANES = 128
EXTRA = 16
NEG = -1e30
EPS = 1e-05
IN_VMEM = pl.BlockSpec(memory_space=pltpu.VMEM)
ANYWHERE = pl.BlockSpec(memory_space=pl.ANY)
SCOPE = 16 * 1024 * 1024
HEAVY = 10**11


def dot(a, b):
    return jnp.dot(a, b, preferred_element_type=F32)


def call(kernel, name, operands, outs, far=(), after=(), carry=(), scratch=(), weight=1, **kw):
    given, idle = len(operands) + len(far), len(after) + len(carry)

    def body(*refs):
        rest = refs[given + idle :]
        return kernel(*refs[:given], *rest[: len(outs)], *rest[len(outs) + len(carry) :])

    return pl.pallas_call(
        body,
        name=name,
        in_specs=[IN_VMEM] * len(operands)
        + [ANYWHERE] * len(far)
        + [IN_VMEM] * len(after)
        + [ANYWHERE] * len(carry),
        out_specs=[IN_VMEM] * len(outs) + [ANYWHERE] * len(carry),
        out_shape=[pltpu.VMEM(shape, dtype) for shape, dtype in outs]
        + [jax.ShapeDtypeStruct(a.shape, a.dtype) for a in carry],
        scratch_shapes=list(scratch),
        input_output_aliases={given + len(after) + i: len(outs) + i for i in range(len(carry))},
        compiler_params=pltpu.CompilerParams(vmem_limit_bytes=SCOPE),
        cost_estimate=pl.CostEstimate(flops=weight, bytes_accessed=1, transcendentals=0),
        **kw,
    )(*operands, *far, *after, *carry)


def start_all(sems, pairs):
    fetches = [pltpu.make_async_copy(source, target, sems.at[i]) for i, (source, target) in enumerate(pairs)]
    for fetch in fetches:
        fetch.start()
    return fetches


def tiles(width):
    tile = min(512, width)
    return [slice(i, i + tile) for i in range(0, width, tile)]


def lane_split(head_size, shape):
    return lax.broadcasted_iota(jnp.int32, shape, 1) // head_size


def spread(values, lane_head, first):
    shape = (values.shape[0], LANES)
    out = jnp.broadcast_to(values[:, first : first + 1], shape)
    for k in range(1, lane_head[1]):
        out = jnp.where(lane_head[0] == k, values[:, first + k : first + k + 1], out)
    return out


def lane_heads(head_size):
    return (lane_split(head_size, (1, LANES)), LANES // head_size)


def column(row):
    return jnp.broadcast_to(row, (LANES, row.shape[1])).T[:, :1]


def head_column(row):
    heads = row.shape[1]
    padded = jnp.concatenate([row, jnp.zeros((1, LANES - heads), F32)], axis=1)
    return jnp.broadcast_to(padded, (LANES, LANES)).T[:heads, :1]


def turned(values):
    heads, rows = values.shape
    return jnp.concatenate([values, jnp.zeros((LANES - heads, rows), F32)], axis=0).T[:, :heads]


def prep_kernel(model, head_size, x_all, b_all, raw_all, bias_all, rate_all, skip_all, seg_all, msg_ref, run_ref, q_ref, step_ref, row_ref, *scratch):
    x_ref, b_ref, raw_ref, bias_ref, rate_ref, skip_ref, seg_ref, sems = scratch
    rows, channels = x_ref.shape[1:]
    mine = pl.ds(model, 1)
    cuts = tiles(channels)
    fetches = start_all(
        sems,
        [(raw_all.at[mine], raw_ref), (bias_all, bias_ref), (rate_all, rate_ref), (skip_all, skip_ref)]
        + [(seg_all, seg_ref), (b_all.at[mine], b_ref)]
        + [(x_all.at[mine, :, cut], x_ref.at[:, :, cut]) for cut in cuts],
    )
    for fetch in fetches[:6]:
        fetch.wait()
    heads = raw_ref.shape[1]
    state = b_ref.shape[2]
    step_t = jax.nn.softplus(raw_ref[0] + head_column(bias_ref[model : model + 1, :]))
    log_decay = -head_column(rate_ref[model : model + 1, :]) * step_t
    earlier = lax.broadcasted_iota(jnp.int32, (rows, rows), 0)
    later = lax.broadcasted_iota(jnp.int32, (rows, rows), 1)
    tri = (later >= earlier).astype(F32)
    run_t = jnp.dot(log_decay, tri, precision=lax.Precision.HIGHEST, preferred_element_type=F32)
    run, step = turned(run_t), turned(step_t)
    run_ref[:, :rows] = run_t
    run_ref[:, rows:] = jnp.broadcast_to(head_column(skip_ref[model : model + 1, :]), (heads, LANES))
    step_ref[...] = step_t
    q_ref[...] = run_t - jnp.log(step_t)
    seg_row = seg_ref[...].astype(F32)
    row_ref[...] = seg_row
    seg_col = column(seg_row)
    last = seg_row[:, rows - 1 :]
    total = run[rows - 1 :, :]
    tail = jnp.exp(total - run) * step * (seg_col == last).astype(F32)
    etot = jnp.exp(total)
    b_t = b_ref[0].astype(F32).T.astype(BF16)
    lane_head = lane_heads(head_size)
    row_id = lax.broadcasted_iota(jnp.int32, (EXTRA, LANES), 0)
    for p in range(channels // LANES):
        cols = slice(p * LANES, (p + 1) * LANES)
        first = p * lane_head[1]
        for cut, fetch in zip(cuts, fetches[6:]):
            if cut.start == cols.start:
                fetch.wait()
        xw = (x_ref[0, :, cols].astype(F32) * spread(tail, lane_head, first)).astype(BF16)
        msg_ref[:state, cols] = dot(b_t, xw).astype(BF16)
        decay = spread(etot, lane_head, first)
        high = decay.astype(BF16).astype(F32)
        extra = jnp.where(row_id == 0, high, jnp.where(row_id == 1, decay - high, jnp.where(row_id == 2, last, 0.0)))
        msg_ref[state:, cols] = extra.astype(BF16)


def prep(model, head_size, x, b, raw, bias, rate, skip, seg_row, after=()):
    _, rows, channels = x.shape
    heads, state = raw.shape[1], b.shape[2]
    far = (x, b, raw, bias, rate, skip, seg_row)
    return call(
        functools.partial(prep_kernel, model, head_size),
        f"prep_{model}",
        (),
        [((state + EXTRA, channels), BF16), ((heads, rows + LANES), F32), ((heads, rows), F32), ((heads, rows), F32), ((1, rows), F32)],
        far,
        after,
        scratch=[pltpu.VMEM((1,) + a.shape[1:] if a.ndim == 3 else a.shape, a.dtype) for a in far]
        + [pltpu.SemaphoreType.DMA((6 + len(tiles(channels)),))],
    )


def inside_kernel(model, head_size, run_ref, q_ref, step_ref, seg_ref, x_all, gate_all_, b_all, c_all, yg_ref, fg_ref, *scratch):
    x_ref, gate_ref, b_ref, c_ref, sems = scratch
    rows, channels = x_ref.shape[1:]
    mine = pl.ds(model, 1)
    cuts = tiles(channels)
    fetches = start_all(
        sems,
        [(b_all.at[mine], b_ref), (c_all.at[mine], c_ref)]
        + [pair for cut in cuts for pair in ((x_all.at[mine, :, cut], x_ref.at[:, :, cut]), (gate_all_.at[mine, :, cut], gate_ref.at[:, :, cut]))],
    )
    for fetch in fetches[:2]:
        fetch.wait()
    half = rows // 2
    lane_head = lane_heads(head_size)
    run, step, q = turned(run_ref[:, :rows]), turned(step_ref[...]), q_ref[...]
    skip = turned(run_ref[:, rows:])[:1]
    seg_row = seg_ref[...].astype(F32)
    seg_col = column(seg_row)

    products = lax.dot_general(c_ref[0], b_ref[0], (((1,), (1,)), ((), ())), preferred_element_type=F32)
    tri = lax.broadcasted_iota(jnp.int32, (half, half), 0) >= lax.broadcasted_iota(jnp.int32, (half, half), 1)
    parts = [slice(0, half), slice(half, rows)]
    masks = [tri & (seg_col[part] == seg_row[:, part]) for part in parts]
    diagonal = [products[part, part] for part in parts]
    below = jnp.where(seg_col[parts[1]] == seg_row[:, parts[0]], products[parts[1], parts[0]], 0.0).astype(BF16)
    middle = run[half - 1 : half, :]
    entry = jnp.exp(run[parts[1]] - middle)
    leave = jnp.exp(middle - run[parts[0]]) * step[parts[0]]
    factor = jnp.exp(run)
    for p in range(channels // LANES):
        cols = slice(p * LANES, (p + 1) * LANES)
        first = p * lane_head[1]
        for i, cut in enumerate(cuts):
            if cut.start == cols.start:
                fetches[2 + 2 * i].wait()
                fetches[3 + 2 * i].wait()
        x = x_ref[0, :, cols]
        xf = x.astype(F32)
        ys = []
        for part, mask, prod in zip(parts, masks, diagonal):
            y = None
            for k in range(lane_head[1]):
                h = first + k
                mixing = jnp.exp(jnp.where(mask, run[part, h : h + 1] - q[h : h + 1, part], NEG))
                term = dot((mixing * prod).astype(BF16), x[part])
                y = term if y is None else jnp.where(lane_head[0] == k, term, y)
            ys.append(y)
        sent = (xf[parts[0]] * spread(leave, lane_head, first)).astype(BF16)
        ys[1] = ys[1] + dot(below, sent) * spread(entry, lane_head, first)
        y = jnp.concatenate(ys, axis=0) + spread(skip, lane_head, first) * xf
        v = gate_ref[0, :, cols].astype(F32)
        silu = v / (1.0 + jnp.exp(-v))
        yg_ref[:, cols] = (y * silu).astype(BF16)
        fg_ref[:, cols] = (spread(factor, lane_head, first) * silu).astype(BF16)


def inside(model, head_size, x, gate, b, c, run, q, step, seg_row, after=()):
    _, rows, channels = x.shape
    far = (x, gate, b, c)
    return call(
        functools.partial(inside_kernel, model, head_size),
        f"inside_{model}",
        (run, q, step, seg_row),
        [((rows, channels), BF16)] * 2,
        far,
        after,
        scratch=[pltpu.VMEM((1,) + a.shape[1:], a.dtype) for a in far]
        + [pltpu.SemaphoreType.DMA((2 + 2 * len(tiles(channels)),))],
    )


def load_kernel(w_all, gain_all, w_ref, inverse_ref, gain_ref, sems):
    fetches = start_all(sems, [(gain_all, gain_ref)] + [(w_all.at[i], w_ref.at[i]) for i in range(w_all.shape[0])])
    fetches[0].wait()
    inverse_ref[...] = 1.0 / gain_ref[...]
    for fetch in fetches[1:]:
        fetch.wait()


def load(w, gain, after):
    return call(
        load_kernel,
        "load",
        (),
        [(w.shape, BF16), (gain.shape, F32)],
        (w, gain),
        after,
        scratch=[pltpu.VMEM(gain.shape, F32), pltpu.SemaphoreType.DMA((1 + w.shape[0],))],
    )


def join_kernel(state, own_ref, got_ref, out_ref):
    own, got = own_ref[...].astype(F32), got_ref[...].astype(F32)
    same = (own[state + 2 : state + 3] == got[state + 2 : state + 3]).astype(F32)
    decay = (own[state : state + 1] + own[state + 1 : state + 2]) * same
    out_ref[:state, :] = (own[:state] + decay * got[:state]).astype(BF16)
    out_ref[state:, :] = own_ref[state:, :]


def join(model, state, own, got, after=()):
    return call(functools.partial(join_kernel, state), f"join_{model}", (own, got), [(own.shape, BF16)], (), after)[0]


def gate_kernel(model, state, alone, near_ref, *refs):
    further = 7 if alone else 6
    far_refs, refs = refs[:-further], refs[-further:]
    c_ref, seg_ref, yg_ref, fg_ref, gain_ref, g_ref, *ss_ref = refs
    rows, channels = yg_ref.shape
    paired = True if alone else lax.axis_index("seq") % 2 == 1
    seg_col = column(seg_ref[...])
    squares = jnp.zeros((8, rows), F32)
    for cols in tiles(channels):
        near = near_ref[:, cols].astype(F32)
        far = far_refs[0][:, cols].astype(F32)
        for ref in far_refs[1:]:
            far = far + ref[:, cols].astype(F32)
        last_near, last_far = near[state + 2 : state + 3], far[state + 2 : state + 3]
        decay = (near[state : state + 1] + near[state + 1 : state + 2]) * (last_near == last_far).astype(F32)
        entering = (near[:state] + jnp.where(paired, decay, 1.0) * far[:state]).astype(BF16)
        anchor = jnp.where(paired, last_near, last_far)[:, :1]
        reached = (seg_col == anchor).astype(F32)
        gated = yg_ref[:, cols].astype(F32) + reached * fg_ref[:, cols].astype(F32) * dot(c_ref[model], entering)
        g_ref[:, cols] = (gated * gain_ref[model : model + 1, cols]).astype(BF16)
        if alone:
            ones = jnp.ones((8, cols.stop - cols.start), BF16)
            squares += lax.dot_general(
                ones, (gated * gated).astype(BF16), (((1,), (1,)), ((), ())), preferred_element_type=F32
            )
    if alone:
        ss_ref[0][...] = squares


def gate_all(model, alone, near, far, c, seg_row, yg, fg, gain, after=()):
    return call(
        functools.partial(gate_kernel, model, c.shape[2], alone),
        f"gated_{model}",
        (near, *far, c, seg_row, yg, fg, gain),
        [(yg.shape, BF16)] + [((8, yg.shape[0]), F32)] * alone,
        (),
        after,
    )


def project_kernel(model, shapes, forward, sends, *refs):
    given, (w_ref, inverse_ref, keep_ref, *refs) = refs[: sum(shapes)], refs[sum(shapes) :]
    count = len(shapes)
    half, width = keep_ref.shape[1], w_ref.shape[2]
    send_refs, (*refs, lhs) = refs[: len(sends)], refs[len(sends) :]
    first = lax.axis_index("head") % 2 == 0
    if forward:
        refs[0][...] = given[0][:half, :]
        refs[1][...] = given[1][half:, :]
    row = 0
    for ref in given:
        lhs[row : row + ref.shape[0], :] = ref[...]
        row += ref.shape[0]
    squares = jnp.zeros((row, LANES), F32)
    for part in tiles(w_ref.shape[1]):
        gated = lhs[:, part].astype(F32) * inverse_ref[model : model + 1, part]
        squares += dot((gated * gated).astype(BF16), jnp.ones((part.stop - part.start, LANES), BF16))

    def put(result, ref, blocks, start, at, size):
        for k in range(count):
            early = result[2 * k * half : (2 * k + 1) * half].astype(BF16)
            late = result[(2 * k + 1) * half : (2 * k + 2) * half].astype(BF16)
            keep_ref[k, :, pl.ds(start + at, size)] = jnp.where(first, early, late)
            which, place = (ref, blocks.index(k)) if k in blocks else (None, 0)
            if which is None:
                which, place = [(r, part.index(k)) for r, (part, *_) in zip(send_refs, sends) if k in part][0]
            which[place, :, pl.ds(at, size)] = jnp.where(first, late, early)

    tile = min(512, width)
    done = set()
    for ref, (blocks, start, stop) in zip(send_refs, sends):
        if start in done:
            continue
        done.add(start)

        def step(j, _, ref=ref, blocks=blocks, start=start):
            at = pl.multiple_of(j * tile, tile)
            put(dot(lhs[...], w_ref[model, :, pl.ds(start + at, tile)]), ref, blocks, start, at, tile)
            return 0

        lax.fori_loop(0, (min(stop, width) - start) // tile, step, 0)
        if stop > width:
            put(squares, ref, blocks, start, width - start, LANES)


def project(name, model, blocks, weights, after=(), forward=False, split=None, weight=1):
    w, inverse = weights
    flat = [a for block in blocks for a in block]
    depth, width = w.shape[1:]
    n, full = len(blocks), width + LANES
    half = sum(a.shape[0] for a in flat) // (2 * n)
    if split == "blocks":
        sends = [([k], 0, full) for k in range(n)]
    elif split == "columns":
        sends = [(list(range(n)), 0, width // 2), (list(range(n)), width // 2, full)]
    else:
        sends = [(list(range(n)), 0, full)]
    return call(
        functools.partial(project_kernel, model, [len(block) for block in blocks], forward, sends),
        name,
        (*flat, w, inverse),
        [((n, half, full), BF16)]
        + [((len(part), half, stop - start), BF16) for part, start, stop in sends]
        + [((half, depth), BF16)] * (2 * forward),
        (),
        after,
        scratch=[pltpu.VMEM((2 * half * n, depth), BF16)],
        weight=weight,
    )


def release(name, arrays, after, weight=1):
    return call(lambda *refs: None, name, (), [], (), after, carry=arrays, weight=weight)


def pair_kernel(places, counts, *refs):
    keeps, gots = refs[:2], (refs[2 : 2 + counts[0]], refs[2 + counts[0] : 2 + sum(counts)])
    first_ref, second_ref = refs[-2:]
    turned_round = (lax.axis_index("seq") // 2 + lax.axis_index("head") // 2) % 2 == 0

    def ends(pieces):
        stops = [0]
        for ref in pieces:
            stops.append(stops[-1] + ref.shape[2])
        return stops

    bounds = sorted({*ends(gots[0]), *ends(gots[1])})
    for start, stop in zip(bounds, bounds[1:]):
        sums = []
        for keep, pieces, (at, got_at) in zip(keeps, gots, places):
            stops = ends(pieces)
            piece = max(i for i, lower in enumerate(stops) if lower <= start)
            got = pieces[piece][got_at, :, start - stops[piece] : stop - stops[piece]]
            sums.append(keep[at, :, start:stop].astype(F32) + got.astype(F32))
        first_ref[:, start:stop] = jnp.where(turned_round, sums[1], sums[0]).astype(BF16)
        second_ref[:, start:stop] = jnp.where(turned_round, sums[0], sums[1]).astype(BF16)


def pair_sums(name, one, other, after=()):
    return call(
        functools.partial(pair_kernel, ((one[1], one[3]), (other[1], other[3])), (len(one[2]), len(other[2]))),
        name,
        (one[0], other[0], *one[2], *other[2]),
        [(one[0].shape[1:], BF16)] * 2,
        (),
        after,
    )


def add_kernel(own_ref, got_ref, out_ref):
    out_ref[...] = (own_ref[...].astype(F32) + got_ref[...].astype(F32)).astype(BF16)


def add(name, own, got, after=()):
    return call(add_kernel, name, (own, got), [(own.shape, BF16)], (), after)


def last_kernel(total, model, *refs):
    beside, opposite, out_ref = refs[:4], refs[4:8], refs[8]
    width = out_ref.shape[2]
    s, z = lax.axis_index("seq"), lax.axis_index("head") // 2
    straight = (s == z) | (s + z == 3)
    inner = (z == 1) | (z == 2)

    def write(refs):
        value = jnp.where(inner, refs[0][...], refs[1][...]).astype(F32)
        for ref in refs[2:]:
            value = value + ref[...].astype(F32)
        scale = lax.rsqrt(value[:, width : width + 1] / total + EPS)
        out_ref[0] = (value[:, :width] * scale).astype(BF16)

    pl.when(straight)(lambda: write(opposite))
    pl.when(~straight)(lambda: write(beside))


def last(model, total, beside, opposite, before, after=()):
    half, width = beside[0].shape[0], beside[0].shape[1] - LANES
    operands = (*beside, *opposite)
    earlier = () if before is None else (before,)
    kernel = functools.partial(last_kernel, total, model)
    return pl.pallas_call(
        lambda *refs: kernel(*refs[: len(operands)], refs[-1]),
        name=f"last_{model}",
        grid=(1,),
        in_specs=[IN_VMEM] * (len(operands) + len(after))
        + [ANYWHERE] * len(earlier),
        out_specs=pl.BlockSpec((1, half, width), lambda i: (model, 0, 0)),
        out_shape=jax.ShapeDtypeStruct((2, half, width), BF16),
        input_output_aliases={len(operands) + len(after): 0} if earlier else {},
        compiler_params=pltpu.CompilerParams(vmem_limit_bytes=SCOPE),
        cost_estimate=pl.CostEstimate(flops=1 if earlier else HEAVY, bytes_accessed=1, transcendentals=0),
    )(*operands, *after, *earlier)


def xor_pairs(n, k):
    return [(i, i ^ k) for i in range(n)]


def fast(x, gate, b, c, raw, bias, rate, skip, gain, w, seg):
    raw = jnp.swapaxes(raw, 1, 2)
    head_size = x.shape[2] // raw.shape[1]
    state = b.shape[2]
    n_seq, n_head = lax.axis_size("seq"), lax.axis_size("head")
    total = x.shape[2] * n_head
    seg_row = seg.reshape(1, -1)
    def flat(si, zi, ci):
        return si * n_head + zi * 2 + ci

    def sends(kinds, turn):
        pairs = []
        for si in range(n_seq):
            if 0 in [si ^ k for k in kinds]:
                steps = ([(1, 0), (3, 2), (2, 3), (0, 1)], [], [(2, 0), (1, 3)])[turn]
            else:
                steps = ([(0, 1), (3, 2)], [(0, 1), (3, 2)], [(1, 2), (2, 1)])[turn]
            pairs += [(flat(si, a, ci), flat(si, o, ci)) for a, o in steps for ci in range(2)]
        return pairs

    ring = [(0, 1), (2, 3)]
    across = lambda a: lax.ppermute(a, "head", xor_pairs(n_head, 1))
    beside = lambda a, k: lax.ppermute(a, "seq", xor_pairs(n_seq, k))
    ss = jnp.zeros((8, x.shape[1]), F32)

    x, gate, raw, bias, rate, skip, w = (
        pltpu.with_memory_space_constraint(a, pltpu.HBM) for a in (x, gate, raw, bias, rate, skip, w)
    )
    b_far, c_far, seg_far, gain_far = (pltpu.with_memory_space_constraint(a, pltpu.HBM) for a in (b, c, seg_row, gain))
    msg0, *scan0 = prep(0, head_size, x, b_far, raw, bias, rate, skip, seg_far)
    near0 = lax.ppermute(msg0, "seq", ring)
    msg1, *scan1 = prep(1, head_size, x, b_far, raw, bias, rate, skip, seg_far, (msg0, *scan0))
    near1 = lax.ppermute(msg1, "seq", ring)
    yg0, fg0 = inside(0, head_size, x, gate, b_far, c_far, *scan0, (msg0, msg1, *scan1))
    end0 = join(0, state, msg0, near0, (yg0, fg0, msg1, scan0[-1], *scan1))
    far0 = [lax.ppermute(end0, "seq", [(1, t)]) for t in (2, 3)]
    yg1, fg1 = inside(1, head_size, x, gate, b_far, c_far, *scan1, (end0, yg0, fg0, near0, msg1, scan0[-1]))
    end1 = join(1, state, msg1, near1, (yg0, fg0, near0, yg1, fg1, scan0[-1], scan1[-1], *far0))
    far1 = [lax.ppermute(end1, "seq", [(1, t)]) for t in (2, 3)]
    held = (near1, yg1, fg1, scan1[-1])
    w = load(w, gain_far, (end1, near0, yg0, fg0, scan0[-1], *far0, *held))
    g0, = gate_all(0, False, near0, far0, c, scan0[-1], yg0, fg0, gain, (*w, *far1, *held))
    x0, y0 = beside(g0, 1), beside(g0, 2)
    g1, = gate_all(1, False, near1, far1, c, scan1[-1], yg1, fg1, gain, (*w, g0))
    x1, y1 = beside(g1, 1), beside(g1, 2)

    def both(forwarded):
        return beside(forwarded[0], 2), beside(forwarded[1], 1)

    def turn(value, kinds, i):
        return lax.ppermute(value, ("seq", "head"), sends(kinds, i))

    xy, od = (1, 2), (0, 3)
    keep_o0, send_o0 = project("own_0", 0, [(g0,)], w, (g1,))
    keep_o1, send_o1 = project("own_1", 1, [(g1,)], w, (keep_o0, send_o0))
    held = (*w, keep_o0, keep_o1, send_o1)
    keep_n0, *send_n0, f0, l0 = project("next_0", 0, [(x0,), (y0,)], w, (send_o0, *held), True, "blocks")
    got_n0 = [across(a) for a in send_n0]
    got_o0 = across(send_o0)
    first_n0, second_n0 = pair_sums(
        "sum_next_0", (keep_n0, 0, got_n0[:1], 0), (keep_n0, 1, got_n0[1:], 0), (f0, l0, got_o0, *held)
    )
    one_n0, two_n0 = turn(first_n0, xy, 0), turn(second_n0, xy, 1)
    got_o1 = across(send_o1)
    own0, own1 = (keep_o0, 0, (got_o0,), 0), (keep_o1, 0, (got_o1,), 0)
    held = (*w, keep_o0, keep_o1, first_n0, got_o0)
    f0, l0 = release("release_0", (f0, l0), (x1, y1, second_n0, *held), HEAVY)
    d0 = both((f0, l0))
    held = (*held, second_n0)
    keep_n1, send_n1, f1, l1 = project("next_1", 1, [(x1,), (y1,)], w, (f0, *held), True)
    got_n1 = across(send_n1)
    held = (*held[:-1], keep_n1, f1, l1)
    join_n0, = add("add_next_0", second_n0, one_n0, (got_o1, *held))
    three_n0 = turn(join_n0, xy, 2)
    held = (*held[:-3], got_o1, join_n0)
    f1, l1 = release("release_1", (f1, l1), (*d0, keep_n1, *held))
    d1 = both((f1, l1))
    keep_n1, = release("gate_1", (keep_n1,), (f1, two_n0, *d0, *held), HEAVY)
    held = (*held, two_n0)
    first_n1, second_n1 = pair_sums(
        "sum_next_1", (keep_n1, 0, (got_n1,), 0), (keep_n1, 1, (got_n1,), 1), (*d0, *held)
    )
    held = (*held, first_n1, second_n1)
    keep_d0, *send_d0 = project("opposite_0", 0, [d0], w, held, False, "columns")
    got_d0 = [across(a) for a in send_d0]
    first_d0, second_d0 = pair_sums("sum_opposite_0", own0, (keep_d0, 0, got_d0, 0), held)
    one_d0, two_d0 = turn(first_d0, od, 0), turn(second_d0, od, 1)
    first_n1, = release("release_n1", (first_n1,), (first_d0, second_d0, *held[:-2], second_n1))
    one_n1 = turn(first_n1, xy, 0)
    held = (keep_o1, got_o1, first_n0, join_n0, two_n0, three_n0, first_n1, second_n1, first_d0, second_d0)
    keep_d1, *send_d1 = project("opposite_1", 1, [d1], w, held, False, "columns", HEAVY)
    got_d1 = [across(a) for a in send_d1]
    first_d1, second_d1 = pair_sums("sum_opposite_1", own1, (keep_d1, 0, got_d1, 0), held)
    one_d1, two_d1 = turn(first_d1, od, 0), turn(second_d1, od, 1)
    held = (*held[2:], first_d1, second_d1)
    join_d0, = add("add_opposite_0", second_d0, one_d0, held)
    three_d0 = turn(join_d0, od, 2)
    held = (*held, join_d0)
    join_n1, = add("add_next_1", second_n1, one_n1, held)
    three_n1 = turn(join_n1, xy, 2)
    held = (*held, join_n1)
    join_d1, = add("add_opposite_1", second_d1, one_d1, (three_d0, *held))
    three_d1 = turn(join_d1, od, 2)
    second_n1, = release("release_2", (second_n1,), (join_d1, three_d0, first_n1, join_n1, first_d1))
    two_n1 = turn(second_n1, xy, 1)
    held = (first_n1, join_n1, three_n1, first_d1, join_d1)
    out = last(0, total, (first_n0, join_n0, two_n0, three_n0), (first_d0, join_d0, two_d0, three_d0), None, held)
    return last(1, total, (first_n1, join_n1, two_n1, three_n1), (first_d1, join_d1, two_d1, three_d1), out)


def plain(x, gate, b, c, raw, bias, rate, skip, gain, w, seg):
    raw = jnp.swapaxes(raw, 1, 2)
    head_size = x.shape[2] // raw.shape[1]
    state = b.shape[2]
    n_seq, n_head = lax.axis_size("seq"), lax.axis_size("head")
    total = x.shape[2] * n_head
    seg_row = seg.reshape(1, -1)
    s, h = lax.axis_index("seq"), lax.axis_index("head")
    gs, sums = [], []
    for m in range(2):
        msg, *scan = prep(m, head_size, x, b, raw, bias, rate, skip, seg_row)
        every = lax.all_gather(msg, "seq").astype(F32)
        entering, before = jnp.zeros_like(every[0]), every[0]
        for k in range(n_seq - 1):
            now = every[k]
            same = (now[state + 2] == before[state + 2]).astype(F32)
            decay = (now[state] + now[state + 1]) * same
            new = jnp.concatenate([now[:state] + decay * entering[:state], now[state:]])
            entering = jnp.where(k < s, new, entering)
            before = now
        yg, fg = inside(m, head_size, x, gate, b, c, *scan)
        near = entering.astype(BF16)
        g, ss = gate_all(m, True, near, [jnp.zeros_like(near)], c, scan[-1], yg, fg, gain)
        gs.append(g)
        sums.append(ss[0])
    g = lax.all_gather(jnp.stack(gs), "seq", axis=1, tiled=True)
    terms = jnp.einsum("mtk,mkd->mtd", g, w, preferred_element_type=F32)
    summed = lax.psum_scatter(terms.astype(BF16), "head", scatter_dimension=1, tiled=True)
    squares = lax.all_gather(lax.psum(jnp.stack(sums), "head"), "seq", axis=1, tiled=True)
    mine = lax.dynamic_slice_in_dim(squares, h * summed.shape[1], summed.shape[1], axis=1)
    return (summed.astype(F32) * lax.rsqrt(mine / total + EPS)[:, :, None]).astype(BF16)


def solution(mesh):
    placed = (
        P(None, "seq", "head"),
        P(None, "seq", "head"),
        P(None, "seq", None),
        P(None, "seq", None),
        P(None, "seq", "head"),
        P(None, "head"),
        P(None, "head"),
        P(None, "head"),
        P(None, "head"),
        P(None, "head", "seq"),
        P("seq"),
    )
    local = fast if mesh.shape["seq"] == 4 and mesh.shape["head"] == 8 else plain
    return jax.shard_map(
        local, mesh=mesh, in_specs=placed, out_specs=P(None, "head", "seq"), check_vma=False
    )
```

```python
import functools
import jax
import jax.numpy as jnp
from jax import lax
from jax.experimental import pallas as pl
from jax.experimental.pallas import tpu as pltpu
from jax.sharding import PartitionSpec as P

F32, BF16 = jnp.float32, jnp.bfloat16
LANES = 128
EXTRA = 16
NEG = -1e30
EPS = 1e-05
IN_VMEM = pl.BlockSpec(memory_space=pltpu.VMEM)
ANYWHERE = pl.BlockSpec(memory_space=pl.ANY)
SCOPE = 16 * 1024 * 1024
HEAVY = 10**11


def dot(a, b):
    return jnp.dot(a, b, preferred_element_type=F32)


def call(kernel, name, operands, outs, far=(), after=(), carry=(), scratch=(), weight=1, **kw):
    given, idle = len(operands) + len(far), len(after) + len(carry)

    def body(*refs):
        rest = refs[given + idle :]
        return kernel(*refs[:given], *rest[: len(outs)], *rest[len(outs) + len(carry) :])

    return pl.pallas_call(
        body,
        name=name,
        in_specs=[IN_VMEM] * len(operands)
        + [ANYWHERE] * len(far)
        + [IN_VMEM] * len(after)
        + [ANYWHERE] * len(carry),
        out_specs=[IN_VMEM] * len(outs) + [ANYWHERE] * len(carry),
        out_shape=[pltpu.VMEM(shape, dtype) for shape, dtype in outs]
        + [jax.ShapeDtypeStruct(a.shape, a.dtype) for a in carry],
        scratch_shapes=list(scratch),
        input_output_aliases={given + len(after) + i: len(outs) + i for i in range(len(carry))},
        compiler_params=pltpu.CompilerParams(vmem_limit_bytes=SCOPE),
        cost_estimate=pl.CostEstimate(flops=weight, bytes_accessed=1, transcendentals=0),
        **kw,
    )(*operands, *far, *after, *carry)


def start_all(sems, pairs):
    fetches = [pltpu.make_async_copy(source, target, sems.at[i]) for i, (source, target) in enumerate(pairs)]
    for fetch in fetches:
        fetch.start()
    return fetches


def tiles(width):
    tile = min(512, width)
    return [slice(i, i + tile) for i in range(0, width, tile)]


def lane_split(head_size, shape):
    return lax.broadcasted_iota(jnp.int32, shape, 1) // head_size


def spread(values, lane_head, first):
    shape = (values.shape[0], LANES)
    out = jnp.broadcast_to(values[:, first : first + 1], shape)
    for k in range(1, lane_head[1]):
        out = jnp.where(lane_head[0] == k, values[:, first + k : first + k + 1], out)
    return out


def lane_heads(head_size):
    return (lane_split(head_size, (1, LANES)), LANES // head_size)


def column(row):
    return jnp.broadcast_to(row, (LANES, row.shape[1])).T[:, :1]


def head_column(row):
    heads = row.shape[1]
    padded = jnp.concatenate([row, jnp.zeros((1, LANES - heads), F32)], axis=1)
    return jnp.broadcast_to(padded, (LANES, LANES)).T[:heads, :1]


def turned(values):
    heads, rows = values.shape
    return jnp.concatenate([values, jnp.zeros((LANES - heads, rows), F32)], axis=0).T[:, :heads]


def prep_kernel(model, head_size, x_all, b_all, raw_all, bias_all, rate_all, skip_all, seg_all, msg_ref, run_ref, q_ref, step_ref, row_ref, *scratch):
    x_ref, b_ref, raw_ref, bias_ref, rate_ref, skip_ref, seg_ref, sems = scratch
    rows, channels = x_ref.shape[1:]
    mine = pl.ds(model, 1)
    cuts = tiles(channels)
    fetches = start_all(
        sems,
        [(raw_all.at[mine], raw_ref), (bias_all, bias_ref), (rate_all, rate_ref), (skip_all, skip_ref)]
        + [(seg_all, seg_ref), (b_all.at[mine], b_ref)]
        + [(x_all.at[mine, :, cut], x_ref.at[:, :, cut]) for cut in cuts],
    )
    for fetch in fetches[:6]:
        fetch.wait()
    heads = raw_ref.shape[1]
    state = b_ref.shape[2]
    step_t = jax.nn.softplus(raw_ref[0] + head_column(bias_ref[model : model + 1, :]))
    log_decay = -head_column(rate_ref[model : model + 1, :]) * step_t
    earlier = lax.broadcasted_iota(jnp.int32, (rows, rows), 0)
    later = lax.broadcasted_iota(jnp.int32, (rows, rows), 1)
    tri = (later >= earlier).astype(F32)
    run_t = jnp.dot(log_decay, tri, precision=lax.Precision.HIGHEST, preferred_element_type=F32)
    run, step = turned(run_t), turned(step_t)
    run_ref[:, :rows] = run_t
    run_ref[:, rows:] = jnp.broadcast_to(head_column(skip_ref[model : model + 1, :]), (heads, LANES))
    step_ref[...] = step_t
    q_ref[...] = run_t - jnp.log(step_t)
    seg_row = seg_ref[...].astype(F32)
    row_ref[...] = seg_row
    seg_col = column(seg_row)
    last = seg_row[:, rows - 1 :]
    total = run[rows - 1 :, :]
    tail = jnp.exp(total - run) * step * (seg_col == last).astype(F32)
    etot = jnp.exp(total)
    b_t = b_ref[0].astype(F32).T.astype(BF16)
    lane_head = lane_heads(head_size)
    row_id = lax.broadcasted_iota(jnp.int32, (EXTRA, LANES), 0)
    for p in range(channels // LANES):
        cols = slice(p * LANES, (p + 1) * LANES)
        first = p * lane_head[1]
        for cut, fetch in zip(cuts, fetches[6:]):
            if cut.start == cols.start:
                fetch.wait()
        xw = (x_ref[0, :, cols].astype(F32) * spread(tail, lane_head, first)).astype(BF16)
        msg_ref[:state, cols] = dot(b_t, xw).astype(BF16)
        decay = spread(etot, lane_head, first)
        high = decay.astype(BF16).astype(F32)
        extra = jnp.where(row_id == 0, high, jnp.where(row_id == 1, decay - high, jnp.where(row_id == 2, last, 0.0)))
        msg_ref[state:, cols] = extra.astype(BF16)


def prep(model, head_size, x, b, raw, bias, rate, skip, seg_row, after=()):
    _, rows, channels = x.shape
    heads, state = raw.shape[1], b.shape[2]
    far = (x, b, raw, bias, rate, skip, seg_row)
    return call(
        functools.partial(prep_kernel, model, head_size),
        f"prep_{model}",
        (),
        [((state + EXTRA, channels), BF16), ((heads, rows + LANES), F32), ((heads, rows), F32), ((heads, rows), F32), ((1, rows), F32)],
        far,
        after,
        scratch=[pltpu.VMEM((1,) + a.shape[1:] if a.ndim == 3 else a.shape, a.dtype) for a in far]
        + [pltpu.SemaphoreType.DMA((6 + len(tiles(channels)),))],
    )


def inside_kernel(model, head_size, run_ref, q_ref, step_ref, seg_ref, x_all, gate_all_, b_all, c_all, yg_ref, fg_ref, *scratch):
    x_ref, gate_ref, b_ref, c_ref, sems = scratch
    rows, channels = x_ref.shape[1:]
    mine = pl.ds(model, 1)
    cuts = tiles(channels)
    fetches = start_all(
        sems,
        [(b_all.at[mine], b_ref), (c_all.at[mine], c_ref)]
        + [pair for cut in cuts for pair in ((x_all.at[mine, :, cut], x_ref.at[:, :, cut]), (gate_all_.at[mine, :, cut], gate_ref.at[:, :, cut]))],
    )
    for fetch in fetches[:2]:
        fetch.wait()
    half = rows // 2
    lane_head = lane_heads(head_size)
    run, step, q = turned(run_ref[:, :rows]), turned(step_ref[...]), q_ref[...]
    skip = turned(run_ref[:, rows:])[:1]
    seg_row = seg_ref[...].astype(F32)
    seg_col = column(seg_row)

    products = lax.dot_general(c_ref[0], b_ref[0], (((1,), (1,)), ((), ())), preferred_element_type=F32)
    tri = lax.broadcasted_iota(jnp.int32, (half, half), 0) >= lax.broadcasted_iota(jnp.int32, (half, half), 1)
    parts = [slice(0, half), slice(half, rows)]
    masks = [tri & (seg_col[part] == seg_row[:, part]) for part in parts]
    diagonal = [products[part, part] for part in parts]
    below = jnp.where(seg_col[parts[1]] == seg_row[:, parts[0]], products[parts[1], parts[0]], 0.0).astype(BF16)
    middle = run[half - 1 : half, :]
    entry = jnp.exp(run[parts[1]] - middle)
    leave = jnp.exp(middle - run[parts[0]]) * step[parts[0]]
    factor = jnp.exp(run)
    for p in range(channels // LANES):
        cols = slice(p * LANES, (p + 1) * LANES)
        first = p * lane_head[1]
        for i, cut in enumerate(cuts):
            if cut.start == cols.start:
                fetches[2 + 2 * i].wait()
                fetches[3 + 2 * i].wait()
        x = x_ref[0, :, cols]
        xf = x.astype(F32)
        ys = []
        for part, mask, prod in zip(parts, masks, diagonal):
            y = None
            for k in range(lane_head[1]):
                h = first + k
                mixing = jnp.exp(jnp.where(mask, run[part, h : h + 1] - q[h : h + 1, part], NEG))
                term = dot((mixing * prod).astype(BF16), x[part])
                y = term if y is None else jnp.where(lane_head[0] == k, term, y)
            ys.append(y)
        sent = (xf[parts[0]] * spread(leave, lane_head, first)).astype(BF16)
        ys[1] = ys[1] + dot(below, sent) * spread(entry, lane_head, first)
        y = jnp.concatenate(ys, axis=0) + spread(skip, lane_head, first) * xf
        v = gate_ref[0, :, cols].astype(F32)
        silu = v / (1.0 + jnp.exp(-v))
        yg_ref[:, cols] = (y * silu).astype(BF16)
        fg_ref[:, cols] = (spread(factor, lane_head, first) * silu).astype(BF16)


def inside(model, head_size, x, gate, b, c, run, q, step, seg_row, after=()):
    _, rows, channels = x.shape
    far = (x, gate, b, c)
    return call(
        functools.partial(inside_kernel, model, head_size),
        f"inside_{model}",
        (run, q, step, seg_row),
        [((rows, channels), BF16)] * 2,
        far,
        after,
        scratch=[pltpu.VMEM((1,) + a.shape[1:], a.dtype) for a in far]
        + [pltpu.SemaphoreType.DMA((2 + 2 * len(tiles(channels)),))],
    )


def load_kernel(w_all, w_ref, sems):
    for fetch in start_all(sems, [(w_all.at[i], w_ref.at[i]) for i in range(w_all.shape[0])]):
        fetch.wait()


def load(w, after):
    return call(load_kernel, "load", (), [(w.shape, BF16)], (w,), after, scratch=[pltpu.SemaphoreType.DMA((w.shape[0],))])


def join_kernel(state, own_ref, got_ref, out_ref):
    own, got = own_ref[...].astype(F32), got_ref[...].astype(F32)
    same = (own[state + 2 : state + 3] == got[state + 2 : state + 3]).astype(F32)
    decay = (own[state : state + 1] + own[state + 1 : state + 2]) * same
    out_ref[:state, :] = (own[:state] + decay * got[:state]).astype(BF16)
    out_ref[state:, :] = own_ref[state:, :]


def join(model, state, own, got, after=()):
    return call(functools.partial(join_kernel, state), f"join_{model}", (own, got), [(own.shape, BF16)], (), after)[0]


def gate_kernel(model, state, alone, near_ref, *refs):
    far_refs, refs = refs[:-7], refs[-7:]
    c_ref, seg_ref, yg_ref, fg_ref, gain_ref, g_ref, ss_ref = refs
    rows, channels = yg_ref.shape
    paired = True if alone else lax.axis_index("seq") % 2 == 1
    seg_col = column(seg_ref[...])
    squares = jnp.zeros((8, rows), F32)
    for cols in tiles(channels):
        near = near_ref[:, cols].astype(F32)
        far = far_refs[0][:, cols].astype(F32)
        for ref in far_refs[1:]:
            far = far + ref[:, cols].astype(F32)
        last_near, last_far = near[state + 2 : state + 3], far[state + 2 : state + 3]
        decay = (near[state : state + 1] + near[state + 1 : state + 2]) * (last_near == last_far).astype(F32)
        entering = (near[:state] + jnp.where(paired, decay, 1.0) * far[:state]).astype(BF16)
        anchor = jnp.where(paired, last_near, last_far)[:, :1]
        reached = (seg_col == anchor).astype(F32)
        gated = yg_ref[:, cols].astype(F32) + reached * fg_ref[:, cols].astype(F32) * dot(c_ref[model], entering)
        g_ref[:, cols] = (gated * gain_ref[model : model + 1, cols]).astype(BF16)
        ones = jnp.ones((8, cols.stop - cols.start), BF16)
        squares += lax.dot_general(
            ones, (gated * gated).astype(BF16), (((1,), (1,)), ((), ())), preferred_element_type=F32
        )
    ss_ref[...] = squares


def gate_all(model, alone, near, far, c, seg_row, yg, fg, gain, after=()):
    return call(
        functools.partial(gate_kernel, model, c.shape[2], alone),
        f"gated_{model}",
        (near, *far, c, seg_row, yg, fg, gain),
        [(yg.shape, BF16), ((8, yg.shape[0]), F32)],
        (),
        after,
    )


def project_kernel(model, shapes, forward, sends, *refs):
    given, (w_ref, keep_ref, *refs) = refs[: sum(shapes)], refs[sum(shapes) :]
    count = len(shapes)
    half, width = keep_ref.shape[1], w_ref.shape[2]
    send_refs, (*refs, lhs) = refs[: len(sends)], refs[len(sends) :]
    first = lax.axis_index("head") % 2 == 0
    if forward:
        refs[0][...] = given[0][:half, :]
        refs[1][...] = given[1][half:, :]
    row = 0
    for ref in given:
        lhs[row : row + ref.shape[0], :] = ref[...]
        row += ref.shape[0]
    def put(result, ref, blocks, start, at, size):
        for k in range(count):
            early = result[2 * k * half : (2 * k + 1) * half].astype(BF16)
            late = result[(2 * k + 1) * half : (2 * k + 2) * half].astype(BF16)
            keep_ref[k, :, pl.ds(start + at, size)] = jnp.where(first, early, late)
            which, place = (ref, blocks.index(k)) if k in blocks else (None, 0)
            if which is None:
                which, place = [(r, part.index(k)) for r, (part, *_) in zip(send_refs, sends) if k in part][0]
            which[place, :, pl.ds(at, size)] = jnp.where(first, late, early)

    tile = min(512, width)
    done = set()
    for ref, (blocks, start, stop) in zip(send_refs, sends):
        if start in done:
            continue
        done.add(start)

        def step(j, _, ref=ref, blocks=blocks, start=start):
            at = pl.multiple_of(j * tile, tile)
            put(dot(lhs[...], w_ref[model, :, pl.ds(start + at, tile)]), ref, blocks, start, at, tile)
            return 0

        lax.fori_loop(0, (stop - start) // tile, step, 0)


def project(name, model, blocks, weights, after=(), forward=False, split=None, weight=1):
    w, = weights
    flat = [a for block in blocks for a in block]
    depth, width = w.shape[1:]
    n, full = len(blocks), width
    half = sum(a.shape[0] for a in flat) // (2 * n)
    if split == "blocks":
        sends = [([k], 0, full) for k in range(n)]
    elif split == "columns":
        sends = [(list(range(n)), 0, width // 2), (list(range(n)), width // 2, full)]
    else:
        sends = [(list(range(n)), 0, full)]
    return call(
        functools.partial(project_kernel, model, [len(block) for block in blocks], forward, sends),
        name,
        (*flat, w),
        [((n, half, full), BF16)]
        + [((len(part), half, stop - start), BF16) for part, start, stop in sends]
        + [((half, depth), BF16)] * (2 * forward),
        (),
        after,
        scratch=[pltpu.VMEM((2 * half * n, depth), BF16)],
        weight=weight,
    )


def release(name, arrays, after, weight=1):
    return call(lambda *refs: None, name, (), [], (), after, carry=arrays, weight=weight)


def inner_column():
    s = lax.axis_index("seq")
    return (s == 1) | (s == 2)


def pair_kernel(places, counts, own_sent, *refs):
    keeps, gots = refs[:2], (refs[2 : 2 + counts[0]], refs[2 + counts[0] : 2 + sum(counts)])
    first_ref, second_ref = refs[-2:]
    turned_round = (lax.axis_index("seq") // 2 + lax.axis_index("head") // 2) % 2 == 0
    if own_sent:
        turned_round = turned_round | inner_column()

    def ends(pieces):
        stops = [0]
        for ref in pieces:
            stops.append(stops[-1] + ref.shape[2])
        return stops

    bounds = sorted({*ends(gots[0]), *ends(gots[1])})
    for start, stop in zip(bounds, bounds[1:]):
        sums = []
        for keep, pieces, (at, got_at) in zip(keeps, gots, places):
            stops = ends(pieces)
            piece = max(i for i, lower in enumerate(stops) if lower <= start)
            got = pieces[piece][got_at, :, start - stops[piece] : stop - stops[piece]]
            sums.append(keep[at, :, start:stop].astype(F32) + got.astype(F32))
        first_ref[:, start:stop] = jnp.where(turned_round, sums[1], sums[0]).astype(BF16)
        second_ref[:, start:stop] = jnp.where(turned_round, sums[0], sums[1]).astype(BF16)


def pair_sums(name, one, other, after=(), own_sent=False):
    return call(
        functools.partial(pair_kernel, ((one[1], one[3]), (other[1], other[3])), (len(one[2]), len(other[2])), own_sent),
        name,
        (one[0], other[0], *one[2], *other[2]),
        [(one[0].shape[1:], BF16)] * 2,
        (),
        after,
    )


def add_kernel(own_ref, got_ref, out_ref):
    out_ref[...] = (own_ref[...].astype(F32) + got_ref[...].astype(F32)).astype(BF16)


def add(name, own, got, after=()):
    return call(add_kernel, name, (own, got), [(own.shape, BF16)], (), after)


def join_own_kernel(first_ref, second_ref, one_ref, two_ref, out_ref):
    mine = inner_column() & (lax.axis_index("seq") == lax.axis_index("head") // 2)
    other = inner_column() & ~mine
    base = jnp.where(mine, first_ref[...], second_ref[...])
    got = jnp.where(other, two_ref[...], one_ref[...])
    out_ref[...] = (base.astype(F32) + got.astype(F32)).astype(BF16)


def pick_kernel(beside_ref, *refs):
    *terms, out_ref = refs
    value = sum((ref[...] if len(ref.shape) == 2 else ref[0]).astype(F32) for ref in terms)
    out_ref[...] = jnp.where(inner_column(), value.astype(BF16), beside_ref[...])


def pick(name, beside, terms, after=()):
    return call(pick_kernel, name, (beside, *terms), [(beside.shape, BF16)], (), after)[0]


def first_sums_kernel(one_ref, other_ref, out_ref):
    rows = lax.broadcasted_iota(jnp.int32, out_ref.shape, 0)
    out_ref[...] = jnp.where(rows < 4, one_ref[...], other_ref[...])


def sums_kernel(one_ref, other_ref, out_ref):
    out_ref[...] = one_ref[...] + other_ref[...]


def last_kernel(total, model, own_sent, *refs):
    first_n, join_n, three_n, first_d, second_d, one_d, join_d, three_d, two, ss_ref, out_ref = refs
    half = out_ref.shape[1]
    s, z = lax.axis_index("seq"), lax.axis_index("head") // 2
    row = ss_ref[4 * model : 4 * model + 1, :]
    row = jnp.where(lax.axis_index("head") % 2 == 0, row[:, :half], row[:, half:])
    scale = column(lax.rsqrt(row / total + EPS))
    straight = (s == z) | (s + z == 3)
    inner = inner_column()

    def write(condition, *terms):
        @pl.when(condition)
        def _():
            value = terms[0][...].astype(F32)
            for ref in terms[1:]:
                value = value + ref[...].astype(F32)
            out_ref[0] = (value * scale).astype(BF16)

    write(~straight & ~inner, first_n, two, three_n)
    write(~straight & inner, join_n, three_n)
    write(straight & ~inner, join_d, three_d)
    if own_sent:
        write(straight & inner & (s == z), second_d, two, three_d)
        write(straight & inner & (s != z), first_d, one_d, three_d)
    else:
        write(straight & inner, first_d, two, three_d)


def last(model, total, own_sent, operands, before, after=()):
    half, width = operands[0].shape
    earlier = () if before is None else (before,)
    kernel = functools.partial(last_kernel, total, model, own_sent)
    return pl.pallas_call(
        lambda *refs: kernel(*refs[: len(operands)], refs[-1]),
        name=f"last_{model}",
        grid=(1,),
        in_specs=[IN_VMEM] * (len(operands) + len(after))
        + [ANYWHERE] * len(earlier),
        out_specs=pl.BlockSpec((1, half, width), lambda i: (model, 0, 0)),
        out_shape=jax.ShapeDtypeStruct((2, half, width), BF16),
        input_output_aliases={len(operands) + len(after): 0} if earlier else {},
        compiler_params=pltpu.CompilerParams(vmem_limit_bytes=SCOPE),
        cost_estimate=pl.CostEstimate(flops=1 if earlier else HEAVY, bytes_accessed=1, transcendentals=0),
    )(*operands, *after, *earlier)


def xor_pairs(n, k):
    return [(i, i ^ k) for i in range(n)]


def fast(x, gate, b, c, raw, bias, rate, skip, gain, w, seg):
    raw = jnp.swapaxes(raw, 1, 2)
    head_size = x.shape[2] // raw.shape[1]
    state = b.shape[2]
    n_seq, n_head = lax.axis_size("seq"), lax.axis_size("head")
    total = x.shape[2] * n_head
    seg_row = seg.reshape(1, -1)
    def flat(si, zi, ci):
        return si * n_head + zi * 2 + ci

    def sends(kinds, turn):
        pairs = []
        for si in range(n_seq):
            if turn == 1:
                steps = [(0, 1), (3, 2)]
            elif 0 in [si ^ k for k in kinds]:
                steps = [(1, 0), (3, 2), (2, 3), (0, 1)] if turn == 0 else [(2, 0), (1, 3)]
            else:
                steps = [(0, 1), (3, 2)] if turn == 0 else [(1, 2), (2, 1)]
            pairs += [(flat(si, a, ci), flat(si, o, ci)) for a, o in steps for ci in range(2)]
        return pairs

    ring = [(0, 1), (2, 3)]
    across = lambda a: lax.ppermute(a, "head", xor_pairs(n_head, 1))
    beside = lambda a, k: lax.ppermute(a, "seq", xor_pairs(n_seq, k))
    ss = jnp.zeros((8, x.shape[1]), F32)

    x, gate, raw, bias, rate, skip, w = (
        pltpu.with_memory_space_constraint(a, pltpu.HBM) for a in (x, gate, raw, bias, rate, skip, w)
    )
    b_far, c_far, seg_far = (pltpu.with_memory_space_constraint(a, pltpu.HBM) for a in (b, c, seg_row))
    msg0, *scan0 = prep(0, head_size, x, b_far, raw, bias, rate, skip, seg_far)
    near0 = lax.ppermute(msg0, "seq", ring)
    msg1, *scan1 = prep(1, head_size, x, b_far, raw, bias, rate, skip, seg_far, (msg0, *scan0))
    near1 = lax.ppermute(msg1, "seq", ring)
    yg0, fg0 = inside(0, head_size, x, gate, b_far, c_far, *scan0, (msg0, msg1, *scan1))
    end0 = join(0, state, msg0, near0, (yg0, fg0, msg1, scan0[-1], *scan1))
    far0 = [lax.ppermute(end0, "seq", [(1, t)]) for t in (2, 3)]
    yg1, fg1 = inside(1, head_size, x, gate, b_far, c_far, *scan1, (end0, yg0, fg0, near0, msg1, scan0[-1]))
    end1 = join(1, state, msg1, near1, (yg0, fg0, near0, yg1, fg1, scan0[-1], scan1[-1], *far0))
    far1 = [lax.ppermute(end1, "seq", [(1, t)]) for t in (2, 3)]
    held = (near1, yg1, fg1, scan1[-1])
    w = load(w, (end1, near0, yg0, fg0, scan0[-1], *far0, *held))
    g0, ss0 = gate_all(0, False, near0, far0, c, scan0[-1], yg0, fg0, gain, (*w, *far1, *held))
    x0, y0 = beside(g0, 1), beside(g0, 2)
    g1, ss1 = gate_all(1, False, near1, far1, c, scan1[-1], yg1, fg1, gain, (*w, g0, ss0))
    x1, y1 = beside(g1, 1), beside(g1, 2)

    def both(forwarded):
        return beside(forwarded[0], 2), beside(forwarded[1], 1)

    def turn(value, kinds, i):
        return lax.ppermute(value, ("seq", "head"), sends(kinds, i))

    xy, od = (1, 2), (0, 3)
    def add_sums(k, ss, after):
        return call(sums_kernel, f"sums_{k}", (ss, lax.ppermute(ss, "head", xor_pairs(n_head, k))), [(ss.shape, F32)], (), after)[0]

    ss, = call(first_sums_kernel, "sums_0", (ss0, ss1), [(ss0.shape, F32)], (), (*w, g0, g1))
    keep_o0, send_o0 = project("own_0", 0, [(g0,)], w, (g1, ss))
    ss = add_sums(1, ss, (*w, g1, keep_o0, send_o0))
    keep_o1, send_o1 = project("own_1", 1, [(g1,)], w, (ss, keep_o0, send_o0))
    held = (*w, keep_o0, keep_o1, send_o1)
    ss = add_sums(2, ss, (send_o0, *held))
    ss = add_sums(4, ss, (send_o0, *held))
    keep_n0, *send_n0, f0, l0 = project("next_0", 0, [(x0,), (y0,)], w, (ss, send_o0, *held), True, "blocks")
    got_n0 = [across(a) for a in send_n0]
    got_o0 = across(send_o0)
    first_n0, second_n0 = pair_sums(
        "sum_next_0", (keep_n0, 0, got_n0[:1], 0), (keep_n0, 1, got_n0[1:], 0), (f0, l0, got_o0, *held)
    )
    one_n0 = turn(first_n0, xy, 0)
    third_0 = pick("pick_0", second_n0, (keep_o0, got_o0), (first_n0, f0, l0, *held))
    two_n0 = turn(third_0, xy, 1)
    got_o1 = across(send_o1)
    own0, own1 = (keep_o0, 0, (got_o0,), 0), (keep_o1, 0, (got_o1,), 0)
    held = (*w, keep_o0, keep_o1, first_n0, got_o0)
    f0, l0 = release("release_0", (f0, l0), (x1, y1, second_n0, third_0, *held), HEAVY)
    d0 = both((f0, l0))
    held = (*held, second_n0)
    keep_n1, send_n1, f1, l1 = project("next_1", 1, [(x1,), (y1,)], w, (f0, *held), True)
    got_n1 = across(send_n1)
    held = (*held[:-1], keep_n1, f1, l1)
    join_n0, = add("add_next_0", second_n0, one_n0, (got_o1, *held))
    three_n0 = turn(join_n0, xy, 2)
    held = (*held[:-3], got_o1, join_n0)
    f1, l1 = release("release_1", (f1, l1), (*d0, keep_n1, *held))
    d1 = both((f1, l1))
    keep_n1, = release("gate_1", (keep_n1,), (f1, two_n0, *d0, *held), HEAVY)
    held = (*held, two_n0)
    first_n1, second_n1 = pair_sums(
        "sum_next_1", (keep_n1, 0, (got_n1,), 0), (keep_n1, 1, (got_n1,), 1), (*d0, *held)
    )
    held = (*held, first_n1, second_n1)
    keep_d0, *send_d0 = project("opposite_0", 0, [d0], w, held, False, "columns")
    got_d0 = [across(a) for a in send_d0]
    first_d0, second_d0 = pair_sums("sum_opposite_0", own0, (keep_d0, 0, got_d0, 0), held, True)
    one_d0 = turn(first_d0, od, 0)
    first_n1, = release("release_n1", (first_n1,), (first_d0, second_d0, *held[:-2], second_n1))
    one_n1 = turn(first_n1, xy, 0)
    held = (keep_o1, got_o1, first_n0, join_n0, two_n0, three_n0, first_n1, second_n1, first_d0, second_d0)
    keep_d1, *send_d1 = project("opposite_1", 1, [d1], w, held, False, "columns", HEAVY)
    got_d1 = [across(a) for a in send_d1]
    first_d1, second_d1 = pair_sums("sum_opposite_1", own1, (keep_d1, 0, got_d1, 0), held)
    one_d1 = turn(first_d1, od, 0)
    held = (*held[2:], first_d1, second_d1)
    join_d0, = call(
        join_own_kernel, "add_opposite_0", (first_d0, second_d0, one_d0, two_n0), [(first_d0.shape, BF16)], (), held
    )
    three_d0 = turn(join_d0, od, 2)
    held = (*held, one_d0, join_d0)
    third_1 = pick("pick_1", second_n1, (second_d1,), held)
    two_1 = turn(third_1, xy, 1)
    join_n1, = add("add_next_1", second_n1, one_n1, (third_1, *held))
    three_n1 = turn(join_n1, xy, 2)
    held = (*held, join_n1)
    join_d1, = add("add_opposite_1", second_d1, one_d1, (three_d0, *held))
    three_d1 = turn(join_d1, od, 2)
    ss, = release("release_sums", (ss,), (first_d1, second_d1))
    ss = lax.ppermute(
        ss, ("seq", "head"),
        [(flat(zi, si, ci), flat(si, zi, ci)) for si in range(n_seq) for zi in range(n_seq) for ci in range(2)],
    )
    held = (first_n1, join_n1, three_n1, first_d1, second_d1, one_d1, join_d1, two_1)
    out = last(
        0, total, True, (first_n0, join_n0, three_n0, first_d0, second_d0, one_d0, join_d0, three_d0, two_n0, ss), None, held
    )
    return last(
        1, total, False, (first_n1, join_n1, three_n1, first_d1, second_d1, one_d1, join_d1, three_d1, two_1, ss), out
    )


def plain(x, gate, b, c, raw, bias, rate, skip, gain, w, seg):
    raw = jnp.swapaxes(raw, 1, 2)
    head_size = x.shape[2] // raw.shape[1]
    state = b.shape[2]
    n_seq, n_head = lax.axis_size("seq"), lax.axis_size("head")
    total = x.shape[2] * n_head
    seg_row = seg.reshape(1, -1)
    s, h = lax.axis_index("seq"), lax.axis_index("head")
    gs, sums = [], []
    for m in range(2):
        msg, *scan = prep(m, head_size, x, b, raw, bias, rate, skip, seg_row)
        every = lax.all_gather(msg, "seq").astype(F32)
        entering, before = jnp.zeros_like(every[0]), every[0]
        for k in range(n_seq - 1):
            now = every[k]
            same = (now[state + 2] == before[state + 2]).astype(F32)
            decay = (now[state] + now[state + 1]) * same
            new = jnp.concatenate([now[:state] + decay * entering[:state], now[state:]])
            entering = jnp.where(k < s, new, entering)
            before = now
        yg, fg = inside(m, head_size, x, gate, b, c, *scan)
        near = entering.astype(BF16)
        g, ss = gate_all(m, True, near, [jnp.zeros_like(near)], c, scan[-1], yg, fg, gain)
        gs.append(g)
        sums.append(ss[0])
    g = lax.all_gather(jnp.stack(gs), "seq", axis=1, tiled=True)
    terms = jnp.einsum("mtk,mkd->mtd", g, w, preferred_element_type=F32)
    summed = lax.psum_scatter(terms.astype(BF16), "head", scatter_dimension=1, tiled=True)
    squares = lax.all_gather(lax.psum(jnp.stack(sums), "head"), "seq", axis=1, tiled=True)
    mine = lax.dynamic_slice_in_dim(squares, h * summed.shape[1], summed.shape[1], axis=1)
    return (summed.astype(F32) * lax.rsqrt(mine / total + EPS)[:, :, None]).astype(BF16)


def solution(mesh):
    placed = (
        P(None, "seq", "head"),
        P(None, "seq", "head"),
        P(None, "seq", None),
        P(None, "seq", None),
        P(None, "seq", "head"),
        P(None, "head"),
        P(None, "head"),
        P(None, "head"),
        P(None, "head"),
        P(None, "head", "seq"),
        P("seq"),
    )
    local = fast if mesh.shape["seq"] == 4 and mesh.shape["head"] == 8 else plain
    return jax.shard_map(
        local, mesh=mesh, in_specs=placed, out_specs=P(None, "head", "seq"), check_vma=False
    )
```

```python
import functools
import jax
import jax.numpy as jnp
from jax import lax
from jax.experimental import pallas as pl
from jax.experimental.pallas import tpu as pltpu
from jax.sharding import PartitionSpec as P

F32, BF16 = jnp.float32, jnp.bfloat16
LANES = 128
EXTRA = 16
NEG = -1e30
EPS = 1e-05
IN_VMEM = pl.BlockSpec(memory_space=pltpu.VMEM)
ANYWHERE = pl.BlockSpec(memory_space=pl.ANY)
SCOPE = 16 * 1024 * 1024
HEAVY = 10**11


def dot(a, b):
    return jnp.dot(a, b, preferred_element_type=F32)


def call(kernel, name, operands, outs, far=(), after=(), carry=(), scratch=(), weight=1, **kw):
    given, idle = len(operands) + len(far), len(after) + len(carry)

    def body(*refs):
        rest = refs[given + idle :]
        return kernel(*refs[:given], *rest[: len(outs)], *rest[len(outs) + len(carry) :])

    return pl.pallas_call(
        body,
        name=name,
        in_specs=[IN_VMEM] * len(operands)
        + [ANYWHERE] * len(far)
        + [IN_VMEM] * len(after)
        + [ANYWHERE] * len(carry),
        out_specs=[IN_VMEM] * len(outs) + [ANYWHERE] * len(carry),
        out_shape=[pltpu.VMEM(shape, dtype) for shape, dtype in outs]
        + [jax.ShapeDtypeStruct(a.shape, a.dtype) for a in carry],
        scratch_shapes=list(scratch),
        input_output_aliases={given + len(after) + i: len(outs) + i for i in range(len(carry))},
        compiler_params=pltpu.CompilerParams(vmem_limit_bytes=SCOPE),
        cost_estimate=pl.CostEstimate(flops=weight, bytes_accessed=1, transcendentals=0),
        **kw,
    )(*operands, *far, *after, *carry)


def start_all(sems, pairs):
    fetches = [pltpu.make_async_copy(source, target, sems.at[i]) for i, (source, target) in enumerate(pairs)]
    for fetch in fetches:
        fetch.start()
    return fetches


def tiles(width):
    tile = min(512, width)
    return [slice(i, i + tile) for i in range(0, width, tile)]


def lane_split(head_size, shape):
    return lax.broadcasted_iota(jnp.int32, shape, 1) // head_size


def spread(values, lane_head, first):
    shape = (values.shape[0], LANES)
    out = jnp.broadcast_to(values[:, first : first + 1], shape)
    for k in range(1, lane_head[1]):
        out = jnp.where(lane_head[0] == k, values[:, first + k : first + k + 1], out)
    return out


def lane_heads(head_size):
    return (lane_split(head_size, (1, LANES)), LANES // head_size)


def column(row):
    return jnp.broadcast_to(row, (LANES, row.shape[1])).T[:, :1]


def head_column(row):
    heads = row.shape[1]
    padded = jnp.concatenate([row, jnp.zeros((1, LANES - heads), F32)], axis=1)
    return jnp.broadcast_to(padded, (LANES, LANES)).T[:heads, :1]


def turned(values):
    heads, rows = values.shape
    return jnp.concatenate([values, jnp.zeros((LANES - heads, rows), F32)], axis=0).T[:, :heads]


def prep_kernel(model, head_size, x_all, b_all, raw_all, bias_all, rate_all, skip_all, seg_all, msg_ref, run_ref, q_ref, step_ref, row_ref, *scratch):
    x_ref, b_ref, raw_ref, bias_ref, rate_ref, skip_ref, seg_ref, sems = scratch
    rows, channels = x_ref.shape[1:]
    mine = pl.ds(model, 1)
    cuts = tiles(channels)
    fetches = start_all(
        sems,
        [(raw_all.at[mine], raw_ref), (bias_all, bias_ref), (rate_all, rate_ref), (skip_all, skip_ref)]
        + [(seg_all, seg_ref), (b_all.at[mine], b_ref)]
        + [(x_all.at[mine, :, cut], x_ref.at[:, :, cut]) for cut in cuts],
    )
    for fetch in fetches[:6]:
        fetch.wait()
    heads = raw_ref.shape[1]
    state = b_ref.shape[2]
    step_t = jax.nn.softplus(raw_ref[0] + head_column(bias_ref[model : model + 1, :]))
    log_decay = -head_column(rate_ref[model : model + 1, :]) * step_t
    earlier = lax.broadcasted_iota(jnp.int32, (rows, rows), 0)
    later = lax.broadcasted_iota(jnp.int32, (rows, rows), 1)
    tri = (later >= earlier).astype(F32)
    run_t = jnp.dot(log_decay, tri, precision=lax.Precision.HIGHEST, preferred_element_type=F32)
    run, step = turned(run_t), turned(step_t)
    run_ref[:, :rows] = run_t
    run_ref[:, rows:] = jnp.broadcast_to(head_column(skip_ref[model : model + 1, :]), (heads, LANES))
    step_ref[...] = step_t
    q_ref[...] = run_t - jnp.log(step_t)
    seg_row = seg_ref[...].astype(F32)
    row_ref[...] = seg_row
    seg_col = column(seg_row)
    last = seg_row[:, rows - 1 :]
    total = run[rows - 1 :, :]
    tail = jnp.exp(total - run) * step * (seg_col == last).astype(F32)
    etot = jnp.exp(total)
    b_t = b_ref[0].astype(F32).T.astype(BF16)
    lane_head = lane_heads(head_size)
    row_id = lax.broadcasted_iota(jnp.int32, (EXTRA, LANES), 0)
    for p in range(channels // LANES):
        cols = slice(p * LANES, (p + 1) * LANES)
        first = p * lane_head[1]
        for cut, fetch in zip(cuts, fetches[6:]):
            if cut.start == cols.start:
                fetch.wait()
        xw = (x_ref[0, :, cols].astype(F32) * spread(tail, lane_head, first)).astype(BF16)
        msg_ref[:state, cols] = dot(b_t, xw).astype(BF16)
        decay = spread(etot, lane_head, first)
        high = decay.astype(BF16).astype(F32)
        extra = jnp.where(row_id == 0, high, jnp.where(row_id == 1, decay - high, jnp.where(row_id == 2, last, 0.0)))
        msg_ref[state:, cols] = extra.astype(BF16)


def prep(model, head_size, x, b, raw, bias, rate, skip, seg_row, after=()):
    _, rows, channels = x.shape
    heads, state = raw.shape[1], b.shape[2]
    far = (x, b, raw, bias, rate, skip, seg_row)
    return call(
        functools.partial(prep_kernel, model, head_size),
        f"prep_{model}",
        (),
        [((state + EXTRA, channels), BF16), ((heads, rows + LANES), F32), ((heads, rows), F32), ((heads, rows), F32), ((1, rows), F32)],
        far,
        after,
        scratch=[pltpu.VMEM((1,) + a.shape[1:] if a.ndim == 3 else a.shape, a.dtype) for a in far]
        + [pltpu.SemaphoreType.DMA((6 + len(tiles(channels)),))],
    )


def inside_kernel(model, head_size, run_ref, q_ref, step_ref, seg_ref, x_all, gate_all_, b_all, c_all, yg_ref, fg_ref, *scratch):
    x_ref, gate_ref, b_ref, c_ref, sems = scratch
    rows, channels = x_ref.shape[1:]
    mine = pl.ds(model, 1)
    cuts = tiles(channels)
    fetches = start_all(
        sems,
        [(b_all.at[mine], b_ref), (c_all.at[mine], c_ref)]
        + [pair for cut in cuts for pair in ((x_all.at[mine, :, cut], x_ref.at[:, :, cut]), (gate_all_.at[mine, :, cut], gate_ref.at[:, :, cut]))],
    )
    for fetch in fetches[:2]:
        fetch.wait()
    half = rows // 2
    lane_head = lane_heads(head_size)
    run, step, q = turned(run_ref[:, :rows]), turned(step_ref[...]), q_ref[...]
    skip = turned(run_ref[:, rows:])[:1]
    seg_row = seg_ref[...].astype(F32)
    seg_col = column(seg_row)

    products = lax.dot_general(c_ref[0], b_ref[0], (((1,), (1,)), ((), ())), preferred_element_type=F32)
    tri = lax.broadcasted_iota(jnp.int32, (half, half), 0) >= lax.broadcasted_iota(jnp.int32, (half, half), 1)
    parts = [slice(0, half), slice(half, rows)]
    masks = [tri & (seg_col[part] == seg_row[:, part]) for part in parts]
    diagonal = [products[part, part] for part in parts]
    below = jnp.where(seg_col[parts[1]] == seg_row[:, parts[0]], products[parts[1], parts[0]], 0.0).astype(BF16)
    middle = run[half - 1 : half, :]
    entry = jnp.exp(run[parts[1]] - middle)
    leave = jnp.exp(middle - run[parts[0]]) * step[parts[0]]
    factor = jnp.exp(run)
    for p in range(channels // LANES):
        cols = slice(p * LANES, (p + 1) * LANES)
        first = p * lane_head[1]
        for i, cut in enumerate(cuts):
            if cut.start == cols.start:
                fetches[2 + 2 * i].wait()
                fetches[3 + 2 * i].wait()
        x = x_ref[0, :, cols]
        xf = x.astype(F32)
        ys = []
        for part, mask, prod in zip(parts, masks, diagonal):
            y = None
            for k in range(lane_head[1]):
                h = first + k
                mixing = jnp.exp(jnp.where(mask, run[part, h : h + 1] - q[h : h + 1, part], NEG))
                term = dot((mixing * prod).astype(BF16), x[part])
                y = term if y is None else jnp.where(lane_head[0] == k, term, y)
            ys.append(y)
        sent = (xf[parts[0]] * spread(leave, lane_head, first)).astype(BF16)
        ys[1] = ys[1] + dot(below, sent) * spread(entry, lane_head, first)
        y = jnp.concatenate(ys, axis=0) + spread(skip, lane_head, first) * xf
        v = gate_ref[0, :, cols].astype(F32)
        silu = v / (1.0 + jnp.exp(-v))
        yg_ref[:, cols] = (y * silu).astype(BF16)
        fg_ref[:, cols] = (spread(factor, lane_head, first) * silu).astype(BF16)


def inside(model, head_size, x, gate, b, c, run, q, step, seg_row, after=()):
    _, rows, channels = x.shape
    far = (x, gate, b, c)
    return call(
        functools.partial(inside_kernel, model, head_size),
        f"inside_{model}",
        (run, q, step, seg_row),
        [((rows, channels), BF16)] * 2,
        far,
        after,
        scratch=[pltpu.VMEM((1,) + a.shape[1:], a.dtype) for a in far]
        + [pltpu.SemaphoreType.DMA((2 + 2 * len(tiles(channels)),))],
    )


def load_kernel(w_all, w_ref, sems):
    for fetch in start_all(sems, [(w_all.at[i], w_ref.at[i]) for i in range(w_all.shape[0])]):
        fetch.wait()


def load(w, after):
    return call(load_kernel, "load", (), [(w.shape, BF16)], (w,), after, scratch=[pltpu.SemaphoreType.DMA((w.shape[0],))])


def join_kernel(state, own_ref, got_ref, out_ref):
    own, got = own_ref[...].astype(F32), got_ref[...].astype(F32)
    same = (own[state + 2 : state + 3] == got[state + 2 : state + 3]).astype(F32)
    decay = (own[state : state + 1] + own[state + 1 : state + 2]) * same
    out_ref[:state, :] = (own[:state] + decay * got[:state]).astype(BF16)
    out_ref[state:, :] = own_ref[state:, :]


def join(model, state, own, got, after=()):
    return call(functools.partial(join_kernel, state), f"join_{model}", (own, got), [(own.shape, BF16)], (), after)[0]


def gate_kernel(model, state, alone, near_ref, *refs):
    far_refs, refs = refs[:-7], refs[-7:]
    c_ref, seg_ref, yg_ref, fg_ref, gain_ref, g_ref, ss_ref = refs
    rows, channels = yg_ref.shape
    paired = True if alone else lax.axis_index("seq") % 2 == 1
    seg_col = column(seg_ref[...])
    squares = jnp.zeros((8, rows), F32)
    for cols in tiles(channels):
        near = near_ref[:, cols].astype(F32)
        far = far_refs[0][:, cols].astype(F32)
        for ref in far_refs[1:]:
            far = far + ref[:, cols].astype(F32)
        last_near, last_far = near[state + 2 : state + 3], far[state + 2 : state + 3]
        decay = (near[state : state + 1] + near[state + 1 : state + 2]) * (last_near == last_far).astype(F32)
        entering = (near[:state] + jnp.where(paired, decay, 1.0) * far[:state]).astype(BF16)
        anchor = jnp.where(paired, last_near, last_far)[:, :1]
        reached = (seg_col == anchor).astype(F32)
        gated = yg_ref[:, cols].astype(F32) + reached * fg_ref[:, cols].astype(F32) * dot(c_ref[model], entering)
        g_ref[:, cols] = (gated * gain_ref[model : model + 1, cols]).astype(BF16)
        ones = jnp.ones((8, cols.stop - cols.start), BF16)
        squares += lax.dot_general(
            ones, (gated * gated).astype(BF16), (((1,), (1,)), ((), ())), preferred_element_type=F32
        )
    ss_ref[...] = squares


def gate_all(model, alone, near, far, c, seg_row, yg, fg, gain, after=()):
    return call(
        functools.partial(gate_kernel, model, c.shape[2], alone),
        f"gated_{model}",
        (near, *far, c, seg_row, yg, fg, gain),
        [(yg.shape, BF16), ((8, yg.shape[0]), F32)],
        (),
        after,
    )


def project_kernel(model, shapes, forward, sends, *refs):
    given, (w_ref, keep_ref, *refs) = refs[: sum(shapes)], refs[sum(shapes) :]
    count = len(shapes)
    half, width = keep_ref.shape[1], w_ref.shape[2]
    send_refs, (*refs, lhs) = refs[: len(sends)], refs[len(sends) :]
    first = lax.axis_index("head") % 2 == 0
    if forward:
        refs[0][...] = given[0][:half, :]
        refs[1][...] = given[1][half:, :]
    row = 0
    for ref in given:
        lhs[row : row + ref.shape[0], :] = ref[...]
        row += ref.shape[0]
    def put(result, ref, blocks, start, at, size):
        for k in range(count):
            early = result[2 * k * half : (2 * k + 1) * half].astype(BF16)
            late = result[(2 * k + 1) * half : (2 * k + 2) * half].astype(BF16)
            keep_ref[k, :, pl.ds(start + at, size)] = jnp.where(first, early, late)
            which, place = (ref, blocks.index(k)) if k in blocks else (None, 0)
            if which is None:
                which, place = [(r, part.index(k)) for r, (part, *_) in zip(send_refs, sends) if k in part][0]
            which[place, :, pl.ds(at, size)] = jnp.where(first, late, early)

    tile = min(1024, width)
    done = set()
    for ref, (blocks, start, stop) in zip(send_refs, sends):
        if start in done:
            continue
        done.add(start)

        def step(j, _, ref=ref, blocks=blocks, start=start):
            at = pl.multiple_of(j * tile, tile)
            put(dot(lhs[...], w_ref[model, :, pl.ds(start + at, tile)]), ref, blocks, start, at, tile)
            return 0

        lax.fori_loop(0, (stop - start) // tile, step, 0)


def project(name, model, blocks, weights, after=(), forward=False, split=None, weight=1):
    w, = weights
    flat = [a for block in blocks for a in block]
    depth, width = w.shape[1:]
    n, full = len(blocks), width
    half = sum(a.shape[0] for a in flat) // (2 * n)
    if split == "blocks":
        sends = [([k], 0, full) for k in range(n)]
    elif split == "columns":
        sends = [(list(range(n)), 0, width // 2), (list(range(n)), width // 2, full)]
    else:
        sends = [(list(range(n)), 0, full)]
    return call(
        functools.partial(project_kernel, model, [len(block) for block in blocks], forward, sends),
        name,
        (*flat, w),
        [((n, half, full), BF16)]
        + [((len(part), half, stop - start), BF16) for part, start, stop in sends]
        + [((half, depth), BF16)] * (2 * forward),
        (),
        after,
        scratch=[pltpu.VMEM((2 * half * n, depth), BF16)],
        weight=weight,
    )


def release(name, arrays, after, weight=1):
    return call(lambda *refs: None, name, (), [], (), after, carry=arrays, weight=weight)


def inner_column():
    s = lax.axis_index("seq")
    return (s == 1) | (s == 2)


def pair_kernel(places, counts, own_sent, *refs):
    keeps, gots = refs[:2], (refs[2 : 2 + counts[0]], refs[2 + counts[0] : 2 + sum(counts)])
    first_ref, second_ref = refs[-2:]
    turned_round = (lax.axis_index("seq") // 2 + lax.axis_index("head") // 2) % 2 == 0
    if own_sent:
        turned_round = turned_round | inner_column()

    def ends(pieces):
        stops = [0]
        for ref in pieces:
            stops.append(stops[-1] + ref.shape[2])
        return stops

    bounds = sorted({*ends(gots[0]), *ends(gots[1])})
    for start, stop in zip(bounds, bounds[1:]):
        sums = []
        for keep, pieces, (at, got_at) in zip(keeps, gots, places):
            stops = ends(pieces)
            piece = max(i for i, lower in enumerate(stops) if lower <= start)
            got = pieces[piece][got_at, :, start - stops[piece] : stop - stops[piece]]
            sums.append(keep[at, :, start:stop].astype(F32) + got.astype(F32))
        first_ref[:, start:stop] = jnp.where(turned_round, sums[1], sums[0]).astype(BF16)
        second_ref[:, start:stop] = jnp.where(turned_round, sums[0], sums[1]).astype(BF16)


def pair_sums(name, one, other, after=(), own_sent=False):
    return call(
        functools.partial(pair_kernel, ((one[1], one[3]), (other[1], other[3])), (len(one[2]), len(other[2])), own_sent),
        name,
        (one[0], other[0], *one[2], *other[2]),
        [(one[0].shape[1:], BF16)] * 2,
        (),
        after,
    )


def add_kernel(own_ref, got_ref, out_ref):
    out_ref[...] = (own_ref[...].astype(F32) + got_ref[...].astype(F32)).astype(BF16)


def add(name, own, got, after=()):
    return call(add_kernel, name, (own, got), [(own.shape, BF16)], (), after)


def join_own_kernel(first_ref, second_ref, one_ref, two_ref, out_ref):
    mine = inner_column() & (lax.axis_index("seq") == lax.axis_index("head") // 2)
    other = inner_column() & ~mine
    base = jnp.where(mine, first_ref[...], second_ref[...])
    got = jnp.where(other, two_ref[...], one_ref[...])
    out_ref[...] = (base.astype(F32) + got.astype(F32)).astype(BF16)


def pick_kernel(beside_ref, *refs):
    *terms, out_ref = refs
    value = sum((ref[...] if len(ref.shape) == 2 else ref[0]).astype(F32) for ref in terms)
    out_ref[...] = jnp.where(inner_column(), value.astype(BF16), beside_ref[...])


def pick(name, beside, terms, after=()):
    return call(pick_kernel, name, (beside, *terms), [(beside.shape, BF16)], (), after)[0]


def first_sums_kernel(one_ref, other_ref, out_ref):
    rows = lax.broadcasted_iota(jnp.int32, out_ref.shape, 0)
    out_ref[...] = jnp.where(rows < 4, one_ref[...], other_ref[...])


def sums_kernel(one_ref, other_ref, out_ref):
    out_ref[...] = one_ref[...] + other_ref[...]


def last_kernel(total, model, own_sent, *refs):
    first_n, join_n, three_n, first_d, second_d, one_d, join_d, three_d, two, ss_ref, out_ref = refs
    half = out_ref.shape[1]
    s, z = lax.axis_index("seq"), lax.axis_index("head") // 2
    row = ss_ref[4 * model : 4 * model + 1, :]
    row = jnp.where(lax.axis_index("head") % 2 == 0, row[:, :half], row[:, half:])
    scale = column(lax.rsqrt(row / total + EPS))
    straight = (s == z) | (s + z == 3)
    inner = inner_column()

    def write(condition, *terms):
        @pl.when(condition)
        def _():
            value = terms[0][...].astype(F32)
            for ref in terms[1:]:
                value = value + ref[...].astype(F32)
            out_ref[0] = (value * scale).astype(BF16)

    write(~straight & ~inner, first_n, two, three_n)
    write(~straight & inner, join_n, three_n)
    write(straight & ~inner, join_d, three_d)
    if own_sent:
        write(straight & inner & (s == z), second_d, two, three_d)
        write(straight & inner & (s != z), first_d, one_d, three_d)
    else:
        write(straight & inner, first_d, two, three_d)


def last(model, total, own_sent, operands, before, after=()):
    half, width = operands[0].shape
    earlier = () if before is None else (before,)
    kernel = functools.partial(last_kernel, total, model, own_sent)
    return pl.pallas_call(
        lambda *refs: kernel(*refs[: len(operands)], refs[-1]),
        name=f"last_{model}",
        grid=(1,),
        in_specs=[IN_VMEM] * (len(operands) + len(after))
        + [ANYWHERE] * len(earlier),
        out_specs=pl.BlockSpec((1, half, width), lambda i: (model, 0, 0)),
        out_shape=jax.ShapeDtypeStruct((2, half, width), BF16),
        input_output_aliases={len(operands) + len(after): 0} if earlier else {},
        compiler_params=pltpu.CompilerParams(vmem_limit_bytes=SCOPE),
        cost_estimate=pl.CostEstimate(flops=1 if earlier else HEAVY, bytes_accessed=1, transcendentals=0),
    )(*operands, *after, *earlier)


def xor_pairs(n, k):
    return [(i, i ^ k) for i in range(n)]


def fast(x, gate, b, c, raw, bias, rate, skip, gain, w, seg):
    raw = jnp.swapaxes(raw, 1, 2)
    head_size = x.shape[2] // raw.shape[1]
    state = b.shape[2]
    n_seq, n_head = lax.axis_size("seq"), lax.axis_size("head")
    total = x.shape[2] * n_head
    seg_row = seg.reshape(1, -1)
    def flat(si, zi, ci):
        return si * n_head + zi * 2 + ci

    def sends(kinds, turn):
        pairs = []
        for si in range(n_seq):
            if turn == 1:
                steps = [(0, 1), (3, 2)]
            elif 0 in [si ^ k for k in kinds]:
                steps = [(1, 0), (3, 2), (2, 3), (0, 1)] if turn == 0 else [(2, 0), (1, 3)]
            else:
                steps = [(0, 1), (3, 2)] if turn == 0 else [(1, 2), (2, 1)]
            pairs += [(flat(si, a, ci), flat(si, o, ci)) for a, o in steps for ci in range(2)]
        return pairs

    ring = [(0, 1), (2, 3)]
    across = lambda a: lax.ppermute(a, "head", xor_pairs(n_head, 1))
    beside = lambda a, k: lax.ppermute(a, "seq", xor_pairs(n_seq, k))
    ss = jnp.zeros((8, x.shape[1]), F32)

    x, gate, raw, bias, rate, skip, w = (
        pltpu.with_memory_space_constraint(a, pltpu.HBM) for a in (x, gate, raw, bias, rate, skip, w)
    )
    b_far, c_far, seg_far = (pltpu.with_memory_space_constraint(a, pltpu.HBM) for a in (b, c, seg_row))
    msg0, *scan0 = prep(0, head_size, x, b_far, raw, bias, rate, skip, seg_far)
    near0 = lax.ppermute(msg0, "seq", ring)
    msg1, *scan1 = prep(1, head_size, x, b_far, raw, bias, rate, skip, seg_far, (msg0, *scan0))
    near1 = lax.ppermute(msg1, "seq", ring)
    yg0, fg0 = inside(0, head_size, x, gate, b_far, c_far, *scan0, (msg0, msg1, *scan1))
    end0 = join(0, state, msg0, near0, (yg0, fg0, msg1, scan0[-1], *scan1))
    far0 = [lax.ppermute(end0, "seq", [(1, t)]) for t in (2, 3)]
    yg1, fg1 = inside(1, head_size, x, gate, b_far, c_far, *scan1, (end0, yg0, fg0, near0, msg1, scan0[-1]))
    end1 = join(1, state, msg1, near1, (yg0, fg0, near0, yg1, fg1, scan0[-1], scan1[-1], *far0))
    far1 = [lax.ppermute(end1, "seq", [(1, t)]) for t in (2, 3)]
    held = (near1, yg1, fg1, scan1[-1])
    w = load(w, (end1, near0, yg0, fg0, scan0[-1], *far0, *held))
    g0, ss0 = gate_all(0, False, near0, far0, c, scan0[-1], yg0, fg0, gain, (*w, *far1, *held))
    x0, y0 = beside(g0, 1), beside(g0, 2)
    g1, ss1 = gate_all(1, False, near1, far1, c, scan1[-1], yg1, fg1, gain, (*w, g0, ss0))
    x1, y1 = beside(g1, 1), beside(g1, 2)

    def both(forwarded):
        return beside(forwarded[0], 2), beside(forwarded[1], 1)

    def turn(value, kinds, i):
        return lax.ppermute(value, ("seq", "head"), sends(kinds, i))

    xy, od = (1, 2), (0, 3)
    def add_sums(k, ss, after):
        return call(sums_kernel, f"sums_{k}", (ss, lax.ppermute(ss, "head", xor_pairs(n_head, k))), [(ss.shape, F32)], (), after)[0]

    ss, = call(first_sums_kernel, "sums_0", (ss0, ss1), [(ss0.shape, F32)], (), (*w, g0, g1))
    keep_o0, send_o0 = project("own_0", 0, [(g0,)], w, (g1, ss))
    ss = add_sums(1, ss, (*w, g1, keep_o0, send_o0))
    keep_o1, send_o1 = project("own_1", 1, [(g1,)], w, (ss, keep_o0, send_o0))
    held = (*w, keep_o0, keep_o1, send_o1)
    ss = add_sums(2, ss, (send_o0, *held))
    ss = add_sums(4, ss, (send_o0, *held))
    keep_n0, *send_n0, f0, l0 = project("next_0", 0, [(x0,), (y0,)], w, (ss, send_o0, *held), True, "blocks")
    got_n0 = [across(a) for a in send_n0]
    got_o0 = across(send_o0)
    first_n0, second_n0 = pair_sums(
        "sum_next_0", (keep_n0, 0, got_n0[:1], 0), (keep_n0, 1, got_n0[1:], 0), (f0, l0, got_o0, *held)
    )
    one_n0 = turn(first_n0, xy, 0)
    third_0 = pick("pick_0", second_n0, (keep_o0, got_o0), (first_n0, f0, l0, *held))
    two_n0 = turn(third_0, xy, 1)
    got_o1 = across(send_o1)
    own0, own1 = (keep_o0, 0, (got_o0,), 0), (keep_o1, 0, (got_o1,), 0)
    held = (*w, keep_o0, keep_o1, first_n0, got_o0)
    f0, l0 = release("release_0", (f0, l0), (x1, y1, second_n0, third_0, *held), HEAVY)
    d0 = both((f0, l0))
    held = (*held, second_n0)
    keep_n1, send_n1, f1, l1 = project("next_1", 1, [(x1,), (y1,)], w, (f0, *held), True)
    got_n1 = across(send_n1)
    held = (*held[:-1], keep_n1, f1, l1)
    join_n0, = add("add_next_0", second_n0, one_n0, (got_o1, *held))
    three_n0 = turn(join_n0, xy, 2)
    held = (*held[:-3], got_o1, join_n0)
    f1, l1 = release("release_1", (f1, l1), (*d0, keep_n1, *held))
    d1 = both((f1, l1))
    keep_n1, = release("gate_1", (keep_n1,), (f1, two_n0, *d0, *held), HEAVY)
    held = (*held, two_n0)
    first_n1, second_n1 = pair_sums(
        "sum_next_1", (keep_n1, 0, (got_n1,), 0), (keep_n1, 1, (got_n1,), 1), (*d0, *held)
    )
    held = (*held, first_n1, second_n1)
    keep_d0, *send_d0 = project("opposite_0", 0, [d0], w, held, False, "columns")
    got_d0 = [across(a) for a in send_d0]
    first_d0, second_d0 = pair_sums("sum_opposite_0", own0, (keep_d0, 0, got_d0, 0), held, True)
    one_d0 = turn(first_d0, od, 0)
    first_n1, = release("release_n1", (first_n1,), (first_d0, second_d0, *held[:-2], second_n1))
    one_n1 = turn(first_n1, xy, 0)
    held = (keep_o1, got_o1, first_n0, join_n0, two_n0, three_n0, first_n1, second_n1, first_d0, second_d0)
    keep_d1, *send_d1 = project("opposite_1", 1, [d1], w, held, False, "columns", HEAVY)
    got_d1 = [across(a) for a in send_d1]
    first_d1, second_d1 = pair_sums("sum_opposite_1", own1, (keep_d1, 0, got_d1, 0), held)
    one_d1 = turn(first_d1, od, 0)
    held = (*held[2:], first_d1, second_d1)
    join_d0, = call(
        join_own_kernel, "add_opposite_0", (first_d0, second_d0, one_d0, two_n0), [(first_d0.shape, BF16)], (), held
    )
    three_d0 = turn(join_d0, od, 2)
    held = (*held, one_d0, join_d0)
    third_1 = pick("pick_1", second_n1, (second_d1,), held)
    two_1 = turn(third_1, xy, 1)
    join_n1, = add("add_next_1", second_n1, one_n1, (third_1, *held))
    three_n1 = turn(join_n1, xy, 2)
    held = (*held, join_n1)
    join_d1, = add("add_opposite_1", second_d1, one_d1, (three_d0, *held))
    three_d1 = turn(join_d1, od, 2)
    ss, = release("release_sums", (ss,), (first_d1, second_d1))
    ss = lax.ppermute(
        ss, ("seq", "head"),
        [(flat(zi, si, ci), flat(si, zi, ci)) for si in range(n_seq) for zi in range(n_seq) for ci in range(2)],
    )
    held = (first_n1, join_n1, three_n1, first_d1, second_d1, one_d1, join_d1, two_1)
    out = last(
        0, total, True, (first_n0, join_n0, three_n0, first_d0, second_d0, one_d0, join_d0, three_d0, two_n0, ss), None, held
    )
    return last(
        1, total, False, (first_n1, join_n1, three_n1, first_d1, second_d1, one_d1, join_d1, three_d1, two_1, ss), out
    )


def plain(x, gate, b, c, raw, bias, rate, skip, gain, w, seg):
    raw = jnp.swapaxes(raw, 1, 2)
    head_size = x.shape[2] // raw.shape[1]
    state = b.shape[2]
    n_seq, n_head = lax.axis_size("seq"), lax.axis_size("head")
    total = x.shape[2] * n_head
    seg_row = seg.reshape(1, -1)
    s, h = lax.axis_index("seq"), lax.axis_index("head")
    gs, sums = [], []
    for m in range(2):
        msg, *scan = prep(m, head_size, x, b, raw, bias, rate, skip, seg_row)
        every = lax.all_gather(msg, "seq").astype(F32)
        entering, before = jnp.zeros_like(every[0]), every[0]
        for k in range(n_seq - 1):
            now = every[k]
            same = (now[state + 2] == before[state + 2]).astype(F32)
            decay = (now[state] + now[state + 1]) * same
            new = jnp.concatenate([now[:state] + decay * entering[:state], now[state:]])
            entering = jnp.where(k < s, new, entering)
            before = now
        yg, fg = inside(m, head_size, x, gate, b, c, *scan)
        near = entering.astype(BF16)
        g, ss = gate_all(m, True, near, [jnp.zeros_like(near)], c, scan[-1], yg, fg, gain)
        gs.append(g)
        sums.append(ss[0])
    g = lax.all_gather(jnp.stack(gs), "seq", axis=1, tiled=True)
    terms = jnp.einsum("mtk,mkd->mtd", g, w, preferred_element_type=F32)
    summed = lax.psum_scatter(terms.astype(BF16), "head", scatter_dimension=1, tiled=True)
    squares = lax.all_gather(lax.psum(jnp.stack(sums), "head"), "seq", axis=1, tiled=True)
    mine = lax.dynamic_slice_in_dim(squares, h * summed.shape[1], summed.shape[1], axis=1)
    return (summed.astype(F32) * lax.rsqrt(mine / total + EPS)[:, :, None]).astype(BF16)


def solution(mesh):
    placed = (
        P(None, "seq", "head"),
        P(None, "seq", "head"),
        P(None, "seq", None),
        P(None, "seq", None),
        P(None, "seq", "head"),
        P(None, "head"),
        P(None, "head"),
        P(None, "head"),
        P(None, "head"),
        P(None, "head", "seq"),
        P("seq"),
    )
    local = fast if mesh.shape["seq"] == 4 and mesh.shape["head"] == 8 else plain
    return jax.shard_map(
        local, mesh=mesh, in_specs=placed, out_specs=P(None, "head", "seq"), check_vma=False
    )
```

```python
import functools
import jax
import jax.numpy as jnp
from jax import lax
from jax.experimental import pallas as pl
from jax.experimental.pallas import tpu as pltpu
from jax.sharding import PartitionSpec as P

F32, BF16 = jnp.float32, jnp.bfloat16
LANES = 128
EXTRA = 16
NEG = -1e30
EPS = 1e-05
IN_VMEM = pl.BlockSpec(memory_space=pltpu.VMEM)
ANYWHERE = pl.BlockSpec(memory_space=pl.ANY)
SCOPE = 16 * 1024 * 1024
HEAVY = 10**11


def dot(a, b):
    return jnp.dot(a, b, preferred_element_type=F32)


def call(kernel, name, operands, outs, far=(), after=(), carry=(), scratch=(), weight=1, **kw):
    given, idle = len(operands) + len(far), len(after) + len(carry)

    def body(*refs):
        rest = refs[given + idle :]
        return kernel(*refs[:given], *rest[: len(outs)], *rest[len(outs) + len(carry) :])

    return pl.pallas_call(
        body,
        name=name,
        in_specs=[IN_VMEM] * len(operands)
        + [ANYWHERE] * len(far)
        + [IN_VMEM] * len(after)
        + [ANYWHERE] * len(carry),
        out_specs=[IN_VMEM] * len(outs) + [ANYWHERE] * len(carry),
        out_shape=[pltpu.VMEM(shape, dtype) for shape, dtype in outs]
        + [jax.ShapeDtypeStruct(a.shape, a.dtype) for a in carry],
        scratch_shapes=list(scratch),
        input_output_aliases={given + len(after) + i: len(outs) + i for i in range(len(carry))},
        compiler_params=pltpu.CompilerParams(vmem_limit_bytes=SCOPE),
        cost_estimate=pl.CostEstimate(flops=weight, bytes_accessed=1, transcendentals=0),
        **kw,
    )(*operands, *far, *after, *carry)


def start_all(sems, pairs):
    fetches = [pltpu.make_async_copy(source, target, sems.at[i]) for i, (source, target) in enumerate(pairs)]
    for fetch in fetches:
        fetch.start()
    return fetches


def tiles(width):
    tile = min(512, width)
    return [slice(i, i + tile) for i in range(0, width, tile)]


def lane_split(head_size, shape):
    return lax.broadcasted_iota(jnp.int32, shape, 1) // head_size


def spread(values, lane_head, first):
    shape = (values.shape[0], LANES)
    out = jnp.broadcast_to(values[:, first : first + 1], shape)
    for k in range(1, lane_head[1]):
        out = jnp.where(lane_head[0] == k, values[:, first + k : first + k + 1], out)
    return out


def lane_heads(head_size):
    return (lane_split(head_size, (1, LANES)), LANES // head_size)


def column(row):
    return jnp.broadcast_to(row, (LANES, row.shape[1])).T[:, :1]


def head_column(row):
    heads = row.shape[1]
    padded = jnp.concatenate([row, jnp.zeros((1, LANES - heads), F32)], axis=1)
    return jnp.broadcast_to(padded, (LANES, LANES)).T[:heads, :1]


def turned(values):
    heads, rows = values.shape
    return jnp.concatenate([values, jnp.zeros((LANES - heads, rows), F32)], axis=0).T[:, :heads]


def prep_kernel(model, head_size, x_all, b_all, raw_all, bias_all, rate_all, skip_all, seg_all, msg_ref, run_ref, q_ref, step_ref, row_ref, *scratch):
    x_ref, b_ref, raw_ref, bias_ref, rate_ref, skip_ref, seg_ref, sems = scratch
    rows, channels = x_ref.shape[1:]
    mine = pl.ds(model, 1)
    cuts = tiles(channels)
    fetches = start_all(
        sems,
        [(raw_all.at[mine], raw_ref), (bias_all, bias_ref), (rate_all, rate_ref), (skip_all, skip_ref)]
        + [(seg_all, seg_ref), (b_all.at[mine], b_ref)]
        + [(x_all.at[mine, :, cut], x_ref.at[:, :, cut]) for cut in cuts],
    )
    for fetch in fetches[:6]:
        fetch.wait()
    heads = raw_ref.shape[1]
    state = b_ref.shape[2]
    step_t = jax.nn.softplus(raw_ref[0] + head_column(bias_ref[model : model + 1, :]))
    log_decay = -head_column(rate_ref[model : model + 1, :]) * step_t
    earlier = lax.broadcasted_iota(jnp.int32, (rows, rows), 0)
    later = lax.broadcasted_iota(jnp.int32, (rows, rows), 1)
    tri = (later >= earlier).astype(F32)
    run_t = jnp.dot(log_decay, tri, precision=lax.Precision.HIGHEST, preferred_element_type=F32)
    run, step = turned(run_t), turned(step_t)
    run_ref[:, :rows] = run_t
    run_ref[:, rows:] = jnp.broadcast_to(head_column(skip_ref[model : model + 1, :]), (heads, LANES))
    step_ref[...] = step_t
    q_ref[...] = run_t - jnp.log(step_t)
    seg_row = seg_ref[...].astype(F32)
    row_ref[...] = seg_row
    seg_col = column(seg_row)
    last = seg_row[:, rows - 1 :]
    total = run[rows - 1 :, :]
    tail = jnp.exp(total - run) * step * (seg_col == last).astype(F32)
    etot = jnp.exp(total)
    b_t = b_ref[0].astype(F32).T.astype(BF16)
    lane_head = lane_heads(head_size)
    row_id = lax.broadcasted_iota(jnp.int32, (EXTRA, LANES), 0)
    wide = []
    for p in range(channels // LANES):
        cols = slice(p * LANES, (p + 1) * LANES)
        first = p * lane_head[1]
        for cut, fetch in zip(cuts, fetches[6:]):
            if cut.start == cols.start:
                fetch.wait()
        xw = (x_ref[0, :, cols].astype(F32) * spread(tail, lane_head, first)).astype(BF16)
        wide.append(xw)
        for cut in cuts:
            if cut.stop == cols.stop:
                msg_ref[:state, cut] = dot(b_t, jnp.concatenate(wide, axis=1)).astype(BF16)
                wide = []
        decay = spread(etot, lane_head, first)
        high = decay.astype(BF16).astype(F32)
        extra = jnp.where(row_id == 0, high, jnp.where(row_id == 1, decay - high, jnp.where(row_id == 2, last, 0.0)))
        msg_ref[state:, cols] = extra.astype(BF16)


def prep(model, head_size, x, b, raw, bias, rate, skip, seg_row, after=()):
    _, rows, channels = x.shape
    heads, state = raw.shape[1], b.shape[2]
    far = (x, b, raw, bias, rate, skip, seg_row)
    return call(
        functools.partial(prep_kernel, model, head_size),
        f"prep_{model}",
        (),
        [((state + EXTRA, channels), BF16), ((heads, rows + LANES), F32), ((heads, rows), F32), ((heads, rows), F32), ((1, rows), F32)],
        far,
        after,
        scratch=[pltpu.VMEM((1,) + a.shape[1:] if a.ndim == 3 else a.shape, a.dtype) for a in far]
        + [pltpu.SemaphoreType.DMA((6 + len(tiles(channels)),))],
    )


def inside_kernel(model, head_size, run_ref, q_ref, step_ref, seg_ref, x_all, gate_all_, b_all, c_all, yg_ref, fg_ref, *scratch):
    x_ref, gate_ref, b_ref, c_ref, sems = scratch
    rows, channels = x_ref.shape[1:]
    mine = pl.ds(model, 1)
    cuts = tiles(channels)
    fetches = start_all(
        sems,
        [(b_all.at[mine], b_ref), (c_all.at[mine], c_ref)]
        + [pair for cut in cuts for pair in ((x_all.at[mine, :, cut], x_ref.at[:, :, cut]), (gate_all_.at[mine, :, cut], gate_ref.at[:, :, cut]))],
    )
    for fetch in fetches[:2]:
        fetch.wait()
    half = rows // 2
    lane_head = lane_heads(head_size)
    run, step, q = turned(run_ref[:, :rows]), turned(step_ref[...]), q_ref[...]
    skip = turned(run_ref[:, rows:])[:1]
    seg_row = seg_ref[...].astype(F32)
    seg_col = column(seg_row)

    products = lax.dot_general(c_ref[0], b_ref[0], (((1,), (1,)), ((), ())), preferred_element_type=F32)
    tri = lax.broadcasted_iota(jnp.int32, (half, half), 0) >= lax.broadcasted_iota(jnp.int32, (half, half), 1)
    parts = [slice(0, half), slice(half, rows)]
    masks = [tri & (seg_col[part] == seg_row[:, part]) for part in parts]
    diagonal = [products[part, part] for part in parts]
    below = jnp.where(seg_col[parts[1]] == seg_row[:, parts[0]], products[parts[1], parts[0]], 0.0).astype(BF16)
    middle = run[half - 1 : half, :]
    entry = jnp.exp(run[parts[1]] - middle)
    leave = jnp.exp(middle - run[parts[0]]) * step[parts[0]]
    factor = jnp.exp(run)
    for p in range(channels // LANES):
        cols = slice(p * LANES, (p + 1) * LANES)
        first = p * lane_head[1]
        for i, cut in enumerate(cuts):
            if cut.start == cols.start:
                fetches[2 + 2 * i].wait()
                fetches[3 + 2 * i].wait()
        x = x_ref[0, :, cols]
        xf = x.astype(F32)
        ys = []
        for part, mask, prod in zip(parts, masks, diagonal):
            y = None
            for k in range(lane_head[1]):
                h = first + k
                mixing = jnp.exp(jnp.where(mask, run[part, h : h + 1] - q[h : h + 1, part], NEG))
                term = dot((mixing * prod).astype(BF16), x[part])
                y = term if y is None else jnp.where(lane_head[0] == k, term, y)
            ys.append(y)
        sent = (xf[parts[0]] * spread(leave, lane_head, first)).astype(BF16)
        ys[1] = ys[1] + dot(below, sent) * spread(entry, lane_head, first)
        y = jnp.concatenate(ys, axis=0) + spread(skip, lane_head, first) * xf
        v = gate_ref[0, :, cols].astype(F32)
        silu = v / (1.0 + jnp.exp(-v))
        yg_ref[:, cols] = (y * silu).astype(BF16)
        fg_ref[:, cols] = (spread(factor, lane_head, first) * silu).astype(BF16)


def inside(model, head_size, x, gate, b, c, run, q, step, seg_row, after=()):
    _, rows, channels = x.shape
    far = (x, gate, b, c)
    return call(
        functools.partial(inside_kernel, model, head_size),
        f"inside_{model}",
        (run, q, step, seg_row),
        [((rows, channels), BF16)] * 2,
        far,
        after,
        scratch=[pltpu.VMEM((1,) + a.shape[1:], a.dtype) for a in far]
        + [pltpu.SemaphoreType.DMA((2 + 2 * len(tiles(channels)),))],
    )


def load_kernel(w_all, w_ref, sems):
    for fetch in start_all(sems, [(w_all.at[i], w_ref.at[i]) for i in range(w_all.shape[0])]):
        fetch.wait()


def load(w, after):
    return call(load_kernel, "load", (), [(w.shape, BF16)], (w,), after, scratch=[pltpu.SemaphoreType.DMA((w.shape[0],))])


def join_kernel(state, own_ref, got_ref, out_ref):
    own, got = own_ref[...].astype(F32), got_ref[...].astype(F32)
    same = (own[state + 2 : state + 3] == got[state + 2 : state + 3]).astype(F32)
    decay = (own[state : state + 1] + own[state + 1 : state + 2]) * same
    out_ref[:state, :] = (own[:state] + decay * got[:state]).astype(BF16)
    out_ref[state:, :] = own_ref[state:, :]


def join(model, state, own, got, after=()):
    return call(functools.partial(join_kernel, state), f"join_{model}", (own, got), [(own.shape, BF16)], (), after)[0]


def gate_kernel(model, state, alone, near_ref, *refs):
    far_refs, refs = refs[:-7], refs[-7:]
    c_ref, seg_ref, yg_ref, fg_ref, gain_ref, g_ref, ss_ref = refs
    rows, channels = yg_ref.shape
    paired = True if alone else lax.axis_index("seq") % 2 == 1
    seg_col = column(seg_ref[...])
    squares = jnp.zeros((8, rows), F32)
    for cols in tiles(channels):
        near = near_ref[:, cols].astype(F32)
        far = far_refs[0][:, cols].astype(F32)
        for ref in far_refs[1:]:
            far = far + ref[:, cols].astype(F32)
        last_near, last_far = near[state + 2 : state + 3], far[state + 2 : state + 3]
        decay = (near[state : state + 1] + near[state + 1 : state + 2]) * (last_near == last_far).astype(F32)
        entering = (near[:state] + jnp.where(paired, decay, 1.0) * far[:state]).astype(BF16)
        anchor = jnp.where(paired, last_near, last_far)[:, :1]
        reached = (seg_col == anchor).astype(F32)
        gated = yg_ref[:, cols].astype(F32) + reached * fg_ref[:, cols].astype(F32) * dot(c_ref[model], entering)
        g_ref[:, cols] = (gated * gain_ref[model : model + 1, cols]).astype(BF16)
        ones = jnp.ones((8, cols.stop - cols.start), BF16)
        squares += lax.dot_general(
            ones, (gated * gated).astype(BF16), (((1,), (1,)), ((), ())), preferred_element_type=F32
        )
    ss_ref[...] = squares


def gate_all(model, alone, near, far, c, seg_row, yg, fg, gain, after=()):
    return call(
        functools.partial(gate_kernel, model, c.shape[2], alone),
        f"gated_{model}",
        (near, *far, c, seg_row, yg, fg, gain),
        [(yg.shape, BF16), ((8, yg.shape[0]), F32)],
        (),
        after,
    )


def project_kernel(model, shapes, forward, sends, *refs):
    given, (w_ref, keep_ref, *refs) = refs[: sum(shapes)], refs[sum(shapes) :]
    count = len(shapes)
    half, width = keep_ref.shape[1], w_ref.shape[2]
    send_refs, (*refs, lhs) = refs[: len(sends)], refs[len(sends) :]
    first = lax.axis_index("head") % 2 == 0
    if forward:
        refs[0][...] = given[0][:half, :]
        refs[1][...] = given[1][half:, :]
    row = 0
    for ref in given:
        lhs[row : row + ref.shape[0], :] = ref[...]
        row += ref.shape[0]
    def put(result, ref, blocks, start, at, size):
        for k in range(count):
            early = result[2 * k * half : (2 * k + 1) * half].astype(BF16)
            late = result[(2 * k + 1) * half : (2 * k + 2) * half].astype(BF16)
            keep_ref[k, :, pl.ds(start + at, size)] = jnp.where(first, early, late)
            which, place = (ref, blocks.index(k)) if k in blocks else (None, 0)
            if which is None:
                which, place = [(r, part.index(k)) for r, (part, *_) in zip(send_refs, sends) if k in part][0]
            which[place, :, pl.ds(at, size)] = jnp.where(first, late, early)

    tile = min(1024, width)
    done = set()
    for ref, (blocks, start, stop) in zip(send_refs, sends):
        if start in done:
            continue
        done.add(start)

        def step(j, _, ref=ref, blocks=blocks, start=start):
            at = pl.multiple_of(j * tile, tile)
            put(dot(lhs[...], w_ref[model, :, pl.ds(start + at, tile)]), ref, blocks, start, at, tile)
            return 0

        lax.fori_loop(0, (stop - start) // tile, step, 0)


def project(name, model, blocks, weights, after=(), forward=False, split=None, weight=1):
    w, = weights
    flat = [a for block in blocks for a in block]
    depth, width = w.shape[1:]
    n, full = len(blocks), width
    half = sum(a.shape[0] for a in flat) // (2 * n)
    if split == "blocks":
        sends = [([k], 0, full) for k in range(n)]
    elif split == "columns":
        sends = [(list(range(n)), 0, width // 2), (list(range(n)), width // 2, full)]
    else:
        sends = [(list(range(n)), 0, full)]
    return call(
        functools.partial(project_kernel, model, [len(block) for block in blocks], forward, sends),
        name,
        (*flat, w),
        [((n, half, full), BF16)]
        + [((len(part), half, stop - start), BF16) for part, start, stop in sends]
        + [((half, depth), BF16)] * (2 * forward),
        (),
        after,
        scratch=[pltpu.VMEM((2 * half * n, depth), BF16)],
        weight=weight,
    )


def release(name, arrays, after, weight=1):
    return call(lambda *refs: None, name, (), [], (), after, carry=arrays, weight=weight)


def inner_column():
    s = lax.axis_index("seq")
    return (s == 1) | (s == 2)


def pair_kernel(places, counts, own_sent, *refs):
    keeps, gots = refs[:2], (refs[2 : 2 + counts[0]], refs[2 + counts[0] : 2 + sum(counts)])
    first_ref, second_ref = refs[-2:]
    turned_round = (lax.axis_index("seq") // 2 + lax.axis_index("head") // 2) % 2 == 0
    if own_sent:
        turned_round = turned_round | inner_column()

    def ends(pieces):
        stops = [0]
        for ref in pieces:
            stops.append(stops[-1] + ref.shape[2])
        return stops

    bounds = sorted({*ends(gots[0]), *ends(gots[1])})
    for start, stop in zip(bounds, bounds[1:]):
        sums = []
        for keep, pieces, (at, got_at) in zip(keeps, gots, places):
            stops = ends(pieces)
            piece = max(i for i, lower in enumerate(stops) if lower <= start)
            got = pieces[piece][got_at, :, start - stops[piece] : stop - stops[piece]]
            sums.append(keep[at, :, start:stop].astype(F32) + got.astype(F32))
        first_ref[:, start:stop] = jnp.where(turned_round, sums[1], sums[0]).astype(BF16)
        second_ref[:, start:stop] = jnp.where(turned_round, sums[0], sums[1]).astype(BF16)


def pair_sums(name, one, other, after=(), own_sent=False):
    return call(
        functools.partial(pair_kernel, ((one[1], one[3]), (other[1], other[3])), (len(one[2]), len(other[2])), own_sent),
        name,
        (one[0], other[0], *one[2], *other[2]),
        [(one[0].shape[1:], BF16)] * 2,
        (),
        after,
    )


def add_kernel(own_ref, got_ref, out_ref):
    out_ref[...] = (own_ref[...].astype(F32) + got_ref[...].astype(F32)).astype(BF16)


def add(name, own, got, after=()):
    return call(add_kernel, name, (own, got), [(own.shape, BF16)], (), after)


def join_own_kernel(first_ref, second_ref, one_ref, two_ref, out_ref):
    mine = inner_column() & (lax.axis_index("seq") == lax.axis_index("head") // 2)
    other = inner_column() & ~mine
    base = jnp.where(mine, first_ref[...], second_ref[...])
    got = jnp.where(other, two_ref[...], one_ref[...])
    out_ref[...] = (base.astype(F32) + got.astype(F32)).astype(BF16)


def pick_kernel(beside_ref, *refs):
    *terms, out_ref = refs
    value = sum((ref[...] if len(ref.shape) == 2 else ref[0]).astype(F32) for ref in terms)
    out_ref[...] = jnp.where(inner_column(), value.astype(BF16), beside_ref[...])


def pick(name, beside, terms, after=()):
    return call(pick_kernel, name, (beside, *terms), [(beside.shape, BF16)], (), after)[0]


def first_sums_kernel(one_ref, other_ref, out_ref):
    rows = lax.broadcasted_iota(jnp.int32, out_ref.shape, 0)
    out_ref[...] = jnp.where(rows < 4, one_ref[...], other_ref[...])


def sums_kernel(one_ref, other_ref, out_ref):
    out_ref[...] = one_ref[...] + other_ref[...]


def last_kernel(total, model, own_sent, *refs):
    first_n, join_n, three_n, first_d, second_d, one_d, join_d, three_d, two, ss_ref, out_ref = refs
    half = out_ref.shape[1]
    s, z = lax.axis_index("seq"), lax.axis_index("head") // 2
    row = ss_ref[4 * model : 4 * model + 1, :]
    row = jnp.where(lax.axis_index("head") % 2 == 0, row[:, :half], row[:, half:])
    scale = column(lax.rsqrt(row / total + EPS))
    straight = (s == z) | (s + z == 3)
    inner = inner_column()

    def write(condition, *terms):
        @pl.when(condition)
        def _():
            value = terms[0][...].astype(F32)
            for ref in terms[1:]:
                value = value + ref[...].astype(F32)
            out_ref[0] = (value * scale).astype(BF16)

    write(~straight & ~inner, first_n, two, three_n)
    write(~straight & inner, join_n, three_n)
    write(straight & ~inner, join_d, three_d)
    if own_sent:
        write(straight & inner & (s == z), second_d, two, three_d)
        write(straight & inner & (s != z), first_d, one_d, three_d)
    else:
        write(straight & inner, first_d, two, three_d)


def last(model, total, own_sent, operands, before, after=()):
    half, width = operands[0].shape
    earlier = () if before is None else (before,)
    kernel = functools.partial(last_kernel, total, model, own_sent)
    return pl.pallas_call(
        lambda *refs: kernel(*refs[: len(operands)], refs[-1]),
        name=f"last_{model}",
        grid=(1,),
        in_specs=[IN_VMEM] * (len(operands) + len(after))
        + [ANYWHERE] * len(earlier),
        out_specs=pl.BlockSpec((1, half, width), lambda i: (model, 0, 0)),
        out_shape=jax.ShapeDtypeStruct((2, half, width), BF16),
        input_output_aliases={len(operands) + len(after): 0} if earlier else {},
        compiler_params=pltpu.CompilerParams(vmem_limit_bytes=SCOPE),
        cost_estimate=pl.CostEstimate(flops=1 if earlier else HEAVY, bytes_accessed=1, transcendentals=0),
    )(*operands, *after, *earlier)


def xor_pairs(n, k):
    return [(i, i ^ k) for i in range(n)]


def fast(x, gate, b, c, raw, bias, rate, skip, gain, w, seg):
    raw = jnp.swapaxes(raw, 1, 2)
    head_size = x.shape[2] // raw.shape[1]
    state = b.shape[2]
    n_seq, n_head = lax.axis_size("seq"), lax.axis_size("head")
    total = x.shape[2] * n_head
    seg_row = seg.reshape(1, -1)
    def flat(si, zi, ci):
        return si * n_head + zi * 2 + ci

    def sends(kinds, turn):
        pairs = []
        for si in range(n_seq):
            if turn == 1:
                steps = [(0, 1), (3, 2)]
            elif 0 in [si ^ k for k in kinds]:
                steps = [(1, 0), (3, 2), (2, 3), (0, 1)] if turn == 0 else [(2, 0), (1, 3)]
            else:
                steps = [(0, 1), (3, 2)] if turn == 0 else [(1, 2), (2, 1)]
            pairs += [(flat(si, a, ci), flat(si, o, ci)) for a, o in steps for ci in range(2)]
        return pairs

    ring = [(0, 1), (2, 3)]
    across = lambda a: lax.ppermute(a, "head", xor_pairs(n_head, 1))
    beside = lambda a, k: lax.ppermute(a, "seq", xor_pairs(n_seq, k))
    ss = jnp.zeros((8, x.shape[1]), F32)

    x, gate, raw, bias, rate, skip, w = (
        pltpu.with_memory_space_constraint(a, pltpu.HBM) for a in (x, gate, raw, bias, rate, skip, w)
    )
    b_far, c_far, seg_far = (pltpu.with_memory_space_constraint(a, pltpu.HBM) for a in (b, c, seg_row))
    msg0, *scan0 = prep(0, head_size, x, b_far, raw, bias, rate, skip, seg_far)
    near0 = lax.ppermute(msg0, "seq", ring)
    msg1, *scan1 = prep(1, head_size, x, b_far, raw, bias, rate, skip, seg_far, (msg0, *scan0))
    near1 = lax.ppermute(msg1, "seq", ring)
    yg0, fg0 = inside(0, head_size, x, gate, b_far, c_far, *scan0, (msg0, msg1, *scan1))
    end0 = join(0, state, msg0, near0, (yg0, fg0, msg1, scan0[-1], *scan1))
    far0 = [lax.ppermute(end0, "seq", [(1, t)]) for t in (2, 3)]
    yg1, fg1 = inside(1, head_size, x, gate, b_far, c_far, *scan1, (end0, yg0, fg0, near0, msg1, scan0[-1]))
    end1 = join(1, state, msg1, near1, (yg0, fg0, near0, yg1, fg1, scan0[-1], scan1[-1], *far0))
    far1 = [lax.ppermute(end1, "seq", [(1, t)]) for t in (2, 3)]
    held = (near1, yg1, fg1, scan1[-1])
    w = load(w, (end1, near0, yg0, fg0, scan0[-1], *far0, *held))
    g0, ss0 = gate_all(0, False, near0, far0, c, scan0[-1], yg0, fg0, gain, (*w, *far1, *held))
    x0, y0 = beside(g0, 1), beside(g0, 2)
    g1, ss1 = gate_all(1, False, near1, far1, c, scan1[-1], yg1, fg1, gain, (*w, g0, ss0))
    x1, y1 = beside(g1, 1), beside(g1, 2)

    def both(forwarded):
        return beside(forwarded[0], 2), beside(forwarded[1], 1)

    def turn(value, kinds, i):
        return lax.ppermute(value, ("seq", "head"), sends(kinds, i))

    xy, od = (1, 2), (0, 3)
    def add_sums(k, ss, after):
        return call(sums_kernel, f"sums_{k}", (ss, lax.ppermute(ss, "head", xor_pairs(n_head, k))), [(ss.shape, F32)], (), after)[0]

    ss, = call(first_sums_kernel, "sums_0", (ss0, ss1), [(ss0.shape, F32)], (), (*w, g0, g1))
    keep_o0, send_o0 = project("own_0", 0, [(g0,)], w, (g1, ss))
    ss = add_sums(1, ss, (*w, g1, keep_o0, send_o0))
    keep_o1, send_o1 = project("own_1", 1, [(g1,)], w, (ss, keep_o0, send_o0))
    held = (*w, keep_o0, keep_o1, send_o1)
    ss = add_sums(2, ss, (send_o0, *held))
    ss = add_sums(4, ss, (send_o0, *held))
    keep_n0, *send_n0, f0, l0 = project("next_0", 0, [(x0,), (y0,)], w, (ss, send_o0, *held), True, "blocks")
    got_n0 = [across(a) for a in send_n0]
    got_o0 = across(send_o0)
    first_n0, second_n0 = pair_sums(
        "sum_next_0", (keep_n0, 0, got_n0[:1], 0), (keep_n0, 1, got_n0[1:], 0), (f0, l0, got_o0, *held)
    )
    one_n0 = turn(first_n0, xy, 0)
    third_0 = pick("pick_0", second_n0, (keep_o0, got_o0), (first_n0, f0, l0, *held))
    two_n0 = turn(third_0, xy, 1)
    got_o1 = across(send_o1)
    own0, own1 = (keep_o0, 0, (got_o0,), 0), (keep_o1, 0, (got_o1,), 0)
    held = (*w, keep_o0, keep_o1, first_n0, got_o0)
    f0, l0 = release("release_0", (f0, l0), (x1, y1, second_n0, third_0, *held), HEAVY)
    d0 = both((f0, l0))
    held = (*held, second_n0)
    keep_n1, send_n1, f1, l1 = project("next_1", 1, [(x1,), (y1,)], w, (f0, *held), True)
    got_n1 = across(send_n1)
    held = (*held[:-1], keep_n1, f1, l1)
    join_n0, = add("add_next_0", second_n0, one_n0, (got_o1, *held))
    three_n0 = turn(join_n0, xy, 2)
    held = (*held[:-3], got_o1, join_n0)
    f1, l1 = release("release_1", (f1, l1), (*d0, keep_n1, *held))
    d1 = both((f1, l1))
    keep_n1, = release("gate_1", (keep_n1,), (f1, two_n0, *d0, *held), HEAVY)
    held = (*held, two_n0)
    first_n1, second_n1 = pair_sums(
        "sum_next_1", (keep_n1, 0, (got_n1,), 0), (keep_n1, 1, (got_n1,), 1), (*d0, *held)
    )
    held = (*held, first_n1, second_n1)
    keep_d0, *send_d0 = project("opposite_0", 0, [d0], w, held, False, "columns")
    got_d0 = [across(a) for a in send_d0]
    first_d0, second_d0 = pair_sums("sum_opposite_0", own0, (keep_d0, 0, got_d0, 0), held, True)
    one_d0 = turn(first_d0, od, 0)
    first_n1, = release("release_n1", (first_n1,), (first_d0, second_d0, *held[:-2], second_n1))
    one_n1 = turn(first_n1, xy, 0)
    held = (keep_o1, got_o1, first_n0, join_n0, two_n0, three_n0, first_n1, second_n1, first_d0, second_d0)
    keep_d1, *send_d1 = project("opposite_1", 1, [d1], w, held, False, "columns", HEAVY)
    got_d1 = [across(a) for a in send_d1]
    first_d1, second_d1 = pair_sums("sum_opposite_1", own1, (keep_d1, 0, got_d1, 0), held)
    one_d1 = turn(first_d1, od, 0)
    held = (*held[2:], first_d1, second_d1)
    join_d0, = call(
        join_own_kernel, "add_opposite_0", (first_d0, second_d0, one_d0, two_n0), [(first_d0.shape, BF16)], (), held
    )
    three_d0 = turn(join_d0, od, 2)
    held = (*held, one_d0, join_d0)
    third_1 = pick("pick_1", second_n1, (second_d1,), held)
    two_1 = turn(third_1, xy, 1)
    join_n1, = add("add_next_1", second_n1, one_n1, (third_1, *held))
    three_n1 = turn(join_n1, xy, 2)
    held = (*held, join_n1)
    join_d1, = add("add_opposite_1", second_d1, one_d1, (three_d0, *held))
    three_d1 = turn(join_d1, od, 2)
    ss, = release("release_sums", (ss,), (first_d1, second_d1))
    ss = lax.ppermute(
        ss, ("seq", "head"),
        [(flat(zi, si, ci), flat(si, zi, ci)) for si in range(n_seq) for zi in range(n_seq) for ci in range(2)],
    )
    held = (first_n1, join_n1, three_n1, first_d1, second_d1, one_d1, join_d1, two_1)
    out = last(
        0, total, True, (first_n0, join_n0, three_n0, first_d0, second_d0, one_d0, join_d0, three_d0, two_n0, ss), None, held
    )
    return last(
        1, total, False, (first_n1, join_n1, three_n1, first_d1, second_d1, one_d1, join_d1, three_d1, two_1, ss), out
    )


def plain(x, gate, b, c, raw, bias, rate, skip, gain, w, seg):
    raw = jnp.swapaxes(raw, 1, 2)
    head_size = x.shape[2] // raw.shape[1]
    state = b.shape[2]
    n_seq, n_head = lax.axis_size("seq"), lax.axis_size("head")
    total = x.shape[2] * n_head
    seg_row = seg.reshape(1, -1)
    s, h = lax.axis_index("seq"), lax.axis_index("head")
    gs, sums = [], []
    for m in range(2):
        msg, *scan = prep(m, head_size, x, b, raw, bias, rate, skip, seg_row)
        every = lax.all_gather(msg, "seq").astype(F32)
        entering, before = jnp.zeros_like(every[0]), every[0]
        for k in range(n_seq - 1):
            now = every[k]
            same = (now[state + 2] == before[state + 2]).astype(F32)
            decay = (now[state] + now[state + 1]) * same
            new = jnp.concatenate([now[:state] + decay * entering[:state], now[state:]])
            entering = jnp.where(k < s, new, entering)
            before = now
        yg, fg = inside(m, head_size, x, gate, b, c, *scan)
        near = entering.astype(BF16)
        g, ss = gate_all(m, True, near, [jnp.zeros_like(near)], c, scan[-1], yg, fg, gain)
        gs.append(g)
        sums.append(ss[0])
    g = lax.all_gather(jnp.stack(gs), "seq", axis=1, tiled=True)
    terms = jnp.einsum("mtk,mkd->mtd", g, w, preferred_element_type=F32)
    summed = lax.psum_scatter(terms.astype(BF16), "head", scatter_dimension=1, tiled=True)
    squares = lax.all_gather(lax.psum(jnp.stack(sums), "head"), "seq", axis=1, tiled=True)
    mine = lax.dynamic_slice_in_dim(squares, h * summed.shape[1], summed.shape[1], axis=1)
    return (summed.astype(F32) * lax.rsqrt(mine / total + EPS)[:, :, None]).astype(BF16)


def solution(mesh):
    placed = (
        P(None, "seq", "head"),
        P(None, "seq", "head"),
        P(None, "seq", None),
        P(None, "seq", None),
        P(None, "seq", "head"),
        P(None, "head"),
        P(None, "head"),
        P(None, "head"),
        P(None, "head"),
        P(None, "head", "seq"),
        P("seq"),
    )
    local = fast if mesh.shape["seq"] == 4 and mesh.shape["head"] == 8 else plain
    return jax.shard_map(
        local, mesh=mesh, in_specs=placed, out_specs=P(None, "head", "seq"), check_vma=False
    )
```
